32 devices in a mesh: wide: 8 (over z, x), narrow: 4 (over y, core).
Axes of the slice: x: 2, y: 2, z: 4, core: 2. Of those that a mesh axis runs over, the one named last changes fastest.
Arguments:
- tokens: bfloat16 [32768, 768], P(('wide', 'narrow')), may hold values from -6 to 6
- out_grad: bfloat16 [32768, 768], P(('wide', 'narrow')), may hold values from -6 to 6
- doc_lengths: int32 [16], replicated, may hold values from 1 to 30713, as said below
- w_query: bfloat16 [768, 768], replicated, may hold values from -0.21875 to 0.21875
- b_query: bfloat16 [768], replicated, may hold values from -3 to 3
- w_key: bfloat16 [768, 768], replicated, may hold values from -0.21875 to 0.21875
- b_key: bfloat16 [768], replicated, may hold values from -3 to 3
- w_value: bfloat16 [768, 768], replicated, may hold values from -0.21875 to 0.21875
- b_value: bfloat16 [768], replicated, may hold values from -0.015625 to 0.015625
- w_output: bfloat16 [768, 768], replicated, may hold values from -28 to 28
- b_output: bfloat16 [768], replicated, may hold values from -0.625 to 0.625
- w_inner: bfloat16 [768, 3072], replicated, may hold values from -0.21875 to 0.21875
- b_inner: bfloat16 [3072], replicated, may hold values from -0.625 to 0.625
- w_outer: bfloat16 [3072, 768], replicated, may hold values from -0.109375 to 0.109375
- b_outer: bfloat16 [768], replicated, may hold values from -0.625 to 0.625
- gain_first: bfloat16 [768], replicated, may hold values from 0.5 to 1.5
- shift_first: bfloat16 [768], replicated, may hold values from -0.625 to 0.625
- gain_second: bfloat16 [768], replicated, may hold values from 0.5 to 1.5
- shift_second: bfloat16 [768], replicated, may hold values from -0.625 to 0.625
Outputs:
- block_out: bfloat16 [32768, 768], P(('wide', 'narrow'))
- grad_tokens: bfloat16 [32768, 768], P(('wide', 'narrow'))
- grad_w_query: float32 [768, 768], P(('wide', 'narrow'))
- grad_b_query: float32 [768], P(('wide', 'narrow'))
- grad_w_key: float32 [768, 768], P(('wide', 'narrow'))
- grad_b_key: float32 [768], P(('wide', 'narrow'))
- grad_w_value: float32 [768, 768], P(('wide', 'narrow'))
- grad_b_value: float32 [768], P(('wide', 'narrow'))
- grad_w_output: float32 [768, 768], P(('wide', 'narrow'))
- grad_b_output: float32 [768], P(('wide', 'narrow'))
- grad_w_inner: float32 [768, 3072], P(('wide', 'narrow'))
- grad_b_inner: float32 [3072], P(('wide', 'narrow'))
- grad_w_outer: float32 [3072, 768], P(('wide', 'narrow'))
- grad_b_outer: float32 [768], P(('wide', 'narrow'))
- grad_gain_first: float32 [768], P(('wide', 'narrow'))
- grad_shift_first: float32 [768], P(('wide', 'narrow'))
- grad_gain_second: float32 [768], P(('wide', 'narrow'))
- grad_shift_second: float32 [768], P(('wide', 'narrow'))
The draws below stay inside these ranges and needn't reach their ends.
Inputs may be any that keep to these rules, and one draw needn't show every extreme that they name: `doc_lengths`: one document, at a place in the order drawn from the seed, holds 32768 - 256 - (16 - 2) // 2 * (256 + 1) tokens. Of the others, one has exactly 256 tokens and the rest come in pairs whose lengths sum to 256 + 1 (one pair is 1 and 256), in an order drawn from the seed. The lengths sum to 32768.
All inputs are finite; a program needn't handle non-finite values.
Results may differ from the reference program's by a relative error of at most 0.015.
Values may be sent and summed in bfloat16 or wider, within the bound.
No kernel may reach another device: no remote copies, remote signals or barrier semaphores. Data moves between devices by JAX's collectives and lax.ppermute only.
A program may use at most 192 MiB of HBM per device.

```python
import math
import jax
import jax.numpy as jnp
from jax import lax

D = 768
H = 12
DH = 64
FF = 3072
ATT_BLK = 512
NDOC = 16
TOKENS = 32768
SHORT = 256


def draw_doc_lengths(key, part):
    key = jax.random.fold_in(key, 7)
    key_pair, key_perm, key_big = jax.random.split(key, 3)
    pairs = (NDOC - 2) // 2
    firsts = jax.random.randint(key_pair, (pairs,), 1, SHORT + 1).astype(jnp.int32)
    firsts = jnp.where(jnp.arange(pairs, dtype=jnp.int32) == 0, 1, firsts).astype(jnp.int32)
    seconds = (SHORT + 1 - firsts).astype(jnp.int32)
    shorts = jnp.concatenate([jnp.full((1,), SHORT, jnp.int32), firsts, seconds])
    shorts = jax.random.permutation(key_perm, shorts)
    big = jax.random.randint(key_big, (), 0, NDOC).astype(jnp.int32)
    rest = TOKENS - SHORT - pairs * (SHORT + 1)
    index = jnp.arange(NDOC, dtype=jnp.int32)
    padded = jnp.concatenate([shorts, jnp.zeros((1,), jnp.int32)])
    before = padded[jnp.minimum(index, NDOC - 2)]
    after = padded[jnp.maximum(index - 1, 0)]
    lengths = jnp.where(index < big, before, jnp.where(index == big, rest, after))
    return lengths.astype(jnp.int32)


def spiked(drawn, key, source, target, shards_of, factor):
    def block_of(position):
        return (jnp.arange(drawn.shape[position]) // (drawn.shape[position] // shards_of)).reshape((-1,) + (1,) * (drawn.ndim - 1 - position))

    first = jax.random.permutation(key, shards_of)[block_of(target)]
    far = (block_of(target) + shards_of // 2) % shards_of
    return jnp.where((block_of(source) == first) | (block_of(source) == far), factor * drawn, drawn)


def levels(stream_key, extent, pieces, smallest, top_value):
    def one(dim, parts):
        heights = jax.random.uniform(jax.random.fold_in(jax.random.fold_in(stream_key, 6), dim), (parts,), jnp.float32, smallest / len(pieces), top_value / len(pieces))
        return jnp.repeat(jnp.exp(heights), extent[dim] // parts).reshape((-1,) + (1,) * (len(extent) - dim - 1))

    level = one(*pieces[0])
    for cut in pieces[1:]:
        level = level * one(*cut)
    return level


def normal_values(key, shape, scale, reach, pieces=(), held_as=jnp.bfloat16):
    loudness = levels(key, shape, pieces, -0.22, 0.18) if pieces else 1.0
    values = jax.random.normal(key, shape, jnp.float32) * scale * loudness
    return jnp.minimum(jnp.maximum(values, -reach), reach).astype(held_as)


def heavy_noise(key, dims, spread, most, cuts, heavy, kind=jnp.bfloat16):
    entries = spread * jax.random.normal(key, dims, jnp.float32)
    if cuts:
        entries = entries * levels(key, dims, cuts, -0.22, 0.18)
    return jnp.clip(spiked(entries, jax.random.fold_in(key, 3), *heavy), -most, most).astype(kind)


def setup_inputs(seed: int = 0) -> dict:
    key_of = jax.random.split(jax.random.key(seed), 20)
    return {
        "tokens": heavy_noise(key_of[0], (TOKENS, D), 1.0, 6.0, ((0, 32),), (0, 1, 32, 2.75)),
        "out_grad": normal_values(key_of[1], (TOKENS, D), 1.0, 6.0, ((0, 32),)),
        "doc_lengths": draw_doc_lengths(jax.random.fold_in(key_of[19], 71), 0),
        "w_query": normal_values(key_of[3], (D, D), D ** -0.5, 0.21875),
        "b_query": normal_values(key_of[4], (D,), 0.5, 3.0),
        "w_key": normal_values(key_of[5], (D, D), D ** -0.5, 0.21875),
        "b_key": normal_values(key_of[6], (D,), 0.5, 3.0),
        "w_value": normal_values(key_of[7], (D, D), D ** -0.5, 0.21875),
        "b_value": normal_values(key_of[8], (D,), 0.003, 0.015625),
        "w_output": normal_values(key_of[9], (D, D), (max(1, TOKENS // (2 * D)) ** 0.5), 28.0),
        "b_output": normal_values(key_of[10], (D,), 0.1, 0.625),
        "w_inner": normal_values(key_of[11], (D, FF), D ** -0.5, 0.21875),
        "b_inner": normal_values(key_of[12], (FF,), 0.1, 0.625),
        "w_outer": normal_values(key_of[13], (FF, D), FF ** -0.5, 0.109375),
        "b_outer": normal_values(key_of[14], (D,), 0.1, 0.625),
        "gain_first": jnp.clip(1.0 + 0.1 * jax.random.normal(key_of[15], (D,), jnp.float32), 0.5, 1.5).astype(jnp.bfloat16),
        "shift_first": normal_values(key_of[16], (D,), 0.1, 0.625),
        "gain_second": jnp.clip(1.0 + 0.1 * jax.random.normal(key_of[17], (D,), jnp.float32), 0.5, 1.5).astype(jnp.bfloat16),
        "shift_second": normal_values(key_of[18], (D,), 0.1, 0.625),
    }


@jax.custom_vjp
def low(v):
    return lax.optimization_barrier(v.astype(jnp.bfloat16)).astype(jnp.float32)

@jax.custom_vjp
def low_back(v):
    return v

def low_keep(v):
    return (low(v), None)

def low_pass(kept, grad):
    return (grad,)

def back_keep(v):
    return (v, None)

def back_low(kept, grad):
    return (low(grad),)
low.defvjp(low_keep, low_pass)
low_back.defvjp(back_keep, back_low)
EPS = 1e-05
HALF_PI = math.pi / 2.0

def matmul(left, right):
    return jnp.dot(left, right, precision=lax.Precision.HIGHEST)

def layer_norm(resid, gain, shift):
    mean = lax.optimization_barrier(jnp.mean(resid, axis=-1, keepdims=True))
    cent = resid - mean
    var = lax.optimization_barrier(jnp.mean(cent * cent, axis=-1, keepdims=True))
    return cent * lax.rsqrt(var + EPS) * gain + shift

def features(heads, cos_t, sin_t):
    soft = jax.nn.softplus(heads)
    return jnp.concatenate([soft * cos_t[:, None, None], soft * sin_t[:, None, None]], axis=-1)

def doc_table(doc_lengths, count):
    ends = jnp.cumsum(doc_lengths).astype(jnp.int32)
    starts = (ends - doc_lengths).astype(jnp.int32)
    place = jnp.arange(count, dtype=jnp.int32)
    member = (place[:, None] >= starts[None, :]) & (place[:, None] < ends[None, :])
    index = jnp.arange(doc_lengths.shape[0], dtype=jnp.int32)
    doc_of = lax.optimization_barrier(jnp.sum(jnp.where(member, index[None, :], 0), axis=1)).astype(jnp.int32)
    tok_start = lax.optimization_barrier(jnp.sum(jnp.where(member, starts[None, :], 0), axis=1)).astype(jnp.int32)
    tok_end = lax.optimization_barrier(jnp.sum(jnp.where(member, ends[None, :], 0), axis=1)).astype(jnp.int32)
    angle = HALF_PI * (place - tok_start).astype(jnp.float32) / (tok_end - tok_start).astype(jnp.float32)
    return (doc_of, tok_start, angle)

def reference(tokens, out_grad, doc_lengths, w_query, b_query, w_key, b_key, w_value, b_value, w_output, b_output, w_inner, b_inner, w_outer, b_outer, gain_first, shift_first, gain_second, shift_second):
    doc_of, tok_start, angle = doc_table(doc_lengths, TOKENS)
    cos_t = jnp.cos(angle)
    sin_t = jnp.sin(angle)
    nblocks = TOKENS // ATT_BLK
    block_first = jnp.arange(nblocks, dtype=jnp.int32) * ATT_BLK
    causal = jnp.arange(ATT_BLK)[:, None] >= jnp.arange(ATT_BLK)[None, :]

    def block_step(carry, inputs):
        state, zsum = carry
        qb, kb, vb, docb, startb, first_tok = inputs
        mask = (causal & (docb[:, None] == docb[None, :])).astype(jnp.float32)
        scores = jnp.einsum('ihf,jhf->hij', qb, kb, precision=lax.Precision.HIGHEST)
        probs = low_back(low(scores * mask[None]))
        carried = (startb < first_tok).astype(jnp.float32)
        numer = jnp.einsum('hij,jhd->ihd', probs, vb, precision=lax.Precision.HIGHEST)
        numer = numer + carried[:, None, None] * jnp.einsum('ihf,hfd->ihd', qb, state, precision=lax.Precision.HIGHEST)
        numer = low_back(numer)
        denom = lax.optimization_barrier(jnp.sum(probs, axis=2)).T + carried[:, None] * jnp.einsum('ihf,hf->ih', qb, zsum, precision=lax.Precision.HIGHEST)
        ratio = numer / denom[:, :, None]
        closing = (docb == docb[-1]).astype(jnp.float32)
        keep = (startb[-1] < first_tok).astype(jnp.float32)
        state_next = keep * state + jnp.einsum('jhf,jhd->hfd', kb * closing[:, None, None], vb, precision=lax.Precision.HIGHEST)
        zsum_next = keep * zsum + jnp.einsum('jhf,j->hf', kb, closing, precision=lax.Precision.HIGHEST)
        return ((state_next, zsum_next), ratio)

    def forward(x, wq, bq, wk, bk, wv, bv, wo, bo, w1, b1, w2, b2, g1, e1, g2, e2):
        query = low_back(low(matmul(x, wq) + bq))
        key = low_back(low(matmul(x, wk) + bk))
        value = low_back(low(matmul(x, wv) + bv))
        qf = low(features(query.reshape(TOKENS, H, DH), cos_t, sin_t))
        kf = low(features(key.reshape(TOKENS, H, DH), cos_t, sin_t))
        vh = value.reshape(TOKENS, H, DH)
        init = (jnp.zeros((H, 2 * DH, DH), jnp.float32), jnp.zeros((H, 2 * DH), jnp.float32))
        xs = (qf.reshape(nblocks, ATT_BLK, H, 2 * DH), kf.reshape(nblocks, ATT_BLK, H, 2 * DH), vh.reshape(nblocks, ATT_BLK, H, DH), doc_of.reshape(nblocks, ATT_BLK), tok_start.reshape(nblocks, ATT_BLK), block_first)
        unused, ratios = lax.scan(jax.checkpoint(block_step), init, xs)
        mixed = low_back(low(ratios.reshape(TOKENS, D)))
        branch = low_back(matmul(mixed, wo) + bo)
        first = low(layer_norm(x + branch, g1, e1))
        inner = low_back(matmul(first, w1) + b1)
        activ = low(jax.nn.gelu(inner, approximate=False))
        outer = low_back(matmul(activ, w2) + b2)
        return layer_norm(first + outer, g2, e2)
    weights = [w_query, b_query, w_key, b_key, w_value, b_value, w_output, b_output, w_inner, b_inner, w_outer, b_outer, gain_first, shift_first, gain_second, shift_second]
    weights = [w.astype(jnp.float32) for w in weights]
    result, pullback = jax.vjp(forward, tokens.astype(jnp.float32), *weights)
    grads = pullback(out_grad.astype(jnp.float32))
    return (result.astype(jnp.bfloat16), grads[0].astype(jnp.bfloat16), grads[1], grads[2], grads[3], grads[4], grads[5], grads[6], grads[7], grads[8], grads[9], grads[10], grads[11], grads[12], grads[13], grads[14], grads[15], grads[16])
```

```python
import functools
import math

import jax
import jax.numpy as jnp
from jax import lax
from jax.experimental import pallas as pl
from jax.experimental.pallas import tpu as pltpu
from jax.sharding import PartitionSpec as P

DH = 64
LANES = 128
CHUNK = 256
EPS = 1e-05
HALF_PI = math.pi / 2.0
MIB = 1 << 20
AXES = ("wide", "narrow")

f32 = jnp.float32
bf16 = jnp.bfloat16

R_BQ, R_BK, R_BV, R_BO, R_G1, R_E1, R_B2, R_G2, R_E2, R_B1 = range(10)
V_B2, V_G2, V_E2, V_G1, V_E1, V_BO, V_B1 = range(7)
VEC_ROWS = 16


def nn(a, b):
    return jnp.dot(a, b, preferred_element_type=f32)


def nt(a, b):
    return lax.dot_general(a, b, (((1,), (1,)), ((), ())), preferred_element_type=f32)


def tn(a, b):
    return lax.dot_general(a, b, (((0,), (0,)), ((), ())), preferred_element_type=f32)


def lane_iota(rows, lanes=LANES):
    return lax.broadcasted_iota(jnp.int32, (rows, lanes), 1)


def row_iota(rows, lanes=LANES):
    return lax.broadcasted_iota(jnp.int32, (rows, lanes), 0)


def swap_halves(x):
    return pltpu.roll(x, DH, 1)


def softplus(x):
    return jnp.maximum(x, 0.0) + jnp.log1p(jnp.exp(-jnp.abs(x)))


def sigmoid(x):
    return 1.0 / (1.0 + jnp.exp(-x))


def sine(b):
    s = b * b
    p = 1.0 / 6227020800.0
    for c in (-1.0 / 39916800.0, 1.0 / 362880.0, -1.0 / 5040.0, 1.0 / 120.0, -1.0 / 6.0):
        p = p * s + c
    return b + b * s * p


def features(pair, cs, lo):
    soft = softplus(pair)
    other = swap_halves(soft)
    return (
        (jnp.where(lo, soft, other) * cs).astype(bf16),
        (jnp.where(lo, other, soft) * cs).astype(bf16),
    )


def extended(v, lo):
    one = jnp.ones_like(v)
    return jnp.where(lo, v, one), jnp.where(lo, one, v)


def pairs_of(width):
    return width // LANES


def key_kernel(
    place_ref, len_ref, x_ref, wk_ref, wv_ref, vec_ref,
    k_ref, v_ref, kf_ref, cs_ref, st_ref, en_ref, state_ref,
    *, rows,
):
    step = pl.program_id(0)
    base = place_ref[0]
    first = base + step * CHUNK
    pos = first + row_iota(CHUNK)
    lane = lane_iota(CHUNK)
    lo = lane < DH
    start = jnp.zeros((CHUNK, LANES), jnp.int32)
    end = jnp.zeros((CHUNK, LANES), jnp.int32)
    edge = jnp.int32(0)
    for doc in range(len_ref.shape[0]):
        here = pos >= edge
        after = edge + len_ref[doc]
        start = jnp.where(here, edge, start)
        end = jnp.where(here, after, end)
        edge = after
    part = jnp.where(lo, end - pos, pos - start).astype(f32)
    cs = sine(HALF_PI * part / (end - start).astype(f32))
    cs_ref[...] = cs
    st_ref[...] = start
    en_ref[...] = end

    x = x_ref[...]
    k = (nn(x, wk_ref[...]) + vec_ref[R_BK : R_BK + 1, :]).astype(bf16)
    v = (nn(x, wv_ref[...]) + vec_ref[R_BV : R_BV + 1, :]).astype(bf16)
    k_ref[...] = k
    v_ref[...] = v
    closing = end >= base + rows
    slots = lane_iota(LANES)
    lo_state = slots < DH

    @pl.when(step == 0)
    def _():
        state_ref[...] = jnp.zeros_like(state_ref)

    npair = pairs_of(x.shape[1])
    zcol = jnp.zeros((LANES, LANES), f32)
    for g in range(npair):
        cols = slice(g * LANES, (g + 1) * LANES)
        fa, fb = features(k[:, cols].astype(f32), cs, lo)
        kf_ref[:, 2 * g * LANES : (2 * g + 1) * LANES] = fa
        kf_ref[:, (2 * g + 1) * LANES : (2 * g + 2) * LANES] = fb
        va, vb = extended(v[:, cols], lo)
        zero = jnp.zeros_like(fa)
        sa = tn(jnp.where(closing, fa, zero), va)
        sb = tn(jnp.where(closing, fb, zero), vb)
        state_ref[g] += jnp.where(lo_state, sa, sb)
        zcol = jnp.where(slots == DH + g, sa, jnp.where(slots == g, sb, zcol))
    state_ref[npair] += zcol


def unpack_state(state_ref, g, npair, lo, slots):
    pair = state_ref[g].astype(f32)
    z = state_ref[npair].astype(f32)
    za = z[:, DH + g : DH + g + 1]
    zb = z[:, g : g + 1]
    return jnp.where(lo, pair, za), jnp.where(lo, zb, pair)


def unpack_grad_state(state_ref, g, npair, lo, slots):
    pair = state_ref[g].astype(f32)
    z = state_ref[npair].astype(f32)
    za = jnp.where(slots == DH, z[:, DH + g : DH + g + 1], 0.0)
    zb = jnp.where(slots == 0, z[:, g : g + 1], 0.0)
    return jnp.where(lo, pair, za), jnp.where(lo, zb, pair)


def query_kernel(x_ref, wq_ref, vec_ref, cs_ref, q_ref, qf_ref):
    q = (nn(x_ref[...], wq_ref[...]) + vec_ref[R_BQ : R_BQ + 1, :]).astype(bf16)
    q_ref[...] = q
    lo = lane_iota(CHUNK) < DH
    cs = cs_ref[...]
    for g in range(pairs_of(q.shape[1])):
        fa, fb = features(q[:, g * LANES : (g + 1) * LANES].astype(f32), cs, lo)
        qf_ref[:, 2 * g * LANES : (2 * g + 1) * LANES] = fa
        qf_ref[:, (2 * g + 1) * LANES : (2 * g + 2) * LANES] = fb


def mixer_kernel(place_ref, qf_ref, kf_ref, v_ref, st_ref, en_ref, o_ref, kept_ref, local):
    step = pl.program_id(0)
    first = place_ref[0] + step * CHUNK
    start, end = st_ref[...], en_ref[...]
    start2 = jnp.concatenate([start, start], axis=1)
    ipos = first + row_iota(CHUNK, CHUNK)
    jpos = first + lane_iota(CHUNK, CHUNK)
    mask = (jpos <= ipos) & (jpos >= start2)
    carried = start < first
    closing = end >= first + CHUNK
    keep = start[CHUNK - 1 : CHUNK, :] < first
    lo = lane_iota(CHUNK) < DH

    @pl.when(step == 0)
    def _():
        local[...] = jnp.zeros_like(local)

    for g in range(pairs_of(v_ref.shape[1])):
        vs = extended(v_ref[:, g * LANES : (g + 1) * LANES], lo)
        for s in range(2):
            h = 2 * g + s
            cols = slice(h * LANES, (h + 1) * LANES)
            qf, kf, v = qf_ref[:, cols], kf_ref[:, cols], vs[s]
            probs = jnp.where(mask, nt(qf, kf), 0.0).astype(bf16)
            held = local[h].astype(bf16)
            kept_ref[0, h] = held
            o_ref[:, cols] = nn(probs, v) + jnp.where(carried, nn(qf, held), 0.0)
            local[h] = jnp.where(keep, local[h], 0.0) + tn(
                jnp.where(closing, kf, jnp.zeros_like(kf)), v
            )


def gelu_and_slope(u):
    z = jnp.abs(u) * (1.0 / math.sqrt(2.0))
    t = 1.0 / (1.0 + 0.3275911 * z)
    p = 0.5 * 1.061405429
    for c in (-1.453152027, 1.421413741, -0.284496736, 0.254829592):
        p = p * t + 0.5 * c
    e = jnp.exp(-0.5 * u * u)
    tail = p * t * e
    gauss = jnp.where(u >= 0.0, 1.0 - tail, tail)
    return u * gauss, gauss + u * e * (1.0 / math.sqrt(2.0 * math.pi))


def token_kernel(
    place_ref, o0_ref, o1_ref, o2_ref, qf_ref, state_ref, st_ref, x_ref, go_ref,
    wo_ref, w1_ref, w2_ref, vec_ref,
    out_ref, mixed_ref, first_ref, act_ref, douter_ref, dinner_ref, dbranch_ref, dr1_ref,
    dn_ref, back_ref, vgrad_ref,
    states, ratio, rden_s, slope,
    *, split,
):
    step = pl.program_id(0)
    base = place_ref[0]
    width = x_ref.shape[1]
    ff = w1_ref.shape[1]
    npair = pairs_of(width)
    lane = lane_iota(CHUNK)
    lo = lane < DH
    slots = lane_iota(LANES)
    lo_state = slots < DH
    start = st_ref[...]

    @pl.when(step == 0)
    def _():
        for g in range(npair):
            a, b = unpack_state(state_ref, g, npair, lo_state, slots)
            states[2 * g] = a.astype(bf16)
            states[2 * g + 1] = b.astype(bf16)
        back_ref[...] = jnp.zeros_like(back_ref)
        vgrad_ref[...] = jnp.zeros_like(vgrad_ref)

    carried = start < base
    o_refs = (o0_ref, o1_ref, o2_ref)
    for g in range(npair):
        both = []
        for s in range(2):
            h = 2 * g + s
            o_of = o_refs[h // 4]
            local = o_of[:, (h % 4) * LANES : (h % 4 + 1) * LANES]
            far = nn(qf_ref[:, h * LANES : (h + 1) * LANES], states[h])
            both.append(local + jnp.where(carried, far, 0.0))
        numer = jnp.where(lo, both[0], both[1])
        rden = 1.0 / swap_halves(jnp.where(lo, both[1], both[0]))
        cols = slice(g * LANES, (g + 1) * LANES)
        rden_s[:, cols] = rden
        ratio[:, cols] = numer * rden
    mixed = ratio[...].astype(bf16)
    mixed_ref[...] = mixed

    def row(r):
        return vec_ref[r : r + 1, :]

    def norm(resid):
        cent = resid - jnp.mean(resid, axis=-1, keepdims=True)
        rstd = lax.rsqrt(jnp.mean(cent * cent, axis=-1, keepdims=True) + EPS)
        return cent * rstd, rstd

    r1 = x_ref[...].astype(f32) + nn(mixed, wo_ref[...]) + row(R_BO)
    n1, rstd1 = norm(r1)
    first = (n1 * row(R_G1) + row(R_E1)).astype(bf16)
    first_ref[...] = first

    outer = jnp.zeros((CHUNK, width), f32)
    part = ff // split
    for i in range(split):
        cols = slice(i * part, (i + 1) * part)
        flat = i * part // width
        off = i * part % width
        bias = vec_ref[R_B1 + flat : R_B1 + flat + 1, off : off + part]
        inner = nn(first, w1_ref[:, cols]) + bias
        act, sl = gelu_and_slope(inner)
        act = act.astype(bf16)
        act_ref[:, cols] = act
        slope[:, cols] = sl
        outer = outer + nn(act, w2_ref[cols, :])
    r2 = first.astype(f32) + outer + row(R_B2)
    n2, rstd2 = norm(r2)
    out_ref[...] = (n2 * row(R_G2) + row(R_E2)).astype(bf16)

    def column_sum(r, v):
        vgrad_ref[r : r + 1, :] += jnp.sum(v, axis=0, keepdims=True)

    def norm_back(grad, normed, rstd, gain):
        d_n = grad * gain
        m1 = jnp.mean(d_n, axis=-1, keepdims=True)
        m2 = jnp.mean(d_n * normed, axis=-1, keepdims=True)
        return rstd * (d_n - m1 - normed * m2)

    grad = go_ref[...].astype(f32)
    column_sum(V_G2, grad * n2)
    column_sum(V_E2, grad)
    d_r2 = norm_back(grad, n2, rstd2, row(R_G2))
    d_outer = d_r2.astype(bf16)
    douter_ref[...] = d_outer
    column_sum(V_B2, d_outer.astype(f32))
    d_first = d_r2
    for i in range(split):
        cols = slice(i * part, (i + 1) * part)
        flat = i * part // width
        off = i * part % width
        d_inner = (nt(d_outer, w2_ref[cols, :]) * slope[:, cols]).astype(bf16)
        dinner_ref[:, cols] = d_inner
        vgrad_ref[V_B1 + flat : V_B1 + flat + 1, off : off + part] += jnp.sum(
            d_inner.astype(f32), axis=0, keepdims=True
        )
        d_first = d_first + nt(d_inner, w1_ref[:, cols])
    column_sum(V_G1, d_first * n1)
    column_sum(V_E1, d_first)
    d_r1 = norm_back(d_first, n1, rstd1, row(R_G1))
    dr1_ref[...] = d_r1
    d_branch = d_r1.astype(bf16)
    dbranch_ref[...] = d_branch
    column_sum(V_BO, d_branch.astype(f32))
    d_mixed = nt(d_branch, wo_ref[...]).astype(bf16).astype(f32)
    opening = start <= base
    zcol = jnp.zeros((LANES, LANES), f32)
    for g in range(npair):
        cols = slice(g * LANES, (g + 1) * LANES)
        dm = d_mixed[:, cols]
        rden = rden_s[:, cols]
        dn = dm * rden
        prod = dn * ratio[:, cols]
        dda = -jnp.sum(jnp.where(lo, prod, 0.0), axis=1, keepdims=True)
        ddb = -jnp.sum(jnp.where(lo, 0.0, prod), axis=1, keepdims=True)
        hia, hib = dda.astype(bf16).astype(f32), ddb.astype(bf16).astype(f32)
        exa = jnp.where(lane == DH, hia, jnp.where(lane == DH + 1, dda - hia, 0.0))
        exb = jnp.where(lane == 0, hib, jnp.where(lane == 1, ddb - hib, 0.0))
        dna = jnp.where(lo, dn, exa).astype(bf16)
        dnb = jnp.where(lo, exb, dn).astype(bf16)
        ca = slice(2 * g * LANES, (2 * g + 1) * LANES)
        cb = slice((2 * g + 1) * LANES, (2 * g + 2) * LANES)
        dn_ref[:, ca] = dna
        dn_ref[:, cb] = dnb
        zero = jnp.zeros((CHUNK, LANES), bf16)
        ga = tn(jnp.where(opening, qf_ref[:, ca], zero), dna)
        gb = tn(jnp.where(opening, qf_ref[:, cb], zero), dnb)
        back_ref[g] += jnp.where(lo_state, ga, gb)
        za = ga[:, DH : DH + 1] + ga[:, DH + 1 : DH + 2]
        zb = gb[:, 0:1] + gb[:, 1:2]
        zcol = jnp.where(slots == DH + g, za, jnp.where(slots == g, zb, zcol))
    back_ref[npair] += zcol


def mixer_back_kernel(
    place_ref, qf_ref, kf_ref, v_ref, dn_ref, q_ref, kept_ref, state_ref, st_ref, en_ref, cs_ref,
    dq_ref, dk_ref, dv_ref, onward_state,
    *, pair0, npair, nchunk,
):
    step = nchunk - 1 - pl.program_id(0)
    base = place_ref[0]
    first = base + step * CHUNK
    start, end, cs = st_ref[...], en_ref[...], cs_ref[...]
    end2 = jnp.concatenate([end, end], axis=1)
    jpos = first + row_iota(CHUNK, CHUNK)
    ipos = first + lane_iota(CHUNK, CHUNK)
    mask = (jpos <= ipos) & (ipos < end2)
    carried = start < first
    onward = end > first + CHUNK
    opening = start <= first
    from_far = start[0:1, :] < base
    keep = end[0:1, :] > first + CHUNK
    lo = lane_iota(CHUNK) < DH
    slots = lane_iota(LANES)
    lo_state = slots < DH

    @pl.when(pl.program_id(0) == 0)
    def _():
        onward_state[...] = jnp.zeros_like(onward_state)

    for g in range(pairs_of(v_ref.shape[1])):
        pair = slice(g * LANES, (g + 1) * LANES)
        vs = extended(v_ref[:, pair], lo)
        far = unpack_state(state_ref, pair0 + g, npair, lo_state, slots)
        dqs, dks, dvs = [], [], []
        for s in range(2):
            h = 2 * g + s
            cols = slice(h * LANES, (h + 1) * LANES)
            qf, kf, v, dn = qf_ref[:, cols], kf_ref[:, cols], vs[s], dn_ref[:, cols]
            held = (kept_ref[0, h].astype(f32) + jnp.where(from_far, far[s], 0.0)).astype(bf16)
            ahead = onward_state[h]
            ahead16 = ahead.astype(bf16)
            probs = jnp.where(mask, nt(kf, qf), 0.0).astype(bf16)
            d_probs = jnp.where(mask, nt(v, dn), 0.0).astype(bf16)
            d_qf = tn(d_probs, kf) + jnp.where(carried, nt(dn, held), 0.0)
            d_kf = nn(d_probs, qf) + jnp.where(onward, nt(v, ahead16), 0.0)
            dvs.append(nn(probs, dn) + jnp.where(onward, nn(kf, ahead16), 0.0))
            onward_state[h] = jnp.where(keep, ahead, 0.0) + tn(
                jnp.where(opening, qf, jnp.zeros_like(qf)), dn
            )
            tq, tk = d_qf * cs, d_kf * cs
            dqs.append(tq + swap_halves(tq))
            dks.append(tk + swap_halves(tk))
        sig = sigmoid(q_ref[:, pair].astype(f32))
        dq_ref[:, pair] = (jnp.where(lo, dqs[0], dqs[1]) * sig).astype(bf16)
        dk_ref[:, pair] = jnp.where(lo, dks[0], dks[1])
        dv_ref[:, pair] = jnp.where(lo, dvs[0], dvs[1])


def store_pieces(own, value, rows, send_ref, keep_ref, at):
    count = value.shape[0] // rows
    value = value.astype(bf16)
    for bit in range(2):

        @pl.when(own == bit)
        def _():
            for d in range(count):
                ref = keep_ref if d % 2 == bit else send_ref
                ref[d // 2, at : at + rows, :] = value[d * rows : (d + 1) * rows, :]


def qkv_back_kernel(
    place_ref, dk0, dk1, dk2, dv0, dv1, dv2, dq0, dq1, dq2, k_ref, kf_ref, v_ref, back_ref, en_ref, cs_ref, x_ref,
    dkey_ref, dval_ref, send_ref, keep_ref, key_s, val_s, vec_s,
    *, rows, nchunk, piece,
):
    step = pl.program_id(0)
    base = place_ref[0]
    own = place_ref[1]
    lo = lane_iota(CHUNK) < DH
    slots = lane_iota(LANES)
    lo_state = slots < DH
    npair = pairs_of(x_ref.shape[1])

    @pl.when(step == 0)
    def _():
        vec_s[...] = jnp.zeros_like(vec_s)

    @pl.when(step < nchunk)
    def _():
        onward = en_ref[...] > base + rows
        cs = cs_ref[...]
        dks, dvs = (dk0, dk1, dk2), (dv0, dv1, dv2)
        for g in range(npair):
            pair = slice(g * LANES, (g + 1) * LANES)
            sub = slice((g % 2) * LANES, (g % 2 + 1) * LANES)
            ga, gb = unpack_grad_state(back_ref, g, npair, lo_state, slots)
            ga, gb = ga.astype(bf16), gb.astype(bf16)
            va, vb = extended(v_ref[:, pair], lo)
            ta = nt(va, ga) * cs
            tb = nt(vb, gb) * cs
            far = jnp.where(lo, ta + swap_halves(ta), tb + swap_halves(tb))
            far_v = jnp.where(
                lo,
                nn(kf_ref[:, 2 * g * LANES : (2 * g + 1) * LANES], ga),
                nn(kf_ref[:, (2 * g + 1) * LANES : (2 * g + 2) * LANES], gb),
            )
            sig = sigmoid(k_ref[:, pair].astype(f32))
            d_key = ((dks[g // 2][:, sub] + jnp.where(onward, far, 0.0)) * sig).astype(bf16)
            d_val = (dvs[g // 2][:, sub] + jnp.where(onward, far_v, 0.0)).astype(bf16)
            dkey_ref[:, pair] = d_key
            dval_ref[:, pair] = d_val
            at = pl.ds(pl.multiple_of(step * CHUNK, CHUNK), CHUNK)
            key_s[at, pair] = d_key
            val_s[at, pair] = d_val

    @pl.when(step == nchunk)
    def _():
        x = x_ref[...]
        q = jnp.concatenate([dq0[...], dq1[...], dq2[...]], axis=1)
        vec_s[0:1, :] = jnp.sum(q.astype(f32), axis=0, keepdims=True)
        store_pieces(own, tn(x, q), piece, send_ref, keep_ref, 0)
        vec_s[1:2, :] = jnp.sum(key_s[...].astype(f32), axis=0, keepdims=True)
        store_pieces(own, tn(x, key_s[...]), piece, send_ref, keep_ref, piece)
        vec_s[2:3, :] = jnp.sum(val_s[...].astype(f32), axis=0, keepdims=True)
        store_pieces(own, tn(x, val_s[...]), piece, send_ref, keep_ref, 2 * piece)
        vec = vec_s[...].astype(bf16)
        for m in range(send_ref.shape[0]):
            send_ref[m, 3 * piece : 3 * piece + 8, :] = vec
            keep_ref[m, 3 * piece : 3 * piece + 8, :] = vec


def outer_grad_kernel(place_ref, act_ref, d_ref, send_ref, keep_ref, *, piece):
    store_pieces(place_ref[1], tn(act_ref[...], d_ref[...]), piece, send_ref, keep_ref, 0)


def inner_grad_kernel(
    place_ref, first_ref, dinner_ref, mixed_ref, dbranch_ref, vec_ref, send_ref, keep_ref,
    *, piece, parts,
):
    step = pl.program_id(0)
    own = place_ref[1]
    for i in range(parts):

        @pl.when(step == i)
        def _():
            value = tn(first_ref[...], dinner_ref[...])
            store_pieces(own, value, piece, send_ref, keep_ref, i * piece)

    @pl.when(step == parts)
    def _():
        value = tn(mixed_ref[...], dbranch_ref[...])
        store_pieces(own, value, piece, send_ref, keep_ref, parts * piece)
        vec = vec_ref[...].astype(bf16)
        at = (parts + 1) * piece
        for m in range(send_ref.shape[0]):
            send_ref[m, at : at + VEC_ROWS, :] = vec
            keep_ref[m, at : at + VEC_ROWS, :] = vec


def tokens_grad_kernel(dr1_ref, dq0, dq1, dq2, dk_ref, dv_ref, wq_ref, wk_ref, wv_ref, out_ref):
    q = jnp.concatenate([dq0[...], dq1[...], dq2[...]], axis=1)
    total = dr1_ref[...] + nt(q, wq_ref[...])
    total = total + nt(dk_ref[...], wk_ref[...]) + nt(dv_ref[...], wv_ref[...])
    out_ref[...] = total.astype(bf16)


def flip(x, bit, count):
    return lax.ppermute(x, AXES, [(i, i ^ (1 << bit)) for i in range(count)])


def edges(doc_lengths):
    ends = jnp.cumsum(doc_lengths)
    return ends - doc_lengths, ends


def doc_start(starts, ends, t):
    return jnp.sum(jnp.where((starts <= t) & (t < ends), starts, 0))


def doc_end(starts, ends, t):
    return jnp.sum(jnp.where((starts <= t) & (t < ends), ends, 0))


def earlier_state(total, place, rows, count, starts, ends):
    base = place * rows
    before = jnp.zeros_like(total)
    entering = doc_start(starts, ends, base - 1)
    for bit in range(count.bit_length() - 1):
        size = 1 << bit
        theirs = flip(total.astype(bf16), bit, count).astype(f32)
        upper = (place >> bit) & 1
        low = (place >> bit) << bit
        take = (upper == 1) & (entering < low * rows)
        before = before + jnp.where(take | ((upper == 1) & (low == place)), theirs, 0.0)
        later = jnp.where(upper == 1, low, low + size)
        keep = doc_start(starts, ends, (later + size) * rows - 1) < later * rows
        mine_scale = jnp.where((upper == 1) | keep, 1.0, 0.0)
        their_scale = jnp.where((upper == 0) | keep, 1.0, 0.0)
        total = mine_scale * total + their_scale * theirs
    return before.astype(bf16)


def later_state(total, place, rows, count, starts, ends):
    after = jnp.zeros_like(total)
    leaving = doc_end(starts, ends, (place + 1) * rows)
    for bit in range(count.bit_length() - 1):
        size = 1 << bit
        theirs = flip(total.astype(bf16), bit, count).astype(f32)
        upper = (place >> bit) & 1
        low = (place >> bit) << bit
        take = (upper == 0) & ((leaving > (low + size) * rows) | (low + size == place + 1))
        after = after + jnp.where(take, theirs, 0.0)
        sooner = jnp.where(upper == 1, low - size, low)
        keep = doc_end(starts, ends, sooner * rows) > (sooner + size) * rows
        mine_scale = jnp.where((upper == 0) | keep, 1.0, 0.0)
        their_scale = jnp.where((upper == 1) | keep, 1.0, 0.0)
        total = mine_scale * total + their_scale * theirs
    return after.astype(bf16)


def shared_sum(send, keep, place, count, order):
    nbits = count.bit_length() - 1
    tail = send.shape[1:]
    left = list(range(nbits - 1, 0, -1))
    shape = (2,) * len(left) + tail
    keep = keep.reshape(shape)
    recv = flip(send, 0, count).reshape(shape)
    for bit in order:
        axis = left.index(bit)
        own = (place >> bit) & 1

        def part(which):
            a = lax.dynamic_index_in_dim(keep, which, axis, keepdims=False)
            b = lax.dynamic_index_in_dim(recv, which, axis, keepdims=False)
            return (a.astype(f32) + b.astype(f32)).astype(bf16)

        sent = part(1 - own)
        keep = part(own)
        recv = flip(sent, bit, count)
        left.remove(bit)
    return keep.astype(f32) + recv.astype(f32)


def block(shape, index):
    return pl.BlockSpec(shape, index)


def whole(shape):
    return pl.BlockSpec(shape, lambda i: (0,) * len(shape), pipeline_mode=pl.Buffered(1))


SMEM = pl.BlockSpec(memory_space=pltpu.SMEM)


def call(kernel, grid, in_specs, outs, out_specs, scratch, args, flops, vmem, moved=8e6):
    return pl.pallas_call(
        kernel,
        grid=(grid,),
        in_specs=in_specs,
        out_specs=out_specs,
        out_shape=[jax.ShapeDtypeStruct(s, d) for s, d in outs],
        scratch_shapes=scratch,
        compiler_params=pltpu.CompilerParams(
            dimension_semantics=("arbitrary",), vmem_limit_bytes=vmem * MIB
        ),
        cost_estimate=pl.CostEstimate(
            flops=int(flops), bytes_accessed=int(moved), transcendentals=0
        ),
    )(*args)


def per_device(
    tokens, out_grad, doc_lengths, w_query, b_query, w_key, b_key, w_value, b_value, w_output, b_output,
    w_inner, b_inner, w_outer, b_outer, gain_first, shift_first, gain_second, shift_second,
):
    rows, width = tokens.shape
    ff = w_inner.shape[1]
    count = lax.axis_size("wide") * lax.axis_size("narrow")
    place = lax.axis_index("wide") * lax.axis_size("narrow") + lax.axis_index("narrow")
    place = place.astype(jnp.int32)
    nchunk = rows // CHUNK
    npair = width // LANES
    heads = 2 * npair
    feat = heads * LANES
    nbits = count.bit_length() - 1
    starts, ends = edges(doc_lengths)
    spot = jnp.stack([place * rows, place & 1])
    vecs = jnp.concatenate(
        [
            jnp.stack(
                [b_query, b_key, b_value, b_output, gain_first, shift_first, b_outer, gain_second, shift_second]
            ),
            b_inner.reshape(-1, width),
        ]
    ).astype(f32)
    nvec = vecs.shape[0]
    at = lambda i: (i, 0)
    tile = block((CHUNK, width), at)
    ftile = block((CHUNK, feat), at)
    col = block((CHUNK, LANES), at)
    square = whole((width, width))
    vspec = whole((nvec, width))
    packed = (npair + 1, LANES, LANES)
    pspec = whole(packed)

    k, v, kf, cs, st, en, total = call(
        functools.partial(key_kernel, rows=rows),
        nchunk,
        [SMEM, SMEM, tile, square, square, vspec],
        [
            ((rows, width), bf16), ((rows, width), bf16), ((rows, feat), bf16),
            ((rows, LANES), f32), ((rows, LANES), jnp.int32), ((rows, LANES), jnp.int32), (packed, f32),
        ],
        [tile, tile, ftile, col, col, col, pl.BlockSpec(packed, lambda i: (0, 0, 0))],
        [],
        (spot, doc_lengths, tokens, w_key, w_value, vecs),
        4 * rows * width * width,
        32,
    )
    state_in = earlier_state(total, place, rows, count, starts, ends)

    q, qf = call(
        query_kernel,
        nchunk,
        [tile, square, vspec, col],
        [((rows, width), bf16), ((rows, feat), bf16)],
        [tile, ftile],
        [],
        (tokens, w_query, vecs, cs),
        2 * rows * width * width,
        32,
    )

    groups = 3
    gh = heads // groups
    locals_, kepts = [], []
    for n in range(groups):
        fcol = block((CHUNK, gh * LANES), lambda i, n=n: (i, n))
        vcol = block((CHUNK, gh * DH), lambda i, n=n: (i, n))
        o, kept = call(
            mixer_kernel,
            nchunk,
            [SMEM, fcol, fcol, vcol, col, col],
            [((rows, gh * LANES), f32), ((nchunk, gh, LANES, LANES), bf16)],
            [block((CHUNK, gh * LANES), at), pl.BlockSpec((1, gh, LANES, LANES), lambda i: (i, 0, 0, 0))],
            [pltpu.VMEM((gh, LANES, LANES), f32)],
            (spot, qf, kf, v, st, en),
            8 * rows * gh * LANES * CHUNK,
            32,
        )
        locals_.append(o)
        kepts.append(kept)

    ftile_ff = block((CHUNK, ff), at)
    otile = block((CHUNK, gh * LANES), at)
    (result, mixed, first, act, d_outer, d_inner, d_branch, d_r1, dn, back, vgrad) = call(
        functools.partial(token_kernel, split=4),
        nchunk,
        [
            SMEM, otile, otile, otile, ftile, pspec, col, tile, tile,
            square, whole((width, ff)), whole((ff, width)), vspec,
        ],
        [
            ((rows, width), bf16), ((rows, width), bf16), ((rows, width), bf16), ((rows, ff), bf16),
            ((rows, width), bf16), ((rows, ff), bf16), ((rows, width), bf16), ((rows, width), f32),
            ((rows, feat), bf16), (packed, f32), ((VEC_ROWS, width), f32),
        ],
        [
            tile, tile, tile, ftile_ff, tile, ftile_ff, tile, tile, ftile,
            pl.BlockSpec(packed, lambda i: (0, 0, 0)), pl.BlockSpec((VEC_ROWS, width), lambda i: (0, 0)),
        ],
        [
            pltpu.VMEM((heads, LANES, LANES), bf16),
            pltpu.VMEM((CHUNK, width), f32),
            pltpu.VMEM((CHUNK, width), f32),
            pltpu.VMEM((CHUNK, ff), f32),
        ],
        (spot, *locals_, qf, state_in, st, tokens, out_grad, w_output, w_inner, w_outer, vecs),
        8 * rows * width * ff + 4 * rows * width * width,
        60,
    )
    back_in = later_state(back, place, rows, count, starts, ends)

    half = count // 2
    piece_o = ff // count
    per_step = width // piece_o
    hspec = pl.BlockSpec((per_step // 2, piece_o, width), lambda i: (i, 0, 0))
    send, keep = call(
        functools.partial(outer_grad_kernel, piece=piece_o),
        ff // width,
        [SMEM, block((rows, width), lambda i: (0, i)), whole((rows, width))],
        [((half, piece_o, width), bf16)] * 2,
        [hspec, hspec],
        [],
        (spot, act, d_outer),
        2 * rows * width * ff,
        40,
    )
    up = list(range(1, nbits))
    swapped = up[:2][::-1] + up[2:]
    sum_outer = shared_sum(send, keep, place, count, up)

    piece = width // count
    parts = ff // width
    depth = (parts + 1) * piece + VEC_ROWS
    full = pl.BlockSpec((half, depth, width), lambda i: (0, 0, 0))
    send, keep = call(
        functools.partial(inner_grad_kernel, piece=piece, parts=parts),
        parts + 1,
        [
            SMEM, whole((rows, width)), block((rows, width), lambda i: (0, jnp.minimum(i, parts - 1))),
            whole((rows, width)), whole((rows, width)), whole((VEC_ROWS, width)),
        ],
        [((half, depth, width), bf16)] * 2,
        [full, full],
        [],
        (spot, first, d_inner, mixed, d_branch, vgrad),
        2 * rows * width * ff + 2 * rows * width * width,
        50,
    )
    sum_inner = shared_sum(send, keep, place, count, swapped)

    back_at = lambda i: (nchunk - 1 - i, 0)
    dqs, dks, dvs = [], [], []
    for n in range(groups):
        fcol = block((CHUNK, gh * LANES), lambda i, n=n: (nchunk - 1 - i, n))
        vcol = block((CHUNK, gh * DH), lambda i, n=n: (nchunk - 1 - i, n))
        bcol = block((CHUNK, LANES), back_at)
        grad = block((CHUNK, gh * DH), back_at)
        dq, dk, dv = call(
            functools.partial(mixer_back_kernel, pair0=n * gh // 2, npair=npair, nchunk=nchunk),
            nchunk,
            [
                SMEM, fcol, fcol, vcol, fcol, vcol,
                pl.BlockSpec((1, gh, LANES, LANES), lambda i: (nchunk - 1 - i, 0, 0, 0)), pspec, bcol, bcol, bcol,
            ],
            [((rows, gh * DH), bf16), ((rows, gh * DH), f32), ((rows, gh * DH), f32)],
            [grad, grad, grad],
            [pltpu.VMEM((gh, LANES, LANES), f32)],
            (spot, qf, kf, v, dn, q, kepts[n], state_in, st, en, cs),
            20 * rows * gh * LANES * CHUNK,
            32,
        )
        dqs.append(dq)
        dks.append(dk)
        dvs.append(dv)

    last = lambda i: (jnp.minimum(i, nchunk - 1), 0)
    gtile = block((CHUNK, gh * DH), last)
    ltile = block((CHUNK, width), last)
    lcol = block((CHUNK, LANES), last)
    qwhole = whole((rows, gh * DH))
    depth_q = 3 * piece + 8
    fullq = pl.BlockSpec((half, depth_q, width), lambda i: (0, 0, 0))
    d_key, d_value, send, keep = call(
        functools.partial(qkv_back_kernel, rows=rows, nchunk=nchunk, piece=piece),
        nchunk + 1,
        [
            SMEM, gtile, gtile, gtile, gtile, gtile, gtile, qwhole, qwhole, qwhole,
            ltile, block((CHUNK, feat), last), ltile, pspec, lcol, lcol, whole((rows, width)),
        ],
        [((rows, width), bf16)] * 2 + [((half, depth_q, width), bf16)] * 2,
        [ltile, ltile, fullq, fullq],
        [
            pltpu.VMEM((rows, width), bf16),
            pltpu.VMEM((rows, width), bf16),
            pltpu.VMEM((8, width), f32),
        ],
        (spot, *dks, *dvs, *dqs, k, kf, v, back_in, en, cs, tokens),
        6 * rows * width * width,
        50,
    )
    sum_qkv = shared_sum(send, keep, place, count, up)

    qtile = block((CHUNK, gh * DH), at)
    (grad_tokens,) = call(
        tokens_grad_kernel,
        nchunk,
        [tile, qtile, qtile, qtile, tile, tile, square, square, square],
        [((rows, width), bf16)],
        [tile],
        [],
        (d_r1, *dqs, d_key, d_value, w_query, w_key, w_value),
        6 * rows * width * width,
        32,
    )

    g_outer = sum_outer
    g_inner = jnp.concatenate([sum_inner[i * piece : (i + 1) * piece] for i in range(parts)], axis=1)
    g_output = sum_inner[parts * piece : (parts + 1) * piece]
    vec = sum_inner[(parts + 1) * piece :]
    vec_q = sum_qkv[3 * piece :]

    def share(line, r):
        return lax.dynamic_slice(line[r], (place * piece,), (piece,))

    b_inner_sum = lax.dynamic_slice(
        vec[V_B1 : V_B1 + parts].reshape(-1), (place * (ff // count),), (ff // count,)
    )
    return (
        result,
        grad_tokens,
        sum_qkv[:piece],
        share(vec_q, 0),
        sum_qkv[piece : 2 * piece],
        share(vec_q, 1),
        sum_qkv[2 * piece : 3 * piece],
        share(vec_q, 2),
        g_output,
        share(vec, V_BO),
        g_inner,
        b_inner_sum,
        g_outer,
        share(vec, V_B2),
        share(vec, V_G1),
        share(vec, V_E1),
        share(vec, V_G2),
        share(vec, V_E2),
    )


def solution(mesh):
    split = P(AXES, None)
    line = P(AXES)
    return jax.shard_map(
        per_device,
        mesh=mesh,
        in_specs=(split, split) + (P(),) * 17,
        out_specs=(split, split) + (split, line) * 6 + (line,) * 4,
        check_vma=False,
    )
```

```python
import functools
import math

import jax
import jax.numpy as jnp
from jax import lax
from jax.experimental import pallas as pl
from jax.experimental.pallas import tpu as pltpu
from jax.sharding import PartitionSpec as P

DH = 64
LANES = 128
CHUNK = 256
SLICE = 16
EPS = 1e-05
HALF_PI = math.pi / 2.0
MIB = 1 << 20
VMEM = 60
COST = 10
FILL = 40
AXES = ("wide", "narrow")

f32 = jnp.float32
bf16 = jnp.bfloat16

R_BQ, R_BK, R_BV, R_BO, R_G1, R_E1, R_B2, R_G2, R_E2, R_B1 = range(10)
V_B2, V_G2, V_E2, V_G1, V_E1, V_BO, V_B1 = range(7)
VEC_ROWS = 16


def nn(a, b):
    return jnp.dot(a, b, preferred_element_type=f32)


def nt(a, b):
    return lax.dot_general(a, b, (((1,), (1,)), ((), ())), preferred_element_type=f32)


def tn(a, b):
    return lax.dot_general(a, b, (((0,), (0,)), ((), ())), preferred_element_type=f32)


def lane_iota(rows, lanes=LANES):
    return lax.broadcasted_iota(jnp.int32, (rows, lanes), 1)


def row_iota(rows, lanes=LANES):
    return lax.broadcasted_iota(jnp.int32, (rows, lanes), 0)


def swap_halves(x):
    return pltpu.roll(x, DH, 1)


def softplus(x):
    return jnp.maximum(x, 0.0) + jnp.log1p(jnp.exp(-jnp.abs(x)))


def sigmoid(x):
    return 1.0 / (1.0 + jnp.exp(-x))


def sine(b):
    s = b * b
    p = 1.0 / 6227020800.0
    for c in (-1.0 / 39916800.0, 1.0 / 362880.0, -1.0 / 5040.0, 1.0 / 120.0, -1.0 / 6.0):
        p = p * s + c
    return b + b * s * p


def features(pair, cs, lo):
    soft = softplus(pair)
    other = swap_halves(soft)
    return (
        (jnp.where(lo, soft, other) * cs).astype(bf16),
        (jnp.where(lo, other, soft) * cs).astype(bf16),
    )


def extended(v, lo):
    one = jnp.ones_like(v)
    return jnp.where(lo, v, one), jnp.where(lo, one, v)


def pairs_of(width):
    return width // LANES


def lookup(len_ref, pos):
    start = jnp.zeros(pos.shape, jnp.int32)
    end = jnp.zeros(pos.shape, jnp.int32)
    edge = jnp.int32(0)
    for doc in range(len_ref.shape[0]):
        here = pos >= edge
        after = edge + len_ref[doc]
        start = jnp.where(here, edge, start)
        end = jnp.where(here, after, end)
        edge = after
    return start, end


F_BEFORE, F_NEXT_B, F_AFTER, F_NEXT_A, F_CLOSING, F_OPENING = range(6)


def flag_table(len_ref, place, rows):
    bit, lane = row_iota(8), lane_iota(8)
    upper = jnp.bitwise_and(jnp.right_shift(jnp.full_like(bit, place), bit), 1) == 1
    base, close = place * rows, (place + 1) * rows
    is_before = (lane == F_BEFORE) | (lane == F_NEXT_B)
    is_after = (lane == F_AFTER) | (lane == F_NEXT_A)
    pos = jnp.where(
        is_before,
        base - 1,
        jnp.where(is_after, close, jnp.where(lane == F_CLOSING, close - 1, base)),
    )
    start, end = lookup(len_ref, pos)
    one, zero = jnp.ones(bit.shape, f32), jnp.zeros(bit.shape, f32)
    is_long = jnp.where((end - start) > rows, one, zero)
    near = jnp.where((pos >= 0) & (pos < end), 1.0 - is_long, zero)
    out = is_long
    out = jnp.where(lane == F_BEFORE, jnp.where(upper, is_long, zero), out)
    out = jnp.where(lane == F_AFTER, jnp.where(upper, zero, is_long), out)
    return jnp.where((lane == F_NEXT_B) | (lane == F_NEXT_A), near, out)


def key_kernel(
    spot_ref, len_ref, x_ref, wk_ref, wv_ref,
    bq, bk, bv, bo, g1, e1, b2, g2, e2, b1,
    k_ref, v_ref, kf_ref, cs_ref, st_ref, en_ref, state_ref, next_ref, flag_ref, vec_ref,
    total,
    *, rows,
):
    step = pl.program_id(0)
    base = spot_ref[0]
    width = x_ref.shape[1]
    first = base + step * CHUNK
    pos = first + row_iota(CHUNK)
    lane = lane_iota(CHUNK)
    lo = lane < DH

    @pl.when(step == 0)
    def _():
        total[...] = jnp.zeros_like(total)
        flag_ref[...] = flag_table(len_ref, spot_ref[1], rows)
        for r, ref in enumerate((bq, bk, bv, bo, g1, e1, b2, g2, e2)):
            vec_ref[r : r + 1, :] = ref[...].astype(f32).reshape(1, width)
        for r in range(b1.shape[0] // width):
            vec_ref[R_B1 + r : R_B1 + r + 1, :] = (
                b1[r * width : (r + 1) * width].astype(f32).reshape(1, width)
            )

    start, end = lookup(len_ref, pos)
    part = jnp.where(lo, end - pos, pos - start).astype(f32)
    cs = sine(HALF_PI * part / (end - start).astype(f32))
    cs_ref[...] = cs
    st_ref[...] = start
    en_ref[...] = end

    x = x_ref[...]
    k = (nn(x, wk_ref[...]) + vec_ref[R_BK : R_BK + 1, :]).astype(bf16)
    v = (nn(x, wv_ref[...]) + vec_ref[R_BV : R_BV + 1, :]).astype(bf16)
    k_ref[...] = k
    v_ref[...] = v
    closing = end >= base + rows
    slots = lane_iota(LANES)
    lo_state = slots < DH

    npair = pairs_of(width)
    zcol = jnp.zeros((LANES, LANES), f32)
    for g in range(npair):
        cols = slice(g * LANES, (g + 1) * LANES)
        fa, fb = features(k[:, cols].astype(f32), cs, lo)
        kf_ref[:, 2 * g * LANES : (2 * g + 1) * LANES] = fa
        kf_ref[:, (2 * g + 1) * LANES : (2 * g + 2) * LANES] = fb
        va, vb = extended(v[:, cols], lo)
        zero = jnp.zeros_like(fa)
        sa = tn(jnp.where(closing, fa, zero), va)
        sb = tn(jnp.where(closing, fb, zero), vb)
        total[g] += jnp.where(lo_state, sa, sb)
        zcol = jnp.where(slots == DH + g, sa, jnp.where(slots == g, sb, zcol))
    total[npair] += zcol

    @pl.when(step == pl.num_programs(0) - 1)
    def _():
        split_long(total[...], flag_ref[0:1, F_CLOSING : F_CLOSING + 1], state_ref, next_ref)


def split_long(total, flag, long_ref, next_ref):
    long_ref[...] = (total * flag).astype(bf16)
    next_ref[...] = (total * (1.0 - flag)).astype(bf16)


def taken_sum(refs, flags, lane):
    *scans, near = refs
    total = near[...].astype(f32) * flags[0:1, lane + 1 : lane + 2]
    for bit, ref in enumerate(scans):
        total = total + ref[...].astype(f32) * flags[bit : bit + 1, lane : lane + 1]
    return total.astype(bf16)


def unpack_state(state_ref, g, npair, lo, slots):
    pair = state_ref[g].astype(f32)
    z = state_ref[npair].astype(f32)
    za = z[:, DH + g : DH + g + 1]
    zb = z[:, g : g + 1]
    return jnp.where(lo, pair, za), jnp.where(lo, zb, pair)


def unpack_grad_state(state_ref, g, npair, lo, slots):
    pair = state_ref[g].astype(f32)
    z = state_ref[npair].astype(f32)
    za = jnp.where(slots == DH, z[:, DH + g : DH + g + 1], 0.0)
    zb = jnp.where(slots == 0, z[:, g : g + 1], 0.0)
    return jnp.where(lo, pair, za), jnp.where(lo, zb, pair)


def query_kernel(spot_ref, x_ref, wq_ref, vec_ref, cs_ref, q_ref, qf_ref):
    q = (nn(x_ref[...], wq_ref[...]) + vec_ref[R_BQ : R_BQ + 1, :]).astype(bf16)
    q_ref[...] = q
    lo = lane_iota(CHUNK) < DH
    cs = cs_ref[...]
    for g in range(pairs_of(q.shape[1])):
        fa, fb = features(q[:, g * LANES : (g + 1) * LANES].astype(f32), cs, lo)
        qf_ref[:, 2 * g * LANES : (2 * g + 1) * LANES] = fa
        qf_ref[:, (2 * g + 1) * LANES : (2 * g + 2) * LANES] = fb


def mixer_kernel(spot_ref, qf_ref, kf_ref, v_ref, st_ref, en_ref, o_ref, kept_ref, local):
    step = pl.program_id(0)
    first = spot_ref[0] + step * CHUNK
    start, end = st_ref[...], en_ref[...]
    start2 = jnp.concatenate([start, start], axis=1)
    ipos = first + row_iota(CHUNK, CHUNK)
    jpos = first + lane_iota(CHUNK, CHUNK)
    mask = (jpos <= ipos) & (jpos >= start2)
    carried = start < first
    closing = end >= first + CHUNK
    keep = start[CHUNK - 1 : CHUNK, :] < first
    lo = lane_iota(CHUNK) < DH

    @pl.when(step == 0)
    def _():
        local[...] = jnp.zeros_like(local)

    for g in range(pairs_of(v_ref.shape[1])):
        vs = extended(v_ref[:, g * LANES : (g + 1) * LANES], lo)
        for s in range(2):
            h = 2 * g + s
            cols = slice(h * LANES, (h + 1) * LANES)
            qf, kf, v = qf_ref[:, cols], kf_ref[:, cols], vs[s]
            probs = jnp.where(mask, nt(qf, kf), 0.0).astype(bf16)
            held = local[h].astype(bf16)
            kept_ref[0, h] = held
            o_ref[:, cols] = nn(probs, v) + jnp.where(carried, nn(qf, held), 0.0)
            local[h] = jnp.where(keep, local[h], 0.0) + tn(
                jnp.where(closing, kf, jnp.zeros_like(kf)), v
            )


def gelu_and_slope(u):
    z = jnp.abs(u) * (1.0 / math.sqrt(2.0))
    t = 1.0 / (1.0 + 0.3275911 * z)
    p = 0.5 * 1.061405429
    for c in (-1.453152027, 1.421413741, -0.284496736, 0.254829592):
        p = p * t + 0.5 * c
    e = jnp.exp(-0.5 * u * u)
    tail = p * t * e
    gauss = jnp.where(u >= 0.0, 1.0 - tail, tail)
    return u * gauss, gauss + u * e * (1.0 / math.sqrt(2.0 * math.pi))


def token_kernel(
    spot_ref, o0_ref, o1_ref, o2_ref, qf_ref, st_ref, x_ref, go_ref,
    wo_ref, w1_ref, w2_ref, vec_ref, flag_ref, *refs, split, scans,
):
    theirs = refs[:scans]
    (
        out_ref, mixed_ref, first_ref, act_ref, douter_ref, dinner_ref, dbranch_ref, dr1_ref,
        dn_ref, back_ref, near_ref, vgrad_ref, state_ref,
        states, ratio, rden_s, slope, back_s, flow, norm_s, rstd_s, sums,
    ) = refs[scans:]
    step = pl.program_id(0)
    base = spot_ref[0]
    chunk, width = x_ref.shape
    ff = w1_ref.shape[1]
    npair = pairs_of(width)
    lane = lane_iota(chunk)
    lo = lane < DH
    slots = lane_iota(LANES)
    lo_state = slots < DH
    start = st_ref[...]

    @pl.when(step == 0)
    def _():
        state_ref[...] = taken_sum(theirs, flag_ref[...], F_BEFORE)
        for g in range(npair):
            a, b = unpack_state(state_ref, g, npair, lo_state, slots)
            states[2 * g] = a.astype(bf16)
            states[2 * g + 1] = b.astype(bf16)
        back_s[...] = jnp.zeros_like(back_s)
        sums[...] = jnp.zeros_like(sums)

    carried = start < base
    o_refs = (o0_ref, o1_ref, o2_ref)
    for g in range(npair):
        both = []
        for s in range(2):
            h = 2 * g + s
            o_of = o_refs[h // 4]
            local = o_of[:, (h % 4) * LANES : (h % 4 + 1) * LANES]
            far = nn(qf_ref[:, h * LANES : (h + 1) * LANES], states[h])
            both.append(local + jnp.where(carried, far, 0.0))
        numer = jnp.where(lo, both[0], both[1])
        rden = 1.0 / swap_halves(jnp.where(lo, both[1], both[0]))
        cols = slice(g * LANES, (g + 1) * LANES)
        rden_s[:, cols] = rden
        mix = numer * rden
        ratio[:, cols] = mix
        mixed_ref[:, cols] = mix.astype(bf16)

    def row(r):
        return vec_ref[r : r + 1, :]

    def mean(v):
        return jnp.sum(v, axis=-1, keepdims=True) * (1.0 / width)

    def norm(resid):
        cent = resid - mean(resid)
        rstd = lax.rsqrt(mean(cent * cent) + EPS)
        return cent * rstd, rstd

    def norm_back(grad, normed, rstd, gain):
        d_n = grad * gain
        return rstd * (d_n - mean(d_n) - normed * mean(d_n * normed))

    def add_sum(r, v, cols=slice(None)):
        sums[8 * r : 8 * r + 8, cols] += v

    flow[...] = nn(mixed_ref[...], wo_ref[...])
    for at in range(0, chunk, SLICE):
        sl = slice(at, at + SLICE)
        n1, rstd1 = norm(x_ref[sl, :].astype(f32) + flow[sl, :] + row(R_BO))
        norm_s[sl, :] = n1
        rstd_s[sl, :] = jnp.broadcast_to(rstd1, (SLICE, LANES))
        first_ref[sl, :] = (n1 * row(R_G1) + row(R_E1)).astype(bf16)

    part = ff // split

    def inner_of(i):
        flat, off = i * part // width, i * part % width
        bias = vec_ref[R_B1 + flat : R_B1 + flat + 1, off : off + part]
        return nn(first_ref[...], w1_ref[:, i * part : (i + 1) * part]) + bias

    ahead = inner_of(0)
    outer = jnp.zeros((chunk, width), f32)
    last = None
    for i in range(split):
        cols = slice(i * part, (i + 1) * part)
        now = ahead
        if i + 1 < split:
            ahead = inner_of(i + 1)
        if last is not None:
            outer = outer + nn(last, w2_ref[(i - 1) * part : i * part, :])
        act, sl = gelu_and_slope(now)
        last = act.astype(bf16)
        act_ref[:, cols] = last
        slope[:, cols] = sl
    flow[...] = outer + nn(last, w2_ref[(split - 1) * part :, :])

    g2_sum = e2_sum = b2_sum = jnp.zeros((8, width), f32)
    for at in range(0, chunk, SLICE):
        sl = slice(at, at + SLICE)
        n2, rstd2 = norm(first_ref[sl, :].astype(f32) + flow[sl, :] + row(R_B2))
        out_ref[sl, :] = (n2 * row(R_G2) + row(R_E2)).astype(bf16)
        grad = go_ref[sl, :].astype(f32)
        g2_sum = g2_sum + fold_rows(grad * n2)
        e2_sum = e2_sum + fold_rows(grad)
        d_r2 = norm_back(grad, n2, rstd2, row(R_G2))
        b2_sum = b2_sum + fold_rows(d_r2)
        douter_ref[sl, :] = d_r2.astype(bf16)
        dr1_ref[sl, :] = d_r2
    add_sum(V_G2, g2_sum)
    add_sum(V_E2, e2_sum)
    add_sum(V_B2, b2_sum)

    for i in range(split):
        cols = slice(i * part, (i + 1) * part)
        flat = i * part // width
        off = i * part % width
        d_inner = nt(douter_ref[...], w2_ref[cols, :]) * slope[:, cols]
        dinner_ref[:, cols] = d_inner.astype(bf16)
        add_sum(V_B1 + flat, fold_rows(d_inner), slice(off, off + part))
    flow[...] = nt(dinner_ref[...], w1_ref[...])

    g1_sum = e1_sum = bo_sum = jnp.zeros((8, width), f32)
    for at in range(0, chunk, SLICE):
        sl = slice(at, at + SLICE)
        d_first = dr1_ref[sl, :] + flow[sl, :]
        n1 = norm_s[sl, :]
        g1_sum = g1_sum + fold_rows(d_first * n1)
        e1_sum = e1_sum + fold_rows(d_first)
        d_r1 = norm_back(d_first, n1, rstd_s[sl, 0:1], row(R_G1))
        bo_sum = bo_sum + fold_rows(d_r1)
        dr1_ref[sl, :] = d_r1
        dbranch_ref[sl, :] = d_r1.astype(bf16)
    add_sum(V_G1, g1_sum)
    add_sum(V_E1, e1_sum)
    add_sum(V_BO, bo_sum)

    flow[...] = nt(dbranch_ref[...], wo_ref[...])
    opening = start <= base
    zcol = jnp.zeros((LANES, LANES), f32)
    for g in range(npair):
        cols = slice(g * LANES, (g + 1) * LANES)
        dn = flow[:, cols] * rden_s[:, cols]
        prod = dn * ratio[:, cols]
        dda = -jnp.sum(jnp.where(lo, prod, 0.0), axis=1, keepdims=True)
        ddb = -jnp.sum(jnp.where(lo, 0.0, prod), axis=1, keepdims=True)
        hia, hib = dda.astype(bf16).astype(f32), ddb.astype(bf16).astype(f32)
        exa = jnp.where(lane == DH, hia, jnp.where(lane == DH + 1, dda - hia, 0.0))
        exb = jnp.where(lane == 0, hib, jnp.where(lane == 1, ddb - hib, 0.0))
        dna = jnp.where(lo, dn, exa).astype(bf16)
        dnb = jnp.where(lo, exb, dn).astype(bf16)
        ca = slice(2 * g * LANES, (2 * g + 1) * LANES)
        cb = slice((2 * g + 1) * LANES, (2 * g + 2) * LANES)
        dn_ref[:, ca] = dna
        dn_ref[:, cb] = dnb
        zero = jnp.zeros((chunk, LANES), bf16)
        ga = tn(jnp.where(opening, qf_ref[:, ca], zero), dna)
        gb = tn(jnp.where(opening, qf_ref[:, cb], zero), dnb)
        back_s[g] += jnp.where(lo_state, ga, gb)
        za = ga[:, DH : DH + 1] + ga[:, DH + 1 : DH + 2]
        zb = gb[:, 0:1] + gb[:, 1:2]
        zcol = jnp.where(slots == DH + g, za, jnp.where(slots == g, zb, zcol))
    back_s[npair] += zcol

    @pl.when(step == pl.num_programs(0) - 1)
    def _():
        split_long(back_s[...], flag_ref[0:1, F_OPENING : F_OPENING + 1], back_ref, near_ref)
        vgrad_ref[...] = jnp.zeros_like(vgrad_ref)
        for r in range(sums.shape[0] // 8):
            vgrad_ref[r : r + 1, :] = jnp.sum(sums[8 * r : 8 * r + 8, :], axis=0, keepdims=True)


def fold_rows(v):
    return jnp.sum(v.reshape(v.shape[0] // 8, 8, v.shape[1]), axis=0)


def store_pieces(own, value, rows, send_ref, keep_ref, at):
    count = value.shape[0] // rows
    value = value.astype(bf16)
    for bit in range(2):

        @pl.when(own == bit)
        def _():
            for d in range(count):
                ref = keep_ref if d % 2 == bit else send_ref
                ref[d // 2, at : at + rows, :] = value[d * rows : (d + 1) * rows, :]


def store_lines(line, send_ref, keep_ref, at):
    line = line.astype(bf16)
    for m in range(send_ref.shape[0]):
        send_ref[m, at : at + line.shape[0], :] = line
        keep_ref[m, at : at + line.shape[0], :] = line


def query_back_kernel(
    spot_ref, qf_ref, kf_ref, v_ref, dn_ref, q_ref, kept0, kept1, kept2, state_ref,
    st_ref, cs_ref, x_ref, mixed_ref, dbranch_ref, vec_ref,
    dq_ref, send_ref, keep_ref,
    grads, lines,
    *, npair, nchunk, piece,
):
    step = pl.program_id(0)
    base = spot_ref[0]
    keepers = (kept0, kept1, kept2)

    @pl.when(step == 0)
    def _():
        lines[...] = jnp.zeros_like(lines)

    @pl.when(step < nchunk)
    def _():
        lo = lane_iota(CHUNK) < DH
        slots = lane_iota(LANES)
        lo_state = slots < DH
        first = base + step * CHUNK
        start, cs = st_ref[...], cs_ref[...]
        start2 = jnp.concatenate([start, start], axis=1)
        ipos = first + row_iota(CHUNK, CHUNK)
        jpos = first + lane_iota(CHUNK, CHUNK)
        mask = (jpos <= ipos) & (jpos >= start2)
        carried = start < first
        from_far = start[0:1, :] < base
        at = pl.ds(pl.multiple_of(step * CHUNK, CHUNK), CHUNK)
        for g in range(npair):
            pair = slice(g * LANES, (g + 1) * LANES)
            vs = extended(v_ref[:, pair], lo)
            far = unpack_state(state_ref, g, npair, lo_state, slots)
            dns = [dn_ref[:, (2 * g + s) * LANES : (2 * g + s + 1) * LANES] for s in range(2)]
            d_probs = [nt(dns[s], vs[s]) for s in range(2)]
            d_probs = [jnp.where(mask, d, 0.0).astype(bf16) for d in d_probs]
            held = [
                (keepers[h // 4][0, h % 4].astype(f32) + jnp.where(from_far, far[h - 2 * g], 0.0)).astype(bf16)
                for h in (2 * g, 2 * g + 1)
            ]
            d_qf = [
                nn(d_probs[s], kf_ref[:, (2 * g + s) * LANES : (2 * g + s + 1) * LANES])
                + jnp.where(carried, nt(dns[s], held[s]), 0.0)
                for s in range(2)
            ]
            turned = [d * cs for d in d_qf]
            turned = [t + swap_halves(t) for t in turned]
            value = jnp.where(lo, turned[0], turned[1]) * sigmoid(q_ref[:, pair].astype(f32))
            lines[0:8, pair] += fold_rows(value)
            value = value.astype(bf16)
            dq_ref[:, pair] = value
            grads[at, pair] = value

    @pl.when(step == nchunk)
    def _():
        own = spot_ref[2]
        store_pieces(own, tn(x_ref[...], grads[...]), piece, send_ref, keep_ref, 0)
        store_pieces(own, tn(mixed_ref[...], dbranch_ref[...]), piece, send_ref, keep_ref, piece)
        total = jnp.sum(lines[...], axis=0, keepdims=True)
        vec = jnp.where(row_iota(VEC_ROWS, total.shape[1]) == VEC_ROWS - 1, total, vec_ref[...])
        store_lines(vec, send_ref, keep_ref, 2 * piece)


def value_back_kernel(
    spot_ref, qf_ref, kf_ref, v_ref, dn_ref, k_ref, back_ref, st_ref, en_ref, cs_ref, x_ref,
    dk_ref, dv_ref, send_ref, keep_ref,
    onward_state, grads, lines,
    *, pair0, npair, nchunk, piece, rows,
):
    base = spot_ref[0]
    wide = v_ref.shape[1]

    @pl.when(pl.program_id(0) == 0)
    def _():
        onward_state[...] = jnp.zeros_like(onward_state)
        lines[...] = jnp.zeros_like(lines)

    @pl.when(pl.program_id(0) < nchunk)
    def _():
        lo = lane_iota(CHUNK) < DH
        slots = lane_iota(LANES)
        lo_state = slots < DH
        step = nchunk - 1 - pl.program_id(0)
        first = base + step * CHUNK
        start, end, cs = st_ref[...], en_ref[...], cs_ref[...]
        end2 = jnp.concatenate([end, end], axis=1)
        jpos = first + row_iota(CHUNK, CHUNK)
        ipos = first + lane_iota(CHUNK, CHUNK)
        mask = (jpos <= ipos) & (ipos < end2)
        onward = end > first + CHUNK
        opening = start <= first
        to_far = end[CHUNK - 1 : CHUNK, :] > base + rows
        keep = end[0:1, :] > first + CHUNK
        at = pl.ds(pl.multiple_of(step * CHUNK, CHUNK), CHUNK)
        zero = jnp.zeros((CHUNK, LANES), bf16)
        two = range(2)
        for g in range(pairs_of(wide)):
            pair = slice(g * LANES, (g + 1) * LANES)
            cols = [slice((2 * g + s) * LANES, (2 * g + s + 1) * LANES) for s in two]
            vs = extended(v_ref[:, pair], lo)
            far = unpack_grad_state(back_ref, pair0 + g, npair, lo_state, slots)
            qf, kf = [qf_ref[:, c] for c in cols], [kf_ref[:, c] for c in cols]
            dn = [dn_ref[:, c] for c in cols]
            probs = [nt(kf[s], qf[s]) for s in two]
            d_probs = [nt(vs[s], dn[s]) for s in two]
            probs = [jnp.where(mask, p, 0.0).astype(bf16) for p in probs]
            d_probs = [jnp.where(mask, p, 0.0).astype(bf16) for p in d_probs]
            ahead = [onward_state[2 * g + s] for s in two]
            ahead16 = [(ahead[s] + jnp.where(to_far, far[s], 0.0)).astype(bf16) for s in two]
            more = [tn(jnp.where(opening, qf[s], zero), dn[s]) for s in two]
            d_kf = [nn(d_probs[s], qf[s]) + jnp.where(onward, nt(vs[s], ahead16[s]), 0.0) for s in two]
            d_v = [nn(probs[s], dn[s]) + jnp.where(onward, nn(kf[s], ahead16[s]), 0.0) for s in two]
            for s in two:
                onward_state[2 * g + s] = jnp.where(keep, ahead[s], 0.0) + more[s]
            turned = [d * cs for d in d_kf]
            turned = [t + swap_halves(t) for t in turned]
            both = (
                (jnp.where(lo, turned[0], turned[1]) * sigmoid(k_ref[:, pair].astype(f32)), dk_ref),
                (jnp.where(lo, d_v[0], d_v[1]), dv_ref),
            )
            for n, (value, ref) in enumerate(both):
                spread = slice(n * wide + g * LANES, n * wide + (g + 1) * LANES)
                lines[0:8, spread] += fold_rows(value)
                value = value.astype(bf16)
                ref[:, pair] = value
                grads[at, spread] = value

    @pl.when(pl.program_id(0) == nchunk)
    def _():
        store_pieces(spot_ref[2], tn(x_ref[...], grads[...]), piece, send_ref, keep_ref, 0)
        total = jnp.sum(lines[...], axis=0, keepdims=True)
        store_lines(jnp.broadcast_to(total, lines.shape), send_ref, keep_ref, piece)


def outer_grad_kernel(spot_ref, act_ref, d_ref, send_ref, keep_ref, *, piece):
    store_pieces(spot_ref[2], tn(act_ref[...], d_ref[...]), piece, send_ref, keep_ref, 0)


def inner_grad_kernel(spot_ref, first_ref, dinner_ref, send_ref, keep_ref, *, piece, parts):
    for i in range(parts):

        @pl.when(pl.program_id(0) == i)
        def _():
            value = tn(first_ref[...], dinner_ref[...])
            store_pieces(spot_ref[2], value, piece, send_ref, keep_ref, i * piece)


def tokens_grad_kernel(spot_ref, dr1_ref, q_ref, k0, k1, v0, v1, wq_ref, wk_ref, wv_ref, out_ref):
    total = dr1_ref[...] + nt(q_ref[...], wq_ref[...])
    for refs, w in (((k0, k1), wk_ref), ((v0, v1), wv_ref)):
        total = total + nt(jnp.concatenate([r[...] for r in refs], axis=1), w[...])
    out_ref[...] = total.astype(bf16)


def taken_kernel(spot_ref, *refs, lane):
    *theirs, flag_ref, out_ref = refs
    out_ref[...] = taken_sum(theirs, flag_ref[...], lane)


def exchange(x, mask, count):
    return lax.ppermute(x, AXES, [(i, i ^ mask) for i in range(count)])


def flip(x, bit, count):
    return exchange(x, 1 << bit, count)


class Halving:

    def __init__(self, send, keep, count, order):
        self.count = count
        self.left = list(range(count.bit_length() - 2, 0, -1))
        self.order = list(order)
        self.tail = send.shape[1:]
        self.keep = keep
        self.recv = flip(send, 0, count)

    def advance(self):
        self.bit = self.order.pop(0)
        axis = self.left.index(self.bit)
        self.a, self.b = 1 << axis, 1 << (len(self.left) - 1 - axis)
        self.left.remove(self.bit)
        view = (self.a, 2, self.b, *self.tail)
        full = jax.ShapeDtypeStruct((self.a, self.b, *self.tail), bf16)
        return self.keep.reshape(view), self.recv.reshape(view), full

    def specs(self, steps):
        keep, recv, full = self.advance()
        bit, rank = self.bit, len(self.tail)
        used = min(self.a * self.b, 4, steps)
        while used & (used - 1):
            used -= 1
        ca = min(self.a, used)
        cb = used // ca
        shape = (self.a // ca, None, self.b // cb, *self.tail)

        def index(i, spot, other):
            i = jnp.minimum(i, used - 1)
            own = spot[2 + bit]
            return (i // cb, 1 - own if other else own, i % cb) + (0,) * rank

        def out_index(i, spot):
            i = jnp.minimum(i, used - 1)
            return (i // cb, i % cb) + (0,) * rank

        ins = [pl.BlockSpec(shape, functools.partial(index, other=o)) for o in (True, True, False, False)]
        out = pl.BlockSpec((shape[0], shape[2], *self.tail), out_index)
        return ins, [keep, recv, keep, recv], [out, out], [full, full]

    def take(self, send, keep):
        self.keep = keep
        self.recv = flip(send, self.bit, self.count)

    def result(self):
        return self.keep.reshape(self.tail).astype(f32) + self.recv.reshape(self.tail).astype(f32)


def add_step(spot, sums, after=()):
    for one in sums:
        assert one.order
    views = [one.advance() for one in sums]

    def body(spot_ref, *refs):
        ins, outs = refs[: 2 * len(sums)], refs[2 * len(sums) + len(after) :]
        for n, one in enumerate(sums):
            keep, recv = ins[2 * n : 2 * n + 2]
            own = spot_ref[2 + one.bit]
            for half, ref in ((1 - own, outs[2 * n]), (own, outs[2 * n + 1])):
                ref[...] = (keep[:, half].astype(f32) + recv[:, half].astype(f32)).astype(bf16)

    vmem = pl.BlockSpec(memory_space=pltpu.VMEM)
    out = pl.pallas_call(
        body,
        in_specs=[pl.BlockSpec(memory_space=pltpu.SMEM)]
        + [vmem] * (2 * len(sums))
        + [pl.BlockSpec(memory_space=pl.ANY)] * len(after),
        out_specs=[vmem] * (2 * len(sums)),
        out_shape=[v[2] for v in views for _ in range(2)],
        compiler_params=pltpu.CompilerParams(vmem_limit_bytes=8 * MIB),
        cost_estimate=pl.CostEstimate(flops=int(1e5), bytes_accessed=int(1e5), transcendentals=0),
    )(spot, *[x for v in views for x in v[:2]], *after)
    for n, one in enumerate(sums):
        one.take(*out[2 * n : 2 * n + 2])
    return out[-1]


def block(shape, index):
    return pl.BlockSpec(shape, lambda i, spot: index(i))


def whole(shape):
    return pl.BlockSpec(shape, lambda i, spot: (0,) * len(shape), pipeline_mode=pl.Buffered(1))


SMEM = pl.BlockSpec(memory_space=pltpu.SMEM)


def call(kernel, grid, in_specs, outs, out_specs, scratch, spot, args, micros, rides=(), after=(), thread=(), vmem=VMEM):
    nin, nout, nafter, nthread = len(in_specs), len(outs), len(after), len(thread)
    in_specs, out_specs = list(in_specs), list(out_specs)
    out_shape = [jax.ShapeDtypeStruct(s, d) for s, d in outs]
    args = list(args)
    counts = []
    for ride in rides:
        i_specs, i_args, o_specs, o_shape = ride.specs(grid)
        in_specs += i_specs
        args += i_args
        out_specs += o_specs
        out_shape += o_shape
        counts.append(len(o_specs))
    nride = sum(counts)
    hbm = pl.BlockSpec(memory_space=pl.ANY)
    in_specs += [hbm] * (nafter + nthread)
    out_specs += [hbm] * nthread
    out_shape += [jax.ShapeDtypeStruct(t.shape, t.dtype) for t in thread]
    first_thread = 1 + nin + 2 * nride + nafter
    args += list(after) + list(thread)

    def body(spot_ref, *refs):
        ins = refs[:nin]
        ride_ins = refs[nin : nin + 2 * nride]
        rest = refs[nin + 2 * nride + nafter + nthread :]
        host_outs = rest[:nout]
        ride_outs = rest[nout : nout + nride]
        held = rest[nout + nride + nthread :]
        for n in range(nride):
            a, b = ride_ins[2 * n : 2 * n + 2]
            ride_outs[n][...] = (a[...].astype(f32) + b[...].astype(f32)).astype(bf16)
        kernel(spot_ref, *ins, *host_outs, *held)

    out = pl.pallas_call(
        body,
        grid_spec=pltpu.PrefetchScalarGridSpec(
            num_scalar_prefetch=1,
            grid=(grid,),
            in_specs=in_specs,
            out_specs=out_specs,
            scratch_shapes=scratch,
        ),
        out_shape=out_shape,
        input_output_aliases={first_thread + n: nout + nride + n for n in range(nthread)},
        compiler_params=pltpu.CompilerParams(
            dimension_semantics=("arbitrary",), vmem_limit_bytes=vmem * MIB
        ),
        cost_estimate=pl.CostEstimate(flops=int(COST * 1e9 * micros), bytes_accessed=int(1e4), transcendentals=0),
    )(spot, *args)
    at = nout
    for ride, n in zip(rides, counts):
        ride.take(*out[at : at + n])
        at += n
    return out[:nout] + out[at:]


def per_device(
    tokens, out_grad, doc_lengths, w_query, b_query, w_key, b_key, w_value, b_value, w_output, b_output,
    w_inner, b_inner, w_outer, b_outer, gain_first, shift_first, gain_second, shift_second,
):
    rows, width = tokens.shape
    ff = w_inner.shape[1]
    count = lax.axis_size("wide") * lax.axis_size("narrow")
    place = lax.axis_index("wide") * lax.axis_size("narrow") + lax.axis_index("narrow")
    place = place.astype(jnp.int32)
    nchunk = rows // CHUNK
    npair = width // LANES
    heads = 2 * npair
    feat = heads * LANES
    nbits = count.bit_length() - 1
    half = count // 2
    parts = ff // width
    spot = jnp.stack([place * rows, place] + [(place >> b) & 1 for b in range(nbits)])
    at = lambda i: (i, 0)
    tile = block((CHUNK, width), at)
    ftile = block((CHUNK, feat), at)
    col = block((CHUNK, LANES), at)
    square = whole((width, width))
    nvec = R_B1 + parts
    vspec = whole((nvec, width))
    packed = (npair + 1, LANES, LANES)
    pspec = whole(packed)
    fspec = whole((8, LANES))
    fixed = lambda shape: pl.BlockSpec(shape, lambda i, spot: (0,) * len(shape))
    up = list(range(1, nbits))
    swapped = up[:2][::-1] + up[2:]

    lines = (b_query, b_key, b_value, b_output, gain_first, shift_first, b_outer, gain_second, shift_second)
    k, v, kf, cs, st, en, total, near, flags, vecs = call(
        functools.partial(key_kernel, rows=rows),
        nchunk,
        [SMEM, tile, square, square] + [whole((width,))] * 9 + [whole((ff,))],
        [
            ((rows, width), bf16), ((rows, width), bf16), ((rows, feat), bf16),
            ((rows, LANES), f32), ((rows, LANES), jnp.int32), ((rows, LANES), jnp.int32), (packed, bf16), (packed, bf16),
            ((8, LANES), f32), ((nvec, width), f32),
        ],
        [tile, tile, ftile, col, col, col, fixed(packed), fixed(packed), fixed((8, LANES)), fixed((nvec, width))],
        [pltpu.VMEM(packed, f32)],
        spot,
        (doc_lengths, tokens, w_key, w_value, *lines, b_inner),
        12,
    )

    def run_query(sent):
        return call(
            query_kernel,
            nchunk,
            [tile, square, vspec, col],
            [((rows, width), bf16), ((rows, feat), bf16)],
            [tile, ftile],
            [],
            spot,
            (tokens, w_query, vecs, cs),
            4,
            after=(sent,),
            vmem=FILL,
        )

    groups = 3
    gh = heads // groups
    locals_, kepts = [], []

    def run_mixer(sent):
        n = len(kepts)
        fcol = block((CHUNK, gh * LANES), lambda i: (i, n))
        vcol = block((CHUNK, gh * DH), lambda i: (i, n))
        o, kept = call(
            mixer_kernel,
            nchunk,
            [fcol, fcol, vcol, col, col],
            [((rows, gh * LANES), f32), ((nchunk, gh, LANES, LANES), bf16)],
            [block((CHUNK, gh * LANES), at), block((1, gh, LANES, LANES), lambda i: (i, 0, 0, 0))],
            [pltpu.VMEM((gh, LANES, LANES), f32)],
            spot,
            (qf, kf, v, st, en),
            4,
            after=(sent,),
            vmem=FILL,
        )
        locals_.append(o)
        kepts.append(kept)
        return (o,)

    def joined(a, b, after=()):
        a, b, *after = lax.optimization_barrier((a, b, *after))
        return (a.astype(f32) + b.astype(f32)).astype(bf16)

    before = []
    done = ()
    for bit in range(nbits):
        before.append(flip(total, bit, count))
        if bit == 1:
            q, qf = run_query(total)
            done = (q,)
            from_last = lax.ppermute(near, AXES, [(i, i + 1) for i in range(count - 1)])
        elif bit >= 2 and len(kepts) < groups:
            done = run_mixer(total)
        if bit < nbits - 1:
            total = joined(total, before[-1], done)
    while len(kepts) < groups:
        run_mixer(total)
    before.append(from_last)

    ftile_ff = block((CHUNK, ff), at)
    otile = block((CHUNK, gh * LANES), at)
    (result, mixed, first, act, d_outer, d_inner, d_branch, d_r1, dn, back, near, vgrad, state_in) = call(
        functools.partial(token_kernel, split=12, scans=nbits + 1),
        nchunk,
        [
            otile, otile, otile, ftile, col, tile, tile,
            square, whole((width, ff)), whole((ff, width)), vspec, fspec,
        ] + [pspec] * (nbits + 1),
        [
            ((rows, width), bf16), ((rows, width), bf16), ((rows, width), bf16), ((rows, ff), bf16),
            ((rows, width), bf16), ((rows, ff), bf16), ((rows, width), bf16), ((rows, width), f32),
            ((rows, feat), bf16), (packed, bf16), (packed, bf16), ((VEC_ROWS, width), f32), (packed, bf16),
        ],
        [
            tile, tile, tile, ftile_ff, tile, ftile_ff, tile, tile, ftile,
            fixed(packed), fixed(packed), fixed((VEC_ROWS, width)), fixed(packed),
        ],
        [
            pltpu.VMEM((heads, LANES, LANES), bf16),
            pltpu.VMEM((CHUNK, width), f32),
            pltpu.VMEM((CHUNK, width), f32),
            pltpu.VMEM((CHUNK, ff), f32),
            pltpu.VMEM(packed, f32),
            pltpu.VMEM((CHUNK, width), f32),
            pltpu.VMEM((CHUNK, width), f32),
            pltpu.VMEM((CHUNK, LANES), f32),
            pltpu.VMEM((8 * (V_B1 + parts), width), f32),
        ],
        spot,
        (*locals_, qf, st, tokens, out_grad, w_output, w_inner, w_outer, vecs, flags, *before),
        50,
    )

    piece_o = ff // count
    piece = width // count
    per_step = width // piece_o
    sums = {}

    def run_outer(after):
        spec = block((per_step // 2, piece_o, width), lambda i: (i, 0, 0))
        send, keep = call(
            functools.partial(outer_grad_kernel, piece=piece_o),
            parts,
            [block((rows, width), lambda i: (0, i)), whole((rows, width))],
            [((half, piece_o, width), bf16)] * 2,
            [spec, spec],
            [],
            spot,
            (act, d_outer),
            9,
            after=after,
            vmem=FILL,
        )
        sums["outer"] = Halving(send, keep, count, up)
        return (keep,)

    def run_inner(after, lead, order, rides=()):
        n = parts // 2
        full = fixed((half, n * piece, width))
        send, keep = call(
            functools.partial(inner_grad_kernel, piece=piece, parts=n),
            n,
            [whole((rows, width)), block((rows, width), lambda i: (0, lead * n + i))],
            [((half, n * piece, width), bf16)] * 2,
            [full, full],
            [],
            spot,
            (first, d_inner),
            5,
            rides=rides,
            after=after,
            vmem=FILL,
        )
        sums[f"inner{lead}"] = Halving(send, keep, count, order)
        return (keep,)

    def run_query_back(after, rides=()):
        last = lambda i: jnp.minimum(i, nchunk - 1)
        ltile = block((CHUNK, width), lambda i: (last(i), 0))
        lf = block((CHUNK, feat), lambda i: (last(i), 0))
        lcol = block((CHUNK, LANES), lambda i: (last(i), 0))
        kept = block((1, gh, LANES, LANES), lambda i: (last(i), 0, 0, 0))
        depth = 2 * piece + VEC_ROWS
        full = fixed((half, depth, width))
        wide = whole((rows, width))
        dq, send, keep = call(
            functools.partial(query_back_kernel, npair=npair, nchunk=nchunk, piece=piece),
            nchunk + 1,
            [lf, lf, ltile, lf, ltile, kept, kept, kept, pspec, lcol, lcol, wide, wide, wide, whole((VEC_ROWS, width))],
            [((rows, width), bf16)] + [((half, depth, width), bf16)] * 2,
            [ltile, full, full],
            [pltpu.VMEM((rows, width), bf16), pltpu.VMEM((8, width), f32)],
            spot,
            (qf, kf, v, dn, q, *kepts, state_in, st, cs, tokens, mixed, d_branch, vgrad),
            15,
            rides=rides,
            after=after,
            vmem=FILL,
        )
        sums["query"] = Halving(send, keep, count, up)
        return dq

    after_ = []
    done = ()
    for bit in range(nbits):
        after_.append(flip(back, bit, count))
        sent = (back, *done)
        if bit == 2:
            from_next = lax.ppermute(near, AXES, [(i + 1, i) for i in range(count - 1)])
        if bit == 1:
            done = run_outer(sent)
        elif bit == 2:
            done = run_inner(sent, 0, swapped)
        elif bit == 3:
            done = (add_step(spot, [sums["outer"]], sent),)
            done = run_inner((*sent, *done), 1, up)
        elif bit == 4:
            done = (add_step(spot, [sums["inner0"]], sent),)
            dq = run_query_back((*sent, *done))
            done = (dq,)
        if bit < nbits - 1:
            back = joined(back, after_[-1], done)
    after_.append(from_next)
    (back_in,) = call(
        functools.partial(taken_kernel, lane=F_AFTER),
        1,
        [pspec] * (nbits + 1) + [fspec],
        [(packed, bf16)],
        [fixed(packed)],
        [],
        spot,
        (*after_, flags),
        1,
        after=done,
        vmem=4,
    )

    halves = 2
    hp = npair // halves
    hw = hp * LANES
    dks, dvs = [], []

    def run_value_back(n, order, rides=(), after=()):
        index = lambda i: nchunk - 1 - jnp.minimum(i, nchunk - 1)
        fcol = block((CHUNK, 2 * hw), lambda i: (index(i), n))
        vcol = block((CHUNK, hw), lambda i: (index(i), n))
        bcol = block((CHUNK, LANES), lambda i: (index(i), 0))
        grad = block((CHUNK, hw), lambda i: (index(i), 0))
        full = fixed((half, piece + 8, 2 * hw))
        dk, dv, send, keep = call(
            functools.partial(
                value_back_kernel, pair0=n * hp, npair=npair, nchunk=nchunk, piece=piece, rows=rows
            ),
            nchunk + 1,
            [fcol, fcol, vcol, fcol, vcol, pspec, bcol, bcol, bcol, whole((rows, width))],
            [((rows, hw), bf16)] * 2 + [((half, piece + 8, 2 * hw), bf16)] * 2,
            [grad, grad, full, full],
            [
                pltpu.VMEM((2 * hp, LANES, LANES), f32),
                pltpu.VMEM((rows, 2 * hw), bf16),
                pltpu.VMEM((8, 2 * hw), f32),
            ],
            spot,
            (qf, kf, v, dn, k, back_in, st, en, cs, tokens),
            10,
            rides=rides,
            after=after,
            vmem=FILL,
        )
        dks.append(dk)
        dvs.append(dv)
        sums[f"value{n}"] = Halving(send, keep, count, order)

    done = (add_step(spot, [sums["inner1"]], (back_in,)),)
    run_value_back(0, swapped, after=done)
    done = (add_step(spot, [sums["query"], sums["outer"]], (dks[0],)),)
    run_value_back(1, up, after=done)
    done = (add_step(spot, [sums["value0"], sums["inner0"], sums["inner1"]], (dks[1],)),)
    done = (add_step(spot, [sums["value1"]], done),)

    (grad_tokens,) = call(
        tokens_grad_kernel,
        nchunk,
        [tile, tile] + [block((CHUNK, hw), at)] * 4 + [square] * 3,
        [((rows, width), bf16)],
        [tile],
        [],
        spot,
        (d_r1, dq, *dks, *dvs, w_query, w_key, w_value),
        8,
        after=done,
        vmem=FILL,
    )
    done = (grad_tokens,)
    while True:
        left = [s for s in sums.values() if s.order]
        if not left:
            break
        done = (add_step(spot, left, done),)

    g_outer = sums["outer"].result()
    inner0, inner1 = sums["inner0"].result(), sums["inner1"].result()
    cuts = [inner0[i * piece : (i + 1) * piece] for i in range(parts // 2)]
    cuts += [inner1[i * piece : (i + 1) * piece] for i in range(parts // 2)]
    g_inner = jnp.concatenate(cuts, axis=1)
    query = sums["query"].result()
    g_query, g_output, vec = query[:piece], query[piece : 2 * piece], query[2 * piece :]
    kv = [sums[f"value{n}"].result() for n in range(halves)]
    g_kv = [jnp.concatenate([s[:piece, m * hw : (m + 1) * hw] for s in kv], axis=1) for m in range(2)]
    b_kv = [jnp.concatenate([s[piece, m * hw : (m + 1) * hw] for s in kv]) for m in range(2)]

    def share(line):
        size = line.shape[0] // count
        return lax.dynamic_slice(line, (place * size,), (size,))

    return (
        result,
        grad_tokens,
        g_query,
        share(vec[VEC_ROWS - 1]),
        g_kv[0],
        share(b_kv[0]),
        g_kv[1],
        share(b_kv[1]),
        g_output,
        share(vec[V_BO]),
        g_inner,
        share(vec[V_B1 : V_B1 + parts].reshape(-1)),
        g_outer,
        share(vec[V_B2]),
        share(vec[V_G1]),
        share(vec[V_E1]),
        share(vec[V_G2]),
        share(vec[V_E2]),
    )


def solution(mesh):
    split = P(AXES, None)
    line = P(AXES)
    return jax.shard_map(
        per_device,
        mesh=mesh,
        in_specs=(split, split) + (P(),) * 17,
        out_specs=(split, split) + (split, line) * 6 + (line,) * 4,
        check_vma=False,
    )
```

```python
import functools
import math

import jax
import jax.numpy as jnp
from jax import lax
from jax.experimental import pallas as pl
from jax.experimental.pallas import tpu as pltpu
from jax.sharding import PartitionSpec as P

DH = 64
LANES = 128
CHUNK = 256
SLICE = 16
EPS = 1e-05
HALF_PI = math.pi / 2.0
MIB = 1 << 20
VMEM = 60
COST = 0.01
FILL = 20
AXES = ("wide", "narrow")

f32 = jnp.float32
bf16 = jnp.bfloat16

R_BQ, R_BK, R_BV, R_BO, R_G1, R_E1, R_B2, R_G2, R_E2, R_B1 = range(10)
V_B2, V_G2, V_E2, V_G1, V_E1, V_BO, V_B1 = range(7)
VEC_ROWS = 16


def nn(a, b):
    return jnp.dot(a, b, preferred_element_type=f32)


def nt(a, b):
    return lax.dot_general(a, b, (((1,), (1,)), ((), ())), preferred_element_type=f32)


def tn(a, b):
    return lax.dot_general(a, b, (((0,), (0,)), ((), ())), preferred_element_type=f32)


def lane_iota(rows, lanes=LANES):
    return lax.broadcasted_iota(jnp.int32, (rows, lanes), 1)


def row_iota(rows, lanes=LANES):
    return lax.broadcasted_iota(jnp.int32, (rows, lanes), 0)


def swap_halves(x):
    return pltpu.roll(x, DH, 1)


def softplus(x):
    return jnp.maximum(x, 0.0) + jnp.log1p(jnp.exp(-jnp.abs(x)))


def sigmoid(x):
    return 1.0 / (1.0 + jnp.exp(-x))


def sine(b):
    s = b * b
    p = 1.0 / 6227020800.0
    for c in (-1.0 / 39916800.0, 1.0 / 362880.0, -1.0 / 5040.0, 1.0 / 120.0, -1.0 / 6.0):
        p = p * s + c
    return b + b * s * p


def features(pair, cs, lo):
    soft = softplus(pair)
    other = swap_halves(soft)
    return (
        (jnp.where(lo, soft, other) * cs).astype(bf16),
        (jnp.where(lo, other, soft) * cs).astype(bf16),
    )


def extended(v, lo):
    one = jnp.ones_like(v)
    return jnp.where(lo, v, one), jnp.where(lo, one, v)


def pairs_of(width):
    return width // LANES


def lookup(len_ref, pos):
    start = jnp.zeros(pos.shape, jnp.int32)
    end = jnp.zeros(pos.shape, jnp.int32)
    edge = jnp.int32(0)
    for doc in range(len_ref.shape[0]):
        here = pos >= edge
        after = edge + len_ref[doc]
        start = jnp.where(here, edge, start)
        end = jnp.where(here, after, end)
        edge = after
    return start, end


F_BEFORE, F_NEXT_B, F_AFTER, F_NEXT_A, F_CLOSING, F_OPENING = range(6)


def flag_table(len_ref, place, rows):
    bit, lane = row_iota(8), lane_iota(8)
    upper = jnp.bitwise_and(jnp.right_shift(jnp.full_like(bit, place), bit), 1) == 1
    base, close = place * rows, (place + 1) * rows
    is_before = (lane == F_BEFORE) | (lane == F_NEXT_B)
    is_after = (lane == F_AFTER) | (lane == F_NEXT_A)
    pos = jnp.where(
        is_before,
        base - 1,
        jnp.where(is_after, close, jnp.where(lane == F_CLOSING, close - 1, base)),
    )
    start, end = lookup(len_ref, pos)
    one, zero = jnp.ones(bit.shape, f32), jnp.zeros(bit.shape, f32)
    is_long = jnp.where((end - start) > rows, one, zero)
    near = jnp.where((pos >= 0) & (pos < end), 1.0 - is_long, zero)
    out = is_long
    out = jnp.where(lane == F_BEFORE, jnp.where(upper, is_long, zero), out)
    out = jnp.where(lane == F_AFTER, jnp.where(upper, zero, is_long), out)
    return jnp.where((lane == F_NEXT_B) | (lane == F_NEXT_A), near, out)


def key_kernel(
    spot_ref, len_ref, x_ref, wk_ref, wv_ref,
    bq, bk, bv, bo, g1, e1, b2, g2, e2, b1,
    k_ref, v_ref, kf_ref, cs_ref, st_ref, en_ref, state_ref, next_ref, flag_ref, vec_ref,
    total,
    *, rows,
):
    step = pl.program_id(0)
    base = spot_ref[0]
    width = x_ref.shape[1]
    first = base + step * CHUNK
    pos = first + row_iota(CHUNK)
    lane = lane_iota(CHUNK)
    lo = lane < DH

    @pl.when(step == 0)
    def _():
        total[...] = jnp.zeros_like(total)
        flag_ref[...] = flag_table(len_ref, spot_ref[1], rows)
        for r, ref in enumerate((bq, bk, bv, bo, g1, e1, b2, g2, e2)):
            vec_ref[r : r + 1, :] = ref[...].astype(f32).reshape(1, width)
        for r in range(b1.shape[0] // width):
            vec_ref[R_B1 + r : R_B1 + r + 1, :] = (
                b1[r * width : (r + 1) * width].astype(f32).reshape(1, width)
            )

    start, end = lookup(len_ref, pos)
    part = jnp.where(lo, end - pos, pos - start).astype(f32)
    cs = sine(HALF_PI * part / (end - start).astype(f32))
    cs_ref[...] = cs
    st_ref[...] = start
    en_ref[...] = end

    x = x_ref[...]
    k = (nn(x, wk_ref[...]) + vec_ref[R_BK : R_BK + 1, :]).astype(bf16)
    v = (nn(x, wv_ref[...]) + vec_ref[R_BV : R_BV + 1, :]).astype(bf16)
    k_ref[...] = k
    v_ref[...] = v
    closing = end >= base + rows
    slots = lane_iota(LANES)
    lo_state = slots < DH

    npair = pairs_of(width)
    zcol = jnp.zeros((LANES, LANES), f32)
    for g in range(npair):
        cols = slice(g * LANES, (g + 1) * LANES)
        fa, fb = features(k[:, cols].astype(f32), cs, lo)
        kf_ref[:, 2 * g * LANES : (2 * g + 1) * LANES] = fa
        kf_ref[:, (2 * g + 1) * LANES : (2 * g + 2) * LANES] = fb
        va, vb = extended(v[:, cols], lo)
        zero = jnp.zeros_like(fa)
        sa = tn(jnp.where(closing, fa, zero), va)
        sb = tn(jnp.where(closing, fb, zero), vb)
        total[g] += jnp.where(lo_state, sa, sb)
        zcol = jnp.where(slots == DH + g, sa, jnp.where(slots == g, sb, zcol))
    total[npair] += zcol

    @pl.when(step == pl.num_programs(0) - 1)
    def _():
        split_long(total[...], flag_ref[0:1, F_CLOSING : F_CLOSING + 1], state_ref, next_ref)


def split_long(total, flag, long_ref, next_ref):
    long_ref[...] = (total * flag).astype(bf16)
    next_ref[...] = (total * (1.0 - flag)).astype(bf16)


def taken_sum(refs, flags, lane):
    *scans, near = refs
    total = near[...].astype(f32) * flags[0:1, lane + 1 : lane + 2]
    for bit, ref in enumerate(scans):
        total = total + ref[...].astype(f32) * flags[bit : bit + 1, lane : lane + 1]
    return total.astype(bf16)


def unpack_state(state_ref, g, npair, lo, slots):
    pair = state_ref[g].astype(f32)
    z = state_ref[npair].astype(f32)
    za = z[:, DH + g : DH + g + 1]
    zb = z[:, g : g + 1]
    return jnp.where(lo, pair, za), jnp.where(lo, zb, pair)


def unpack_grad_state(state_ref, g, npair, lo, slots):
    pair = state_ref[g].astype(f32)
    z = state_ref[npair].astype(f32)
    za = jnp.where(slots == DH, z[:, DH + g : DH + g + 1], 0.0)
    zb = jnp.where(slots == 0, z[:, g : g + 1], 0.0)
    return jnp.where(lo, pair, za), jnp.where(lo, zb, pair)


def query_kernel(spot_ref, x_ref, wq_ref, vec_ref, cs_ref, q_ref, qf_ref):
    q = (nn(x_ref[...], wq_ref[...]) + vec_ref[R_BQ : R_BQ + 1, :]).astype(bf16)
    q_ref[...] = q
    lo = lane_iota(CHUNK) < DH
    cs = cs_ref[...]
    for g in range(pairs_of(q.shape[1])):
        fa, fb = features(q[:, g * LANES : (g + 1) * LANES].astype(f32), cs, lo)
        qf_ref[:, 2 * g * LANES : (2 * g + 1) * LANES] = fa
        qf_ref[:, (2 * g + 1) * LANES : (2 * g + 2) * LANES] = fb


def mixer_kernel(spot_ref, qf_ref, kf_ref, v_ref, st_ref, en_ref, o_ref, kept_ref, local):
    step = pl.program_id(0)
    first = spot_ref[0] + step * CHUNK
    start, end = st_ref[...], en_ref[...]
    start2 = jnp.concatenate([start, start], axis=1)
    ipos = first + row_iota(CHUNK, CHUNK)
    jpos = first + lane_iota(CHUNK, CHUNK)
    mask = (jpos <= ipos) & (jpos >= start2)
    carried = start < first
    closing = end >= first + CHUNK
    keep = start[CHUNK - 1 : CHUNK, :] < first
    lo = lane_iota(CHUNK) < DH

    @pl.when(step == 0)
    def _():
        local[...] = jnp.zeros_like(local)

    for g in range(pairs_of(v_ref.shape[1])):
        vs = extended(v_ref[:, g * LANES : (g + 1) * LANES], lo)
        for s in range(2):
            h = 2 * g + s
            cols = slice(h * LANES, (h + 1) * LANES)
            qf, kf, v = qf_ref[:, cols], kf_ref[:, cols], vs[s]
            probs = jnp.where(mask, nt(qf, kf), 0.0).astype(bf16)
            held = local[h].astype(bf16)
            kept_ref[0, h] = held
            o_ref[:, cols] = nn(probs, v) + jnp.where(carried, nn(qf, held), 0.0)
            local[h] = jnp.where(keep, local[h], 0.0) + tn(
                jnp.where(closing, kf, jnp.zeros_like(kf)), v
            )


def gelu_and_slope(u):
    z = jnp.abs(u) * (1.0 / math.sqrt(2.0))
    t = 1.0 / (1.0 + 0.3275911 * z)
    p = 0.5 * 1.061405429
    for c in (-1.453152027, 1.421413741, -0.284496736, 0.254829592):
        p = p * t + 0.5 * c
    e = jnp.exp(-0.5 * u * u)
    tail = p * t * e
    gauss = jnp.where(u >= 0.0, 1.0 - tail, tail)
    return u * gauss, gauss + u * e * (1.0 / math.sqrt(2.0 * math.pi))


def token_kernel(
    spot_ref, o0_ref, o1_ref, o2_ref, qf_ref, st_ref, x_ref, go_ref,
    wo_ref, w1_ref, w2_ref, vec_ref, flag_ref, *refs, split, scans,
):
    theirs = refs[:scans]
    (
        out_ref, mixed_ref, first_ref, act_ref, douter_ref, dinner_ref, dbranch_ref, dr1_ref,
        dn_ref, back_ref, near_ref, vgrad_ref, state_ref,
        states, ratio, rden_s, slope, back_s, flow, norm_s, rstd_s, sums,
    ) = refs[scans:]
    step = pl.program_id(0)
    base = spot_ref[0]
    chunk, width = x_ref.shape
    ff = w1_ref.shape[1]
    npair = pairs_of(width)
    lane = lane_iota(chunk)
    lo = lane < DH
    slots = lane_iota(LANES)
    lo_state = slots < DH
    start = st_ref[...]

    @pl.when(step == 0)
    def _():
        state_ref[...] = taken_sum(theirs, flag_ref[...], F_BEFORE)
        for g in range(npair):
            a, b = unpack_state(state_ref, g, npair, lo_state, slots)
            states[2 * g] = a.astype(bf16)
            states[2 * g + 1] = b.astype(bf16)
        back_s[...] = jnp.zeros_like(back_s)
        sums[...] = jnp.zeros_like(sums)

    carried = start < base
    o_refs = (o0_ref, o1_ref, o2_ref)
    for g in range(npair):
        both = []
        for s in range(2):
            h = 2 * g + s
            o_of = o_refs[h // 4]
            local = o_of[:, (h % 4) * LANES : (h % 4 + 1) * LANES]
            far = nn(qf_ref[:, h * LANES : (h + 1) * LANES], states[h])
            both.append(local + jnp.where(carried, far, 0.0))
        numer = jnp.where(lo, both[0], both[1])
        rden = 1.0 / swap_halves(jnp.where(lo, both[1], both[0]))
        cols = slice(g * LANES, (g + 1) * LANES)
        rden_s[:, cols] = rden
        mix = numer * rden
        ratio[:, cols] = mix
        mixed_ref[:, cols] = mix.astype(bf16)

    def row(r):
        return vec_ref[r : r + 1, :]

    def mean(v):
        return jnp.sum(v, axis=-1, keepdims=True) * (1.0 / width)

    def norm(resid):
        cent = resid - mean(resid)
        rstd = lax.rsqrt(mean(cent * cent) + EPS)
        return cent * rstd, rstd

    def norm_back(grad, normed, rstd, gain):
        d_n = grad * gain
        return rstd * (d_n - mean(d_n) - normed * mean(d_n * normed))

    def add_sum(r, v, cols=slice(None)):
        sums[8 * r : 8 * r + 8, cols] += v

    flow[...] = nn(mixed_ref[...], wo_ref[...])
    for at in range(0, chunk, SLICE):
        sl = slice(at, at + SLICE)
        n1, rstd1 = norm(x_ref[sl, :].astype(f32) + flow[sl, :] + row(R_BO))
        norm_s[sl, :] = n1
        rstd_s[sl, :] = jnp.broadcast_to(rstd1, (SLICE, LANES))
        first_ref[sl, :] = (n1 * row(R_G1) + row(R_E1)).astype(bf16)

    part = ff // split

    def inner_of(i):
        flat, off = i * part // width, i * part % width
        bias = vec_ref[R_B1 + flat : R_B1 + flat + 1, off : off + part]
        return nn(first_ref[...], w1_ref[:, i * part : (i + 1) * part]) + bias

    ahead = inner_of(0)
    outer = jnp.zeros((chunk, width), f32)
    last = None
    for i in range(split):
        cols = slice(i * part, (i + 1) * part)
        now = ahead
        if i + 1 < split:
            ahead = inner_of(i + 1)
        if last is not None:
            outer = outer + nn(last, w2_ref[(i - 1) * part : i * part, :])
        act, sl = gelu_and_slope(now)
        last = act.astype(bf16)
        act_ref[:, cols] = last
        slope[:, cols] = sl
    flow[...] = outer + nn(last, w2_ref[(split - 1) * part :, :])

    g2_sum = e2_sum = b2_sum = jnp.zeros((8, width), f32)
    for at in range(0, chunk, SLICE):
        sl = slice(at, at + SLICE)
        n2, rstd2 = norm(first_ref[sl, :].astype(f32) + flow[sl, :] + row(R_B2))
        out_ref[sl, :] = (n2 * row(R_G2) + row(R_E2)).astype(bf16)
        grad = go_ref[sl, :].astype(f32)
        g2_sum = g2_sum + fold_rows(grad * n2)
        e2_sum = e2_sum + fold_rows(grad)
        d_r2 = norm_back(grad, n2, rstd2, row(R_G2))
        b2_sum = b2_sum + fold_rows(d_r2)
        douter_ref[sl, :] = d_r2.astype(bf16)
        dr1_ref[sl, :] = d_r2
    add_sum(V_G2, g2_sum)
    add_sum(V_E2, e2_sum)
    add_sum(V_B2, b2_sum)

    for i in range(split):
        cols = slice(i * part, (i + 1) * part)
        flat = i * part // width
        off = i * part % width
        d_inner = nt(douter_ref[...], w2_ref[cols, :]) * slope[:, cols]
        dinner_ref[:, cols] = d_inner.astype(bf16)
        add_sum(V_B1 + flat, fold_rows(d_inner), slice(off, off + part))
    flow[...] = nt(dinner_ref[...], w1_ref[...])

    g1_sum = e1_sum = bo_sum = jnp.zeros((8, width), f32)
    for at in range(0, chunk, SLICE):
        sl = slice(at, at + SLICE)
        d_first = dr1_ref[sl, :] + flow[sl, :]
        n1 = norm_s[sl, :]
        g1_sum = g1_sum + fold_rows(d_first * n1)
        e1_sum = e1_sum + fold_rows(d_first)
        d_r1 = norm_back(d_first, n1, rstd_s[sl, 0:1], row(R_G1))
        bo_sum = bo_sum + fold_rows(d_r1)
        dr1_ref[sl, :] = d_r1
        dbranch_ref[sl, :] = d_r1.astype(bf16)
    add_sum(V_G1, g1_sum)
    add_sum(V_E1, e1_sum)
    add_sum(V_BO, bo_sum)

    flow[...] = nt(dbranch_ref[...], wo_ref[...])
    opening = start <= base
    zcol = jnp.zeros((LANES, LANES), f32)
    for g in range(npair):
        cols = slice(g * LANES, (g + 1) * LANES)
        dn = flow[:, cols] * rden_s[:, cols]
        prod = dn * ratio[:, cols]
        dda = -jnp.sum(jnp.where(lo, prod, 0.0), axis=1, keepdims=True)
        ddb = -jnp.sum(jnp.where(lo, 0.0, prod), axis=1, keepdims=True)
        hia, hib = dda.astype(bf16).astype(f32), ddb.astype(bf16).astype(f32)
        exa = jnp.where(lane == DH, hia, jnp.where(lane == DH + 1, dda - hia, 0.0))
        exb = jnp.where(lane == 0, hib, jnp.where(lane == 1, ddb - hib, 0.0))
        dna = jnp.where(lo, dn, exa).astype(bf16)
        dnb = jnp.where(lo, exb, dn).astype(bf16)
        ca = slice(2 * g * LANES, (2 * g + 1) * LANES)
        cb = slice((2 * g + 1) * LANES, (2 * g + 2) * LANES)
        dn_ref[:, ca] = dna
        dn_ref[:, cb] = dnb
        zero = jnp.zeros((chunk, LANES), bf16)
        ga = tn(jnp.where(opening, qf_ref[:, ca], zero), dna)
        gb = tn(jnp.where(opening, qf_ref[:, cb], zero), dnb)
        back_s[g] += jnp.where(lo_state, ga, gb)
        za = ga[:, DH : DH + 1] + ga[:, DH + 1 : DH + 2]
        zb = gb[:, 0:1] + gb[:, 1:2]
        zcol = jnp.where(slots == DH + g, za, jnp.where(slots == g, zb, zcol))
    back_s[npair] += zcol

    @pl.when(step == pl.num_programs(0) - 1)
    def _():
        split_long(back_s[...], flag_ref[0:1, F_OPENING : F_OPENING + 1], back_ref, near_ref)
        vgrad_ref[...] = jnp.zeros_like(vgrad_ref)
        for r in range(sums.shape[0] // 8):
            vgrad_ref[r : r + 1, :] = jnp.sum(sums[8 * r : 8 * r + 8, :], axis=0, keepdims=True)


def fold_rows(v):
    return jnp.sum(v.reshape(v.shape[0] // 8, 8, v.shape[1]), axis=0)


def store_pieces(own, value, rows, send_ref, keep_ref, at):
    count = value.shape[0] // rows
    value = value.astype(bf16)
    for bit in range(2):

        @pl.when(own == bit)
        def _():
            for d in range(count):
                ref = keep_ref if d % 2 == bit else send_ref
                ref[d // 2, at : at + rows, :] = value[d * rows : (d + 1) * rows, :]


def store_lines(line, send_ref, keep_ref, at):
    line = line.astype(bf16)
    for m in range(send_ref.shape[0]):
        send_ref[m, at : at + line.shape[0], :] = line
        keep_ref[m, at : at + line.shape[0], :] = line


def query_back_kernel(
    spot_ref, qf_ref, kf_ref, v_ref, dn_ref, q_ref, kept0, kept1, kept2, state_ref, st_ref, cs_ref, *refs,
    pair0, npair, nchunk, piece, last,
):
    if last:
        x_ref, other_ref, mixed_ref, dbranch_ref, vec_ref, dq_ref, send0, keep0, send1, keep1, grads = refs
    else:
        (dq_ref,) = refs
    step = pl.program_id(0)
    base = spot_ref[0]
    keepers = (kept0, kept1, kept2)
    two = range(2)

    def chunk_step():
        lo = lane_iota(CHUNK) < DH
        slots = lane_iota(LANES)
        lo_state = slots < DH
        first = base + step * CHUNK
        start, cs = st_ref[...], cs_ref[...]
        start2 = jnp.concatenate([start, start], axis=1)
        ipos = first + row_iota(CHUNK, CHUNK)
        jpos = first + lane_iota(CHUNK, CHUNK)
        mask = (jpos <= ipos) & (jpos >= start2)
        carried = start < first
        from_far = start[0:1, :] < base
        at = pl.ds(pl.multiple_of(step * CHUNK, CHUNK), CHUNK)
        for g in range(pairs_of(v_ref.shape[1])):
            pair = slice(g * LANES, (g + 1) * LANES)
            cols = [slice((2 * g + s) * LANES, (2 * g + s + 1) * LANES) for s in two]
            heads = [2 * (pair0 + g) + s for s in two]
            vs = extended(v_ref[:, pair], lo)
            far = unpack_state(state_ref, pair0 + g, npair, lo_state, slots)
            dns = [dn_ref[:, c] for c in cols]
            d_probs = [nt(dns[s], vs[s]) for s in two]
            d_probs = [jnp.where(mask, d, 0.0).astype(bf16) for d in d_probs]
            held = [
                (keepers[heads[s] // 4][0, heads[s] % 4].astype(f32) + jnp.where(from_far, far[s], 0.0)).astype(bf16)
                for s in two
            ]
            d_qf = [
                nn(d_probs[s], kf_ref[:, cols[s]]) + jnp.where(carried, nt(dns[s], held[s]), 0.0) for s in two
            ]
            turned = [d * cs for d in d_qf]
            turned = [t + swap_halves(t) for t in turned]
            value = jnp.where(lo, turned[0], turned[1]) * sigmoid(q_ref[:, pair].astype(f32))
            value = value.astype(bf16)
            dq_ref[:, pair] = value
            if last:
                grads[at, pair] = value

    if not last:
        chunk_step()
        return

    pl.when(step < nchunk)(chunk_step)

    @pl.when(step == nchunk)
    def _():
        own = spot_ref[2]
        whole_q = jnp.concatenate([other_ref[...], grads[...]], axis=1)
        store_pieces(own, tn(x_ref[...], whole_q), piece, send0, keep0, 0)
        store_pieces(own, tn(mixed_ref[...], dbranch_ref[...]), piece, send1, keep1, 0)
        total = jnp.sum(fold_rows(whole_q.astype(f32)), axis=0, keepdims=True)
        vec = jnp.where(row_iota(VEC_ROWS, total.shape[1]) == VEC_ROWS - 1, total, vec_ref[...])
        store_lines(vec[:8], send0, keep0, piece)
        store_lines(vec[8:], send1, keep1, piece)


def value_back_kernel(
    spot_ref, qf_ref, kf_ref, v_ref, dn_ref, k_ref, back_ref, st_ref, en_ref, cs_ref, x_ref,
    dk_ref, dv_ref, send_ref, keep_ref,
    onward_state, grads, lines,
    *, pair0, npair, nchunk, piece, rows,
):
    base = spot_ref[0]
    wide = v_ref.shape[1]

    @pl.when(pl.program_id(0) == 0)
    def _():
        onward_state[...] = jnp.zeros_like(onward_state)
        lines[...] = jnp.zeros_like(lines)

    @pl.when(pl.program_id(0) < nchunk)
    def _():
        lo = lane_iota(CHUNK) < DH
        slots = lane_iota(LANES)
        lo_state = slots < DH
        step = nchunk - 1 - pl.program_id(0)
        first = base + step * CHUNK
        start, end, cs = st_ref[...], en_ref[...], cs_ref[...]
        end2 = jnp.concatenate([end, end], axis=1)
        jpos = first + row_iota(CHUNK, CHUNK)
        ipos = first + lane_iota(CHUNK, CHUNK)
        mask = (jpos <= ipos) & (ipos < end2)
        onward = end > first + CHUNK
        opening = start <= first
        to_far = end[CHUNK - 1 : CHUNK, :] > base + rows
        keep = end[0:1, :] > first + CHUNK
        at = pl.ds(pl.multiple_of(step * CHUNK, CHUNK), CHUNK)
        zero = jnp.zeros((CHUNK, LANES), bf16)
        two = range(2)
        for g in range(pairs_of(wide)):
            pair = slice(g * LANES, (g + 1) * LANES)
            cols = [slice((2 * g + s) * LANES, (2 * g + s + 1) * LANES) for s in two]
            vs = extended(v_ref[:, pair], lo)
            far = unpack_grad_state(back_ref, pair0 + g, npair, lo_state, slots)
            qf, kf = [qf_ref[:, c] for c in cols], [kf_ref[:, c] for c in cols]
            dn = [dn_ref[:, c] for c in cols]
            probs = [nt(kf[s], qf[s]) for s in two]
            d_probs = [nt(vs[s], dn[s]) for s in two]
            probs = [jnp.where(mask, p, 0.0).astype(bf16) for p in probs]
            d_probs = [jnp.where(mask, p, 0.0).astype(bf16) for p in d_probs]
            ahead = [onward_state[2 * g + s] for s in two]
            ahead16 = [(ahead[s] + jnp.where(to_far, far[s], 0.0)).astype(bf16) for s in two]
            more = [tn(jnp.where(opening, qf[s], zero), dn[s]) for s in two]
            d_kf = [nn(d_probs[s], qf[s]) + jnp.where(onward, nt(vs[s], ahead16[s]), 0.0) for s in two]
            d_v = [nn(probs[s], dn[s]) + jnp.where(onward, nn(kf[s], ahead16[s]), 0.0) for s in two]
            for s in two:
                onward_state[2 * g + s] = jnp.where(keep, ahead[s], 0.0) + more[s]
            turned = [d * cs for d in d_kf]
            turned = [t + swap_halves(t) for t in turned]
            both = (
                (jnp.where(lo, turned[0], turned[1]) * sigmoid(k_ref[:, pair].astype(f32)), dk_ref),
                (jnp.where(lo, d_v[0], d_v[1]), dv_ref),
            )
            for n, (value, ref) in enumerate(both):
                spread = slice(n * wide + g * LANES, n * wide + (g + 1) * LANES)
                lines[0:8, spread] += fold_rows(value)
                value = value.astype(bf16)
                ref[:, pair] = value
                grads[at, spread] = value

    @pl.when(pl.program_id(0) == nchunk)
    def _():
        store_pieces(spot_ref[2], tn(x_ref[...], grads[...]), piece, send_ref, keep_ref, 0)
        total = jnp.sum(lines[...], axis=0, keepdims=True)
        store_lines(jnp.broadcast_to(total, lines.shape), send_ref, keep_ref, piece)


def outer_grad_kernel(spot_ref, act_ref, d_ref, send0, keep0, send1, keep1, *, piece):
    value = tn(act_ref[...], d_ref[...]).astype(bf16)
    cut = piece // 2
    for bit in range(2):

        @pl.when(spot_ref[2] == bit)
        def _():
            for d in range(value.shape[0] // piece):
                first, second = (keep0, keep1) if d % 2 == bit else (send0, send1)
                first[d // 2] = value[d * piece : d * piece + cut, :]
                second[d // 2] = value[d * piece + cut : (d + 1) * piece, :]


def inner_grad_kernel(spot_ref, first_ref, dinner_ref, send_ref, keep_ref, *, piece, parts):
    for i in range(parts):

        @pl.when(pl.program_id(0) == i)
        def _():
            value = tn(first_ref[...], dinner_ref[...])
            store_pieces(spot_ref[2], value, piece, send_ref, keep_ref, i * piece)


def tokens_grad_kernel(spot_ref, dr1_ref, q0, q1, k0, k1, v0, v1, wq_ref, wk_ref, wv_ref, out_ref):
    total = dr1_ref[...]
    for refs, w in (((q0, q1), wq_ref), ((k0, k1), wk_ref), ((v0, v1), wv_ref)):
        total = total + nt(jnp.concatenate([r[...] for r in refs], axis=1), w[...])
    out_ref[...] = total.astype(bf16)


def taken_kernel(spot_ref, *refs, lane):
    *theirs, flag_ref, out_ref = refs
    out_ref[...] = taken_sum(theirs, flag_ref[...], lane)


def exchange(x, mask, count):
    return lax.ppermute(x, AXES, [(i, i ^ mask) for i in range(count)])


def flip(x, bit, count):
    return exchange(x, 1 << bit, count)


class Halving:

    def __init__(self, name, send, keep, count):
        self.count = count
        self.left = list(range(count.bit_length() - 2, 0, -1))
        self.tail = send.shape[1:]
        self.parts = [(name, self.tail[0])]
        self.keep = keep
        self.send = send
        self.bit = 0

    def launch(self, *after):
        send, *_ = lax.optimization_barrier((self.send, *after))
        self.recv = exchange(send, 1 << self.bit, self.count)

    def view(self, bit):
        axis = self.left.index(bit)
        a, b = 1 << axis, 1 << (len(self.left) - 1 - axis)
        shape = (a, 2, b, *self.tail)
        return self.keep.reshape(shape), self.recv.reshape(shape)

    def result(self):
        total = self.keep.reshape(self.tail).astype(f32) + self.recv.reshape(self.tail).astype(f32)
        out, at = {}, 0
        for name, n in self.parts:
            out[name] = total[at : at + n]
            at += n
        return out


def add_step(spot, groups, after=()):
    args, shapes, spans = [], [], []
    for sums, bit in groups:
        views = [one.view(bit) for one in sums]
        args += [x for v in views for x in v]
        a, _, b = views[0][0].shape[:3]
        rows = sum(one.tail[0] for one in sums)
        shapes += [jax.ShapeDtypeStruct((a, b, rows, sums[0].tail[1]), bf16)] * 2
    nargs = len(args)

    def body(spot_ref, *refs):
        ins, outs = iter(refs[:nargs]), iter(refs[nargs + len(after) :])
        for sums, bit in groups:
            send, left = next(outs), next(outs)
            own = spot_ref[2 + bit]
            at = 0
            for one in sums:
                keep, recv = next(ins), next(ins)
                n = one.tail[0]
                for half, ref in ((1 - own, send), (own, left)):
                    ref[:, :, at : at + n, :] = (keep[:, half].astype(f32) + recv[:, half].astype(f32)).astype(bf16)
                at += n

    vmem = pl.BlockSpec(memory_space=pltpu.VMEM)
    out = pl.pallas_call(
        body,
        in_specs=[pl.BlockSpec(memory_space=pltpu.SMEM)]
        + [vmem] * nargs
        + [pl.BlockSpec(memory_space=pl.ANY)] * len(after),
        out_specs=[vmem] * len(shapes),
        out_shape=shapes,
        compiler_params=pltpu.CompilerParams(vmem_limit_bytes=16 * MIB),
        cost_estimate=pl.CostEstimate(flops=int(1e5), bytes_accessed=int(1e5), transcendentals=0),
    )(spot, *args, *after)
    got = []
    for n, (sums, bit) in enumerate(groups):
        one = sums[0]
        one.parts = [p for s in sums for p in s.parts]
        one.left = [x for x in one.left if x != bit]
        one.tail = out[2 * n].shape[2:]
        one.send, one.keep, one.bit = out[2 * n], out[2 * n + 1], bit
        one.launch()
        got.append(one)
    return got, (out[-1],)


def block(shape, index):
    return pl.BlockSpec(shape, lambda i, spot: index(i))


def whole(shape):
    return pl.BlockSpec(shape, lambda i, spot: (0,) * len(shape), pipeline_mode=pl.Buffered(1))


SMEM = pl.BlockSpec(memory_space=pltpu.SMEM)


def call(kernel, grid, in_specs, outs, out_specs, scratch, spot, args, micros, after=(), vmem=VMEM):
    nin, nafter = len(in_specs), len(after)

    def body(spot_ref, *refs):
        kernel(spot_ref, *refs[:nin], *refs[nin + nafter :])

    return pl.pallas_call(
        body,
        grid_spec=pltpu.PrefetchScalarGridSpec(
            num_scalar_prefetch=1,
            grid=(grid,),
            in_specs=[*in_specs, *[pl.BlockSpec(memory_space=pl.ANY)] * nafter],
            out_specs=list(out_specs),
            scratch_shapes=scratch,
        ),
        out_shape=[jax.ShapeDtypeStruct(s, d) for s, d in outs],
        compiler_params=pltpu.CompilerParams(
            dimension_semantics=("arbitrary",), vmem_limit_bytes=vmem * MIB
        ),
        cost_estimate=pl.CostEstimate(flops=int(COST * 1e9 * micros), bytes_accessed=int(1e4), transcendentals=0),
    )(spot, *args, *after)


def per_device(
    tokens, out_grad, doc_lengths, w_query, b_query, w_key, b_key, w_value, b_value, w_output, b_output,
    w_inner, b_inner, w_outer, b_outer, gain_first, shift_first, gain_second, shift_second,
):
    rows, width = tokens.shape
    ff = w_inner.shape[1]
    count = lax.axis_size("wide") * lax.axis_size("narrow")
    place = lax.axis_index("wide") * lax.axis_size("narrow") + lax.axis_index("narrow")
    place = place.astype(jnp.int32)
    nchunk = rows // CHUNK
    npair = width // LANES
    heads = 2 * npair
    feat = heads * LANES
    nbits = count.bit_length() - 1
    half = count // 2
    parts = ff // width
    spot = jnp.stack([place * rows, place] + [(place >> b) & 1 for b in range(nbits)])
    at = lambda i: (i, 0)
    tile = block((CHUNK, width), at)
    ftile = block((CHUNK, feat), at)
    col = block((CHUNK, LANES), at)
    square = whole((width, width))
    nvec = R_B1 + parts
    vspec = whole((nvec, width))
    packed = (npair + 1, LANES, LANES)
    pspec = whole(packed)
    fspec = whole((8, LANES))
    fixed = lambda shape: pl.BlockSpec(shape, lambda i, spot: (0,) * len(shape))

    lines = (b_query, b_key, b_value, b_output, gain_first, shift_first, b_outer, gain_second, shift_second)
    k, v, kf, cs, st, en, total, near, flags, vecs = call(
        functools.partial(key_kernel, rows=rows),
        nchunk,
        [SMEM, tile, square, square] + [whole((width,))] * 9 + [whole((ff,))],
        [
            ((rows, width), bf16), ((rows, width), bf16), ((rows, feat), bf16),
            ((rows, LANES), f32), ((rows, LANES), jnp.int32), ((rows, LANES), jnp.int32), (packed, bf16), (packed, bf16),
            ((8, LANES), f32), ((nvec, width), f32),
        ],
        [tile, tile, ftile, col, col, col, fixed(packed), fixed(packed), fixed((8, LANES)), fixed((nvec, width))],
        [pltpu.VMEM(packed, f32)],
        spot,
        (doc_lengths, tokens, w_key, w_value, *lines, b_inner),
        12,
    )

    def run_query(sent):
        return call(
            query_kernel,
            nchunk,
            [tile, square, vspec, col],
            [((rows, width), bf16), ((rows, feat), bf16)],
            [tile, ftile],
            [],
            spot,
            (tokens, w_query, vecs, cs),
            4,
            after=(sent,),
            vmem=FILL,
        )

    groups = 3
    gh = heads // groups
    locals_, kepts = [], []

    def run_mixer(sent):
        n = len(kepts)
        fcol = block((CHUNK, gh * LANES), lambda i: (i, n))
        vcol = block((CHUNK, gh * DH), lambda i: (i, n))
        o, kept = call(
            mixer_kernel,
            nchunk,
            [fcol, fcol, vcol, col, col],
            [((rows, gh * LANES), f32), ((nchunk, gh, LANES, LANES), bf16)],
            [block((CHUNK, gh * LANES), at), block((1, gh, LANES, LANES), lambda i: (i, 0, 0, 0))],
            [pltpu.VMEM((gh, LANES, LANES), f32)],
            spot,
            (qf, kf, v, st, en),
            4,
            after=(sent,),
            vmem=FILL,
        )
        locals_.append(o)
        kepts.append(kept)
        return (o,)

    def joined(a, b, after=()):
        a, b, *after = lax.optimization_barrier((a, b, *after))
        return (a.astype(f32) + b.astype(f32)).astype(bf16)

    before = []
    done = ()
    for bit in range(nbits):
        before.append(flip(total, bit, count))
        if bit == 1:
            q, qf = run_query(total)
            done = (q,)
            from_last = lax.ppermute(near, AXES, [(i, i + 1) for i in range(count - 1)])
        elif bit >= 2 and len(kepts) < groups:
            done = run_mixer(total)
        if bit < nbits - 1:
            total = joined(total, before[-1], done)
    while len(kepts) < groups:
        run_mixer(total)
    before.append(from_last)

    ftile_ff = block((CHUNK, ff), at)
    otile = block((CHUNK, gh * LANES), at)
    (result, mixed, first, act, d_outer, d_inner, d_branch, d_r1, dn, back, near, vgrad, state_in) = call(
        functools.partial(token_kernel, split=12, scans=nbits + 1),
        nchunk,
        [
            otile, otile, otile, ftile, col, tile, tile,
            square, whole((width, ff)), whole((ff, width)), vspec, fspec,
        ] + [pspec] * (nbits + 1),
        [
            ((rows, width), bf16), ((rows, width), bf16), ((rows, width), bf16), ((rows, ff), bf16),
            ((rows, width), bf16), ((rows, ff), bf16), ((rows, width), bf16), ((rows, width), f32),
            ((rows, feat), bf16), (packed, bf16), (packed, bf16), ((VEC_ROWS, width), f32), (packed, bf16),
        ],
        [
            tile, tile, tile, ftile_ff, tile, ftile_ff, tile, tile, ftile,
            fixed(packed), fixed(packed), fixed((VEC_ROWS, width)), fixed(packed),
        ],
        [
            pltpu.VMEM((heads, LANES, LANES), bf16),
            pltpu.VMEM((CHUNK, width), f32),
            pltpu.VMEM((CHUNK, width), f32),
            pltpu.VMEM((CHUNK, ff), f32),
            pltpu.VMEM(packed, f32),
            pltpu.VMEM((CHUNK, width), f32),
            pltpu.VMEM((CHUNK, width), f32),
            pltpu.VMEM((CHUNK, LANES), f32),
            pltpu.VMEM((8 * (V_B1 + parts), width), f32),
        ],
        spot,
        (*locals_, qf, st, tokens, out_grad, w_output, w_inner, w_outer, vecs, flags, *before),
        50,
    )

    piece_o = ff // count
    piece = width // count
    per_step = width // piece_o
    sums = {}

    def run_outer(after):
        cut = piece_o // 2
        spec = block((per_step // 2, cut, width), lambda i: (i, 0, 0))
        out = call(
            functools.partial(outer_grad_kernel, piece=piece_o),
            parts,
            [block((rows, width), lambda i: (0, i)), whole((rows, width))],
            [((half, cut, width), bf16)] * 4,
            [spec] * 4,
            [],
            spot,
            (act, d_outer),
            9,
            after=after,
            vmem=FILL,
        )
        sums["outer0"] = Halving("outer0", out[0], out[1], count)
        sums["outer1"] = Halving("outer1", out[2], out[3], count)
        return (out[1],)

    def run_inner(after, lead):
        n = parts // 2
        full = fixed((half, n * piece, width))
        send, keep = call(
            functools.partial(inner_grad_kernel, piece=piece, parts=n),
            n,
            [whole((rows, width)), block((rows, width), lambda i: (0, lead * n + i))],
            [((half, n * piece, width), bf16)] * 2,
            [full, full],
            [],
            spot,
            (first, d_inner),
            5,
            after=after,
            vmem=FILL,
        )
        sums[f"inner{lead}"] = Halving(f"inner{lead}", send, keep, count)
        return (keep,)

    halves = 2
    hp = npair // halves
    hw = hp * LANES
    dqs = []

    def run_query_back(n, after):
        last = n == halves - 1
        at_ = (lambda i: jnp.minimum(i, nchunk - 1)) if last else (lambda i: i)
        fcol = block((CHUNK, 2 * hw), lambda i: (at_(i), n))
        vcol = block((CHUNK, hw), lambda i: (at_(i), n))
        lcol = block((CHUNK, LANES), lambda i: (at_(i), 0))
        out = block((CHUNK, hw), lambda i: (at_(i), 0))
        kept = block((1, gh, LANES, LANES), lambda i: (at_(i), 0, 0, 0))
        depth = piece + 8
        full = fixed((half, depth, width))
        wide = whole((rows, width))
        got = call(
            functools.partial(
                query_back_kernel, pair0=n * hp, npair=npair, nchunk=nchunk, piece=piece, last=last
            ),
            nchunk + last,
            [fcol, fcol, vcol, fcol, vcol, kept, kept, kept, pspec, lcol, lcol]
            + [wide, whole((rows, hw)), wide, wide, whole((VEC_ROWS, width))] * last,
            [((rows, hw), bf16)] + [((half, depth, width), bf16)] * (4 * last),
            [out] + [full] * (4 * last),
            [pltpu.VMEM((rows, hw), bf16)] * last,
            spot,
            (qf, kf, v, dn, q, *kepts, state_in, st, cs)
            + ((tokens, dqs[0], mixed, d_branch, vgrad) if last else ()),
            9 if last else 7,
            after=after,
            vmem=FILL,
        )
        dqs.append(got[0])
        if last:
            sums["query"] = Halving("query", got[1], got[2], count)
            sums["output"] = Halving("output", got[3], got[4], count)
        return (got[0],)

    theirs = []
    b1, b2 = 1, 2

    def round_of(bit):
        theirs.append(flip(back, bit, count))

    def recvs(*names):
        return tuple(sums[n].recv for n in names)

    round_of(0)
    back = joined(back, theirs[0])
    round_of(1)
    done = run_outer((back,))
    back = joined(back, theirs[1], done)

    round_of(2)
    sums["outer0"].launch(back)
    sums["outer1"].launch(back)
    done = run_inner((back,), 0)
    done = run_inner(done, 1)
    back = joined(back, theirs[2], done + recvs("outer0", "outer1"))

    round_of(3)
    _, done = add_step(spot, [([sums["outer0"]], b1), ([sums["outer1"]], b2)], (back,))
    sums["inner0"].launch(*done)
    sums["inner1"].launch(*done)
    done = run_query_back(0, done)
    back = joined(back, theirs[3], done + recvs("outer0", "outer1", "inner0", "inner1"))

    round_of(4)
    near, *_ = lax.optimization_barrier((near, back))
    from_next = lax.ppermute(near, AXES, [(i + 1, i) for i in range(count - 1)])
    _, done = add_step(spot, [([sums["inner0"]], b1), ([sums["inner1"]], b2)], (back,))
    done = run_query_back(1, done)
    for bit in range(5, nbits):
        back = joined(back, theirs[-1], done)
        round_of(bit)
    done += recvs("inner0", "inner1")
    (back_in,) = call(
        functools.partial(taken_kernel, lane=F_AFTER),
        1,
        [pspec] * (nbits + 1) + [fspec],
        [(packed, bf16)],
        [fixed(packed)],
        [],
        spot,
        (*theirs, from_next, flags),
        1,
        after=done,
        vmem=4,
    )

    dks, dvs = [], []

    def run_value_back(n, after):
        index = lambda i: nchunk - 1 - jnp.minimum(i, nchunk - 1)
        fcol = block((CHUNK, 2 * hw), lambda i: (index(i), n))
        vcol = block((CHUNK, hw), lambda i: (index(i), n))
        bcol = block((CHUNK, LANES), lambda i: (index(i), 0))
        grad = block((CHUNK, hw), lambda i: (index(i), 0))
        full = fixed((half, piece + 8, 2 * hw))
        dk, dv, send, keep = call(
            functools.partial(
                value_back_kernel, pair0=n * hp, npair=npair, nchunk=nchunk, piece=piece, rows=rows
            ),
            nchunk + 1,
            [fcol, fcol, vcol, fcol, vcol, pspec, bcol, bcol, bcol, whole((rows, width))],
            [((rows, hw), bf16)] * 2 + [((half, piece + 8, 2 * hw), bf16)] * 2,
            [grad, grad, full, full],
            [
                pltpu.VMEM((2 * hp, LANES, LANES), f32),
                pltpu.VMEM((rows, 2 * hw), bf16),
                pltpu.VMEM((8, 2 * hw), f32),
            ],
            spot,
            (qf, kf, v, dn, k, back_in, st, en, cs, tokens),
            10,
            after=after,
            vmem=FILL,
        )
        dks.append(dk)
        dvs.append(dv)
        sums[f"value{n}"] = Halving(f"value{n}", send, keep, count)

    g0, g1 = [sums["outer0"], sums["inner0"]], [sums["outer1"], sums["inner1"]]
    (f0, f1), done = add_step(spot, [(g0, b2), (g1, b1)], (back_in,))
    sums["query"].launch(*done)
    sums["output"].launch(*done)
    run_value_back(0, done)

    rest = list(range(3, nbits))
    q, o, kv0 = sums["query"], sums["output"], sums["value0"]
    done = (dks[0], f0.recv, f1.recv, q.recv, o.recv)
    (ffn, q, o), done = add_step(spot, [([f0, f1], rest[0]), ([q], b1), ([o], b2)], done)
    kv0.launch(*done)
    run_value_back(1, done)

    kv1 = sums["value1"]
    kv1.launch(dks[1], ffn.recv, q.recv, o.recv)
    groups = [([kv1], b1), ([kv0], b2), ([q], b2), ([o], b1), ([ffn], rest[1])]
    (kv1, kv0, q, o, ffn), done = add_step(spot, groups, (dks[1], ffn.recv, q.recv, o.recv))

    (grad_tokens,) = call(
        tokens_grad_kernel,
        nchunk,
        [tile] + [block((CHUNK, hw), at)] * 6 + [square] * 3,
        [((rows, width), bf16)],
        [tile],
        [],
        spot,
        (d_r1, *dqs, *dks, *dvs, w_query, w_key, w_value),
        8,
        after=done,
        vmem=FILL,
    )
    done = (grad_tokens, ffn.recv, q.recv, o.recv, kv0.recv, kv1.recv)
    groups = [([kv1], b2), ([kv0], b1), ([q, o], rest[0])]
    more = [([ffn], rest[2])] if len(rest) > 2 else []
    (kv1, kv0, qo, *_), done = add_step(spot, groups + more, done)
    done = (kv0.recv, kv1.recv, qo.recv)
    (kv, qo), done = add_step(spot, [([kv0, kv1], rest[0]), ([qo], rest[1])], done)
    while kv.left:
        open_ = [one for one in (kv, qo, ffn) if one.left]
        add_step(spot, [([one], one.left[-1]) for one in open_])

    found = {}
    for one in (ffn, qo, kv):
        found.update(one.result())
    g_outer = jnp.concatenate([found["outer0"], found["outer1"]])
    cuts = []
    for lead in range(2):
        block_sum = found[f"inner{lead}"]
        cuts += [block_sum[i * piece : (i + 1) * piece] for i in range(parts // 2)]
    g_inner = jnp.concatenate(cuts, axis=1)
    g_query, g_output = found["query"][:piece], found["output"][:piece]
    vec = jnp.concatenate([found["query"][piece:], found["output"][piece:]])
    kv = [found[f"value{n}"] for n in range(halves)]
    g_kv = [jnp.concatenate([s[:piece, m * hw : (m + 1) * hw] for s in kv], axis=1) for m in range(2)]
    b_kv = [jnp.concatenate([s[piece, m * hw : (m + 1) * hw] for s in kv]) for m in range(2)]

    def share(line):
        size = line.shape[0] // count
        return lax.dynamic_slice(line, (place * size,), (size,))

    return (
        result,
        grad_tokens,
        g_query,
        share(vec[VEC_ROWS - 1]),
        g_kv[0],
        share(b_kv[0]),
        g_kv[1],
        share(b_kv[1]),
        g_output,
        share(vec[V_BO]),
        g_inner,
        share(vec[V_B1 : V_B1 + parts].reshape(-1)),
        g_outer,
        share(vec[V_B2]),
        share(vec[V_G1]),
        share(vec[V_E1]),
        share(vec[V_G2]),
        share(vec[V_E2]),
    )


def solution(mesh):
    split = P(AXES, None)
    line = P(AXES)
    return jax.shard_map(
        per_device,
        mesh=mesh,
        in_specs=(split, split) + (P(),) * 17,
        out_specs=(split, split) + (split, line) * 6 + (line,) * 4,
        check_vma=False,
    )
```

```python
import functools
import math

import jax
import jax.numpy as jnp
from jax import lax
from jax.experimental import pallas as pl
from jax.experimental.pallas import tpu as pltpu
from jax.sharding import PartitionSpec as P

DH = 64
LANES = 128
CHUNK = 256
SLICE = 16
EPS = 1e-05
HALF_PI = math.pi / 2.0
MIB = 1 << 20
VMEM = 60
COST = 0.01
FILL = 30
AXES = ("wide", "narrow")

f32 = jnp.float32
bf16 = jnp.bfloat16

R_BQ, R_BK, R_BV, R_BO, R_G1, R_E1, R_B2, R_G2, R_E2, R_B1 = range(10)
V_B2, V_G2, V_E2, V_G1, V_E1, V_BO, V_B1 = range(7)
VEC_ROWS = 16


def nn(a, b):
    return jnp.dot(a, b, preferred_element_type=f32)


def nt(a, b):
    return lax.dot_general(a, b, (((1,), (1,)), ((), ())), preferred_element_type=f32)


def tn(a, b):
    return lax.dot_general(a, b, (((0,), (0,)), ((), ())), preferred_element_type=f32)


def lane_iota(rows, lanes=LANES):
    return lax.broadcasted_iota(jnp.int32, (rows, lanes), 1)


def row_iota(rows, lanes=LANES):
    return lax.broadcasted_iota(jnp.int32, (rows, lanes), 0)


def swap_halves(x):
    return pltpu.roll(x, DH, 1)


def softplus(x):
    return jnp.maximum(x, 0.0) + jnp.log1p(jnp.exp(-jnp.abs(x)))


def sigmoid(x):
    return 1.0 / (1.0 + jnp.exp(-x))


def sine(b):
    s = b * b
    p = 1.0 / 6227020800.0
    for c in (-1.0 / 39916800.0, 1.0 / 362880.0, -1.0 / 5040.0, 1.0 / 120.0, -1.0 / 6.0):
        p = p * s + c
    return b + b * s * p


def features(pair, cs, lo):
    soft = softplus(pair)
    other = swap_halves(soft)
    return (
        (jnp.where(lo, soft, other) * cs).astype(bf16),
        (jnp.where(lo, other, soft) * cs).astype(bf16),
    )


def extended(v, lo):
    one = jnp.ones_like(v)
    return jnp.where(lo, v, one), jnp.where(lo, one, v)


def pairs_of(width):
    return width // LANES


def lookup(len_ref, pos):
    start = jnp.zeros(pos.shape, jnp.int32)
    end = jnp.zeros(pos.shape, jnp.int32)
    edge = jnp.int32(0)
    for doc in range(len_ref.shape[0]):
        here = pos >= edge
        after = edge + len_ref[doc]
        start = jnp.where(here, edge, start)
        end = jnp.where(here, after, end)
        edge = after
    return start, end


F_BEFORE, F_NEXT_B, F_AFTER, F_NEXT_A, F_CLOSING, F_OPENING = range(6)


def flag_table(len_ref, place, rows):
    bit, lane = row_iota(8), lane_iota(8)
    upper = jnp.bitwise_and(jnp.right_shift(jnp.full_like(bit, place), bit), 1) == 1
    base, close = place * rows, (place + 1) * rows
    is_before = (lane == F_BEFORE) | (lane == F_NEXT_B)
    is_after = (lane == F_AFTER) | (lane == F_NEXT_A)
    pos = jnp.where(
        is_before,
        base - 1,
        jnp.where(is_after, close, jnp.where(lane == F_CLOSING, close - 1, base)),
    )
    start, end = lookup(len_ref, pos)
    one, zero = jnp.ones(bit.shape, f32), jnp.zeros(bit.shape, f32)
    is_long = jnp.where((end - start) > rows, one, zero)
    near = jnp.where((pos >= 0) & (pos < end), 1.0 - is_long, zero)
    out = is_long
    out = jnp.where(lane == F_BEFORE, jnp.where(upper, is_long, zero), out)
    out = jnp.where(lane == F_AFTER, jnp.where(upper, zero, is_long), out)
    return jnp.where((lane == F_NEXT_B) | (lane == F_NEXT_A), near, out)


def key_kernel(
    spot_ref, len_ref, x_ref, wk_ref, wv_ref,
    bq, bk, bv, bo, g1, e1, b2, g2, e2, b1,
    k_ref, v_ref, kf_ref, cs_ref, st_ref, en_ref, state_ref, next_ref, flag_ref, vec_ref,
    total,
    *, rows,
):
    step = pl.program_id(0)
    base = spot_ref[0]
    width = x_ref.shape[1]
    first = base + step * CHUNK
    pos = first + row_iota(CHUNK)
    lane = lane_iota(CHUNK)
    lo = lane < DH

    @pl.when(step == 0)
    def _():
        total[...] = jnp.zeros_like(total)
        flag_ref[...] = flag_table(len_ref, spot_ref[1], rows)
        for r, ref in enumerate((bq, bk, bv, bo, g1, e1, b2, g2, e2)):
            vec_ref[r : r + 1, :] = ref[...].astype(f32).reshape(1, width)
        for r in range(b1.shape[0] // width):
            vec_ref[R_B1 + r : R_B1 + r + 1, :] = (
                b1[r * width : (r + 1) * width].astype(f32).reshape(1, width)
            )

    start, end = lookup(len_ref, pos)
    part = jnp.where(lo, end - pos, pos - start).astype(f32)
    cs = sine(HALF_PI * part / (end - start).astype(f32))
    cs_ref[...] = cs
    st_ref[...] = start
    en_ref[...] = end

    x = x_ref[...]
    k = (nn(x, wk_ref[...]) + vec_ref[R_BK : R_BK + 1, :]).astype(bf16)
    v = (nn(x, wv_ref[...]) + vec_ref[R_BV : R_BV + 1, :]).astype(bf16)
    k_ref[...] = k
    v_ref[...] = v
    closing = end >= base + rows
    slots = lane_iota(LANES)
    lo_state = slots < DH

    npair = pairs_of(width)
    zcol = jnp.zeros((LANES, LANES), f32)
    for g in range(npair):
        cols = slice(g * LANES, (g + 1) * LANES)
        fa, fb = features(k[:, cols].astype(f32), cs, lo)
        kf_ref[:, 2 * g * LANES : (2 * g + 1) * LANES] = fa
        kf_ref[:, (2 * g + 1) * LANES : (2 * g + 2) * LANES] = fb
        va, vb = extended(v[:, cols], lo)
        zero = jnp.zeros_like(fa)
        sa = tn(jnp.where(closing, fa, zero), va)
        sb = tn(jnp.where(closing, fb, zero), vb)
        total[g] += jnp.where(lo_state, sa, sb)
        zcol = jnp.where(slots == DH + g, sa, jnp.where(slots == g, sb, zcol))
    total[npair] += zcol

    @pl.when(step == pl.num_programs(0) - 1)
    def _():
        split_long(total[...], flag_ref[0:1, F_CLOSING : F_CLOSING + 1], state_ref, next_ref)


def split_long(total, flag, long_ref, next_ref):
    long_ref[...] = (total * flag).astype(bf16)
    next_ref[...] = (total * (1.0 - flag)).astype(bf16)


def taken_sum(refs, flags, lane):
    *scans, near = refs
    total = near[...].astype(f32) * flags[0:1, lane + 1 : lane + 2]
    for bit, ref in enumerate(scans):
        total = total + ref[...].astype(f32) * flags[bit : bit + 1, lane : lane + 1]
    return total.astype(bf16)


def unpack_state(state_ref, g, npair, lo, slots):
    pair = state_ref[g].astype(f32)
    z = state_ref[npair].astype(f32)
    za = z[:, DH + g : DH + g + 1]
    zb = z[:, g : g + 1]
    return jnp.where(lo, pair, za), jnp.where(lo, zb, pair)


def unpack_grad_state(state_ref, g, npair, lo, slots):
    pair = state_ref[g].astype(f32)
    z = state_ref[npair].astype(f32)
    za = jnp.where(slots == DH, z[:, DH + g : DH + g + 1], 0.0)
    zb = jnp.where(slots == 0, z[:, g : g + 1], 0.0)
    return jnp.where(lo, pair, za), jnp.where(lo, zb, pair)


def query_kernel(spot_ref, x_ref, wq_ref, vec_ref, cs_ref, q_ref, qf_ref):
    q = (nn(x_ref[...], wq_ref[...]) + vec_ref[R_BQ : R_BQ + 1, :]).astype(bf16)
    q_ref[...] = q
    lo = lane_iota(CHUNK) < DH
    cs = cs_ref[...]
    for g in range(pairs_of(q.shape[1])):
        fa, fb = features(q[:, g * LANES : (g + 1) * LANES].astype(f32), cs, lo)
        qf_ref[:, 2 * g * LANES : (2 * g + 1) * LANES] = fa
        qf_ref[:, (2 * g + 1) * LANES : (2 * g + 2) * LANES] = fb


def mixer_kernel(spot_ref, qf_ref, kf_ref, v_ref, st_ref, en_ref, o_ref, kept_ref, local):
    step = pl.program_id(0)
    first = spot_ref[0] + step * CHUNK
    start, end = st_ref[...], en_ref[...]
    start2 = jnp.concatenate([start, start], axis=1)
    ipos = first + row_iota(CHUNK, CHUNK)
    jpos = first + lane_iota(CHUNK, CHUNK)
    mask = (jpos <= ipos) & (jpos >= start2)
    carried = start < first
    closing = end >= first + CHUNK
    keep = start[CHUNK - 1 : CHUNK, :] < first
    lo = lane_iota(CHUNK) < DH

    @pl.when(step == 0)
    def _():
        local[...] = jnp.zeros_like(local)

    for g in range(pairs_of(v_ref.shape[1])):
        vs = extended(v_ref[:, g * LANES : (g + 1) * LANES], lo)
        for s in range(2):
            h = 2 * g + s
            cols = slice(h * LANES, (h + 1) * LANES)
            qf, kf, v = qf_ref[:, cols], kf_ref[:, cols], vs[s]
            probs = jnp.where(mask, nt(qf, kf), 0.0).astype(bf16)
            held = local[h].astype(bf16)
            kept_ref[0, h] = held
            o_ref[:, cols] = nn(probs, v) + jnp.where(carried, nn(qf, held), 0.0)
            local[h] = jnp.where(keep, local[h], 0.0) + tn(
                jnp.where(closing, kf, jnp.zeros_like(kf)), v
            )


def gelu_and_slope(u):
    z = jnp.abs(u) * (1.0 / math.sqrt(2.0))
    t = 1.0 / (1.0 + 0.3275911 * z)
    p = 0.5 * 1.061405429
    for c in (-1.453152027, 1.421413741, -0.284496736, 0.254829592):
        p = p * t + 0.5 * c
    e = jnp.exp(-0.5 * u * u)
    tail = p * t * e
    gauss = jnp.where(u >= 0.0, 1.0 - tail, tail)
    return u * gauss, gauss + u * e * (1.0 / math.sqrt(2.0 * math.pi))


def token_kernel(
    spot_ref, o0_ref, o1_ref, o2_ref, qf_ref, st_ref, x_ref, go_ref,
    wo_ref, w1_ref, w2_ref, vec_ref, flag_ref, *refs, split, scans,
):
    theirs = refs[:scans]
    (
        out_ref, mixed_ref, first_ref, act_ref, douter_ref, dinner_ref, dbranch_ref, dr1_ref,
        dn_ref, back_ref, near_ref, vgrad_ref, state_ref,
        states, ratio, rden_s, slope, back_s, flow, norm_s, rstd_s, sums,
    ) = refs[scans:]
    step = pl.program_id(0)
    base = spot_ref[0]
    chunk, width = x_ref.shape
    ff = w1_ref.shape[1]
    npair = pairs_of(width)
    lane = lane_iota(chunk)
    lo = lane < DH
    slots = lane_iota(LANES)
    lo_state = slots < DH
    start = st_ref[...]

    @pl.when(step == 0)
    def _():
        state_ref[...] = taken_sum(theirs, flag_ref[...], F_BEFORE)
        for g in range(npair):
            a, b = unpack_state(state_ref, g, npair, lo_state, slots)
            states[2 * g] = a.astype(bf16)
            states[2 * g + 1] = b.astype(bf16)
        back_s[...] = jnp.zeros_like(back_s)
        sums[...] = jnp.zeros_like(sums)

    carried = start < base
    o_refs = (o0_ref, o1_ref, o2_ref)
    for g in range(npair):
        both = []
        for s in range(2):
            h = 2 * g + s
            o_of = o_refs[h // 4]
            local = o_of[:, (h % 4) * LANES : (h % 4 + 1) * LANES]
            far = nn(qf_ref[:, h * LANES : (h + 1) * LANES], states[h])
            both.append(local + jnp.where(carried, far, 0.0))
        numer = jnp.where(lo, both[0], both[1])
        rden = 1.0 / swap_halves(jnp.where(lo, both[1], both[0]))
        cols = slice(g * LANES, (g + 1) * LANES)
        rden_s[:, cols] = rden
        mix = numer * rden
        ratio[:, cols] = mix
        mixed_ref[:, cols] = mix.astype(bf16)

    def row(r):
        return vec_ref[r : r + 1, :]

    def mean(v):
        return jnp.sum(v, axis=-1, keepdims=True) * (1.0 / width)

    def norm(resid):
        cent = resid - mean(resid)
        rstd = lax.rsqrt(mean(cent * cent) + EPS)
        return cent * rstd, rstd

    def norm_back(grad, normed, rstd, gain):
        d_n = grad * gain
        return rstd * (d_n - mean(d_n) - normed * mean(d_n * normed))

    def add_sum(r, v, cols=slice(None)):
        sums[8 * r : 8 * r + 8, cols] += v

    flow[...] = nn(mixed_ref[...], wo_ref[...])
    for at in range(0, chunk, SLICE):
        sl = slice(at, at + SLICE)
        n1, rstd1 = norm(x_ref[sl, :].astype(f32) + flow[sl, :] + row(R_BO))
        norm_s[sl, :] = n1
        rstd_s[sl, :] = jnp.broadcast_to(rstd1, (SLICE, LANES))
        first_ref[sl, :] = (n1 * row(R_G1) + row(R_E1)).astype(bf16)

    part = ff // split

    def inner_of(i):
        flat, off = i * part // width, i * part % width
        bias = vec_ref[R_B1 + flat : R_B1 + flat + 1, off : off + part]
        return nn(first_ref[...], w1_ref[:, i * part : (i + 1) * part]) + bias

    ahead = inner_of(0)
    outer = jnp.zeros((chunk, width), f32)
    last = None
    for i in range(split):
        cols = slice(i * part, (i + 1) * part)
        now = ahead
        if i + 1 < split:
            ahead = inner_of(i + 1)
        if last is not None:
            outer = outer + nn(last, w2_ref[(i - 1) * part : i * part, :])
        act, sl = gelu_and_slope(now)
        last = act.astype(bf16)
        act_ref[:, cols] = last
        slope[:, cols] = sl
    flow[...] = outer + nn(last, w2_ref[(split - 1) * part :, :])

    g2_sum = e2_sum = b2_sum = jnp.zeros((8, width), f32)
    for at in range(0, chunk, SLICE):
        sl = slice(at, at + SLICE)
        n2, rstd2 = norm(first_ref[sl, :].astype(f32) + flow[sl, :] + row(R_B2))
        out_ref[sl, :] = (n2 * row(R_G2) + row(R_E2)).astype(bf16)
        grad = go_ref[sl, :].astype(f32)
        g2_sum = g2_sum + fold_rows(grad * n2)
        e2_sum = e2_sum + fold_rows(grad)
        d_r2 = norm_back(grad, n2, rstd2, row(R_G2))
        b2_sum = b2_sum + fold_rows(d_r2)
        douter_ref[sl, :] = d_r2.astype(bf16)
        dr1_ref[sl, :] = d_r2
    add_sum(V_G2, g2_sum)
    add_sum(V_E2, e2_sum)
    add_sum(V_B2, b2_sum)

    for i in range(split):
        cols = slice(i * part, (i + 1) * part)
        flat = i * part // width
        off = i * part % width
        d_inner = nt(douter_ref[...], w2_ref[cols, :]) * slope[:, cols]
        dinner_ref[:, cols] = d_inner.astype(bf16)
        add_sum(V_B1 + flat, fold_rows(d_inner), slice(off, off + part))
    flow[...] = nt(dinner_ref[...], w1_ref[...])

    g1_sum = e1_sum = bo_sum = jnp.zeros((8, width), f32)
    for at in range(0, chunk, SLICE):
        sl = slice(at, at + SLICE)
        d_first = dr1_ref[sl, :] + flow[sl, :]
        n1 = norm_s[sl, :]
        g1_sum = g1_sum + fold_rows(d_first * n1)
        e1_sum = e1_sum + fold_rows(d_first)
        d_r1 = norm_back(d_first, n1, rstd_s[sl, 0:1], row(R_G1))
        bo_sum = bo_sum + fold_rows(d_r1)
        dr1_ref[sl, :] = d_r1
        dbranch_ref[sl, :] = d_r1.astype(bf16)
    add_sum(V_G1, g1_sum)
    add_sum(V_E1, e1_sum)
    add_sum(V_BO, bo_sum)

    flow[...] = nt(dbranch_ref[...], wo_ref[...])
    opening = start <= base
    zcol = jnp.zeros((LANES, LANES), f32)
    for g in range(npair):
        cols = slice(g * LANES, (g + 1) * LANES)
        dn = flow[:, cols] * rden_s[:, cols]
        prod = dn * ratio[:, cols]
        dda = -jnp.sum(jnp.where(lo, prod, 0.0), axis=1, keepdims=True)
        ddb = -jnp.sum(jnp.where(lo, 0.0, prod), axis=1, keepdims=True)
        hia, hib = dda.astype(bf16).astype(f32), ddb.astype(bf16).astype(f32)
        exa = jnp.where(lane == DH, hia, jnp.where(lane == DH + 1, dda - hia, 0.0))
        exb = jnp.where(lane == 0, hib, jnp.where(lane == 1, ddb - hib, 0.0))
        dna = jnp.where(lo, dn, exa).astype(bf16)
        dnb = jnp.where(lo, exb, dn).astype(bf16)
        ca = slice(2 * g * LANES, (2 * g + 1) * LANES)
        cb = slice((2 * g + 1) * LANES, (2 * g + 2) * LANES)
        dn_ref[:, ca] = dna
        dn_ref[:, cb] = dnb
        zero = jnp.zeros((chunk, LANES), bf16)
        ga = tn(jnp.where(opening, qf_ref[:, ca], zero), dna)
        gb = tn(jnp.where(opening, qf_ref[:, cb], zero), dnb)
        back_s[g] += jnp.where(lo_state, ga, gb)
        za = ga[:, DH : DH + 1] + ga[:, DH + 1 : DH + 2]
        zb = gb[:, 0:1] + gb[:, 1:2]
        zcol = jnp.where(slots == DH + g, za, jnp.where(slots == g, zb, zcol))
    back_s[npair] += zcol

    @pl.when(step == pl.num_programs(0) - 1)
    def _():
        split_long(back_s[...], flag_ref[0:1, F_OPENING : F_OPENING + 1], back_ref, near_ref)
        vgrad_ref[...] = jnp.zeros_like(vgrad_ref)
        for r in range(sums.shape[0] // 8):
            vgrad_ref[r : r + 1, :] = jnp.sum(sums[8 * r : 8 * r + 8, :], axis=0, keepdims=True)


def fold_rows(v):
    return jnp.sum(v.reshape(v.shape[0] // 8, 8, v.shape[1]), axis=0)


def store_pieces(own, value, rows, send_ref, keep_ref, at):
    count = value.shape[0] // rows
    value = value.astype(bf16)
    for bit in range(2):

        @pl.when(own == bit)
        def _():
            for d in range(count):
                ref = keep_ref if d % 2 == bit else send_ref
                ref[d // 2, at : at + rows, :] = value[d * rows : (d + 1) * rows, :]


def store_lines(line, send_ref, keep_ref, at):
    line = line.astype(bf16)
    for m in range(send_ref.shape[0]):
        send_ref[m, at : at + line.shape[0], :] = line
        keep_ref[m, at : at + line.shape[0], :] = line


def query_back_kernel(
    spot_ref, qf_ref, kf_ref, v_ref, dn_ref, q_ref, kept0, kept1, kept2, state_ref, st_ref, cs_ref, *refs,
    pair0, npair, nchunk, piece, last,
):
    if last:
        x_ref, other_ref, mixed_ref, dbranch_ref, vec_ref, dq_ref, send0, keep0, send1, keep1, grads = refs
    else:
        (dq_ref,) = refs
    step = pl.program_id(0)
    base = spot_ref[0]
    keepers = (kept0, kept1, kept2)
    two = range(2)

    def chunk_step():
        lo = lane_iota(CHUNK) < DH
        slots = lane_iota(LANES)
        lo_state = slots < DH
        first = base + step * CHUNK
        start, cs = st_ref[...], cs_ref[...]
        start2 = jnp.concatenate([start, start], axis=1)
        ipos = first + row_iota(CHUNK, CHUNK)
        jpos = first + lane_iota(CHUNK, CHUNK)
        mask = (jpos <= ipos) & (jpos >= start2)
        carried = start < first
        from_far = start[0:1, :] < base
        at = pl.ds(pl.multiple_of(step * CHUNK, CHUNK), CHUNK)
        for g in range(pairs_of(v_ref.shape[1])):
            pair = slice(g * LANES, (g + 1) * LANES)
            cols = [slice((2 * g + s) * LANES, (2 * g + s + 1) * LANES) for s in two]
            heads = [2 * (pair0 + g) + s for s in two]
            vs = extended(v_ref[:, pair], lo)
            far = unpack_state(state_ref, pair0 + g, npair, lo_state, slots)
            dns = [dn_ref[:, c] for c in cols]
            d_probs = [nt(dns[s], vs[s]) for s in two]
            d_probs = [jnp.where(mask, d, 0.0).astype(bf16) for d in d_probs]
            held = [
                (keepers[heads[s] // 4][0, heads[s] % 4].astype(f32) + jnp.where(from_far, far[s], 0.0)).astype(bf16)
                for s in two
            ]
            d_qf = [
                nn(d_probs[s], kf_ref[:, cols[s]]) + jnp.where(carried, nt(dns[s], held[s]), 0.0) for s in two
            ]
            turned = [d * cs for d in d_qf]
            turned = [t + swap_halves(t) for t in turned]
            value = jnp.where(lo, turned[0], turned[1]) * sigmoid(q_ref[:, pair].astype(f32))
            value = value.astype(bf16)
            dq_ref[:, pair] = value
            if last:
                grads[at, pair] = value

    if not last:
        chunk_step()
        return

    pl.when(step < nchunk)(chunk_step)

    @pl.when(step == nchunk)
    def _():
        own = spot_ref[2]
        whole_q = jnp.concatenate([other_ref[...], grads[...]], axis=1)
        store_pieces(own, tn(x_ref[...], whole_q), piece, send0, keep0, 0)
        store_pieces(own, tn(mixed_ref[...], dbranch_ref[...]), piece, send1, keep1, 0)
        total = jnp.sum(fold_rows(whole_q.astype(f32)), axis=0, keepdims=True)
        vec = jnp.where(row_iota(VEC_ROWS, total.shape[1]) == VEC_ROWS - 1, total, vec_ref[...])
        store_lines(vec[:8], send0, keep0, piece)
        store_lines(vec[8:], send1, keep1, piece)


def value_back_kernel(
    spot_ref, qf_ref, kf_ref, v_ref, dn_ref, k_ref, back_ref, st_ref, en_ref, cs_ref, x_ref,
    dk_ref, dv_ref, send_ref, keep_ref,
    onward_state, grads, lines,
    *, pair0, npair, nchunk, piece, rows,
):
    base = spot_ref[0]
    wide = v_ref.shape[1]

    @pl.when(pl.program_id(0) == 0)
    def _():
        onward_state[...] = jnp.zeros_like(onward_state)
        lines[...] = jnp.zeros_like(lines)

    @pl.when(pl.program_id(0) < nchunk)
    def _():
        lo = lane_iota(CHUNK) < DH
        slots = lane_iota(LANES)
        lo_state = slots < DH
        step = nchunk - 1 - pl.program_id(0)
        first = base + step * CHUNK
        start, end, cs = st_ref[...], en_ref[...], cs_ref[...]
        end2 = jnp.concatenate([end, end], axis=1)
        jpos = first + row_iota(CHUNK, CHUNK)
        ipos = first + lane_iota(CHUNK, CHUNK)
        mask = (jpos <= ipos) & (ipos < end2)
        onward = end > first + CHUNK
        opening = start <= first
        to_far = end[CHUNK - 1 : CHUNK, :] > base + rows
        keep = end[0:1, :] > first + CHUNK
        at = pl.ds(pl.multiple_of(step * CHUNK, CHUNK), CHUNK)
        zero = jnp.zeros((CHUNK, LANES), bf16)
        two = range(2)
        for g in range(pairs_of(wide)):
            pair = slice(g * LANES, (g + 1) * LANES)
            cols = [slice((2 * g + s) * LANES, (2 * g + s + 1) * LANES) for s in two]
            vs = extended(v_ref[:, pair], lo)
            far = unpack_grad_state(back_ref, pair0 + g, npair, lo_state, slots)
            qf, kf = [qf_ref[:, c] for c in cols], [kf_ref[:, c] for c in cols]
            dn = [dn_ref[:, c] for c in cols]
            probs = [nt(kf[s], qf[s]) for s in two]
            d_probs = [nt(vs[s], dn[s]) for s in two]
            probs = [jnp.where(mask, p, 0.0).astype(bf16) for p in probs]
            d_probs = [jnp.where(mask, p, 0.0).astype(bf16) for p in d_probs]
            ahead = [onward_state[2 * g + s] for s in two]
            ahead16 = [(ahead[s] + jnp.where(to_far, far[s], 0.0)).astype(bf16) for s in two]
            more = [tn(jnp.where(opening, qf[s], zero), dn[s]) for s in two]
            d_kf = [nn(d_probs[s], qf[s]) + jnp.where(onward, nt(vs[s], ahead16[s]), 0.0) for s in two]
            d_v = [nn(probs[s], dn[s]) + jnp.where(onward, nn(kf[s], ahead16[s]), 0.0) for s in two]
            for s in two:
                onward_state[2 * g + s] = jnp.where(keep, ahead[s], 0.0) + more[s]
            turned = [d * cs for d in d_kf]
            turned = [t + swap_halves(t) for t in turned]
            both = (
                (jnp.where(lo, turned[0], turned[1]) * sigmoid(k_ref[:, pair].astype(f32)), dk_ref),
                (jnp.where(lo, d_v[0], d_v[1]), dv_ref),
            )
            for n, (value, ref) in enumerate(both):
                spread = slice(n * wide + g * LANES, n * wide + (g + 1) * LANES)
                lines[0:8, spread] += fold_rows(value)
                value = value.astype(bf16)
                ref[:, pair] = value
                grads[at, spread] = value

    @pl.when(pl.program_id(0) == nchunk)
    def _():
        store_pieces(spot_ref[2], tn(x_ref[...], grads[...]), piece, send_ref, keep_ref, 0)
        total = jnp.sum(lines[...], axis=0, keepdims=True)
        store_lines(jnp.broadcast_to(total, lines.shape), send_ref, keep_ref, piece)


def outer_grad_kernel(spot_ref, act_ref, d_ref, send0, keep0, send1, keep1, *, piece):
    value = tn(act_ref[...], d_ref[...]).astype(bf16)
    cut = piece // 2
    for bit in range(2):

        @pl.when(spot_ref[2] == bit)
        def _():
            for d in range(value.shape[0] // piece):
                first, second = (keep0, keep1) if d % 2 == bit else (send0, send1)
                first[d // 2] = value[d * piece : d * piece + cut, :]
                second[d // 2] = value[d * piece + cut : (d + 1) * piece, :]


def inner_grad_kernel(spot_ref, first_ref, dinner_ref, send_ref, keep_ref, *, piece, parts):
    for i in range(parts):

        @pl.when(pl.program_id(0) == i)
        def _():
            value = tn(first_ref[...], dinner_ref[...])
            store_pieces(spot_ref[2], value, piece, send_ref, keep_ref, i * piece)


def tokens_grad_kernel(spot_ref, dr1_ref, q0, q1, k0, k1, v0, v1, wq_ref, wk_ref, wv_ref, out_ref):
    total = dr1_ref[...]
    for refs, w in (((q0, q1), wq_ref), ((k0, k1), wk_ref), ((v0, v1), wv_ref)):
        total = total + nt(jnp.concatenate([r[...] for r in refs], axis=1), w[...])
    out_ref[...] = total.astype(bf16)


def taken_kernel(spot_ref, *refs, lane):
    *theirs, flag_ref, out_ref = refs
    out_ref[...] = taken_sum(theirs, flag_ref[...], lane)


def exchange(x, mask, count):
    return lax.ppermute(x, AXES, [(i, i ^ mask) for i in range(count)])


def flip(x, bit, count):
    return exchange(x, 1 << bit, count)


class Halving:

    def __init__(self, name, send, keep, count):
        self.count = count
        self.left = list(range(count.bit_length() - 2, 0, -1))
        self.tail = send.shape[1:]
        self.parts = [(name, self.tail[0])]
        self.keep = keep
        self.send = send
        self.bit = 0

    def launch(self, *after):
        send, *_ = lax.optimization_barrier((self.send, *after))
        self.recv = exchange(send, 1 << self.bit, self.count)

    def view(self, bit):
        axis = self.left.index(bit)
        a, b = 1 << axis, 1 << (len(self.left) - 1 - axis)
        shape = (a, 2, b, *self.tail)
        return self.keep.reshape(shape), self.recv.reshape(shape)

    def result(self):
        total = self.keep.reshape(self.tail).astype(f32) + self.recv.reshape(self.tail).astype(f32)
        out, at = {}, 0
        for name, n in self.parts:
            out[name] = total[at : at + n]
            at += n
        return out


def add_step(spot, groups, after=()):
    args, shapes, spans = [], [], []
    for sums, bit in groups:
        views = [one.view(bit) for one in sums]
        args += [x for v in views for x in v]
        a, _, b = views[0][0].shape[:3]
        rows = sum(one.tail[0] for one in sums)
        shapes += [jax.ShapeDtypeStruct((a, b, rows, sums[0].tail[1]), bf16)] * 2
    nargs = len(args)

    def body(spot_ref, *refs):
        ins, outs = iter(refs[:nargs]), iter(refs[nargs + len(after) :])
        for sums, bit in groups:
            send, left = next(outs), next(outs)
            own = spot_ref[2 + bit]
            at = 0
            for one in sums:
                keep, recv = next(ins), next(ins)
                n = one.tail[0]
                for half, ref in ((1 - own, send), (own, left)):
                    ref[:, :, at : at + n, :] = (keep[:, half].astype(f32) + recv[:, half].astype(f32)).astype(bf16)
                at += n

    vmem = pl.BlockSpec(memory_space=pltpu.VMEM)
    out = pl.pallas_call(
        body,
        in_specs=[pl.BlockSpec(memory_space=pltpu.SMEM)]
        + [vmem] * nargs
        + [pl.BlockSpec(memory_space=pl.ANY)] * len(after),
        out_specs=[vmem] * len(shapes),
        out_shape=shapes,
        compiler_params=pltpu.CompilerParams(vmem_limit_bytes=16 * MIB),
        cost_estimate=pl.CostEstimate(flops=int(1e5), bytes_accessed=int(1e5), transcendentals=0),
    )(spot, *args, *after)
    got = []
    for n, (sums, bit) in enumerate(groups):
        one = sums[0]
        one.parts = [p for s in sums for p in s.parts]
        one.left = [x for x in one.left if x != bit]
        one.tail = out[2 * n].shape[2:]
        one.send, one.keep, one.bit = out[2 * n], out[2 * n + 1], bit
        one.launch()
        got.append(one)
    return got, (out[-1],)


def block(shape, index):
    return pl.BlockSpec(shape, lambda i, spot: index(i))


def whole(shape):
    return pl.BlockSpec(shape, lambda i, spot: (0,) * len(shape), pipeline_mode=pl.Buffered(1))


SMEM = pl.BlockSpec(memory_space=pltpu.SMEM)


def call(kernel, grid, in_specs, outs, out_specs, scratch, spot, args, micros, after=(), vmem=VMEM, hbm=()):
    nin, nafter = len(in_specs), len(after)
    args = [
        pltpu.with_memory_space_constraint(x, pltpu.HBM) if n in hbm else x for n, x in enumerate(args)
    ]

    def body(spot_ref, *refs):
        kernel(spot_ref, *refs[:nin], *refs[nin + nafter :])

    return pl.pallas_call(
        body,
        grid_spec=pltpu.PrefetchScalarGridSpec(
            num_scalar_prefetch=1,
            grid=(grid,),
            in_specs=[*in_specs, *[pl.BlockSpec(memory_space=pl.ANY)] * nafter],
            out_specs=list(out_specs),
            scratch_shapes=scratch,
        ),
        out_shape=[jax.ShapeDtypeStruct(s, d) for s, d in outs],
        compiler_params=pltpu.CompilerParams(
            dimension_semantics=("arbitrary",), vmem_limit_bytes=vmem * MIB
        ),
        cost_estimate=pl.CostEstimate(flops=int(COST * 1e9 * micros), bytes_accessed=int(1e4), transcendentals=0),
    )(spot, *args, *after)


def per_device(
    tokens, out_grad, doc_lengths, w_query, b_query, w_key, b_key, w_value, b_value, w_output, b_output,
    w_inner, b_inner, w_outer, b_outer, gain_first, shift_first, gain_second, shift_second,
):
    rows, width = tokens.shape
    ff = w_inner.shape[1]
    count = lax.axis_size("wide") * lax.axis_size("narrow")
    place = lax.axis_index("wide") * lax.axis_size("narrow") + lax.axis_index("narrow")
    place = place.astype(jnp.int32)
    nchunk = rows // CHUNK
    npair = width // LANES
    heads = 2 * npair
    feat = heads * LANES
    nbits = count.bit_length() - 1
    half = count // 2
    parts = ff // width
    spot = jnp.stack([place * rows, place] + [(place >> b) & 1 for b in range(nbits)])
    at = lambda i: (i, 0)
    tile = block((CHUNK, width), at)
    ftile = block((CHUNK, feat), at)
    col = block((CHUNK, LANES), at)
    square = whole((width, width))
    nvec = R_B1 + parts
    vspec = whole((nvec, width))
    packed = (npair + 1, LANES, LANES)
    pspec = whole(packed)
    fspec = whole((8, LANES))
    fixed = lambda shape: pl.BlockSpec(shape, lambda i, spot: (0,) * len(shape))

    lines = (b_query, b_key, b_value, b_output, gain_first, shift_first, b_outer, gain_second, shift_second)
    k, v, kf, cs, st, en, total, near, flags, vecs = call(
        functools.partial(key_kernel, rows=rows),
        nchunk,
        [SMEM, tile, square, square] + [whole((width,))] * 9 + [whole((ff,))],
        [
            ((rows, width), bf16), ((rows, width), bf16), ((rows, feat), bf16),
            ((rows, LANES), f32), ((rows, LANES), jnp.int32), ((rows, LANES), jnp.int32), (packed, bf16), (packed, bf16),
            ((8, LANES), f32), ((nvec, width), f32),
        ],
        [tile, tile, ftile, col, col, col, fixed(packed), fixed(packed), fixed((8, LANES)), fixed((nvec, width))],
        [pltpu.VMEM(packed, f32)],
        spot,
        (doc_lengths, tokens, w_key, w_value, *lines, b_inner),
        12,
    )

    def run_query(sent):
        return call(
            query_kernel,
            nchunk,
            [tile, square, vspec, col],
            [((rows, width), bf16), ((rows, feat), bf16)],
            [tile, ftile],
            [],
            spot,
            (tokens, w_query, vecs, cs),
            4,
            after=(sent,),
            vmem=FILL,
        )

    groups = 3
    gh = heads // groups
    locals_, kepts = [], []

    def run_mixer(sent):
        n = len(kepts)
        fcol = block((CHUNK, gh * LANES), lambda i: (i, n))
        vcol = block((CHUNK, gh * DH), lambda i: (i, n))
        o, kept = call(
            mixer_kernel,
            nchunk,
            [fcol, fcol, vcol, col, col],
            [((rows, gh * LANES), f32), ((nchunk, gh, LANES, LANES), bf16)],
            [block((CHUNK, gh * LANES), at), block((1, gh, LANES, LANES), lambda i: (i, 0, 0, 0))],
            [pltpu.VMEM((gh, LANES, LANES), f32)],
            spot,
            (qf, kf, v, st, en),
            4,
            after=(sent,),
            vmem=FILL,
        )
        locals_.append(o)
        kepts.append(kept)
        return (o,)

    def joined(a, b, after=()):
        a, b, *after = lax.optimization_barrier((a, b, *after))
        return (a.astype(f32) + b.astype(f32)).astype(bf16)

    before = []
    done = ()
    for bit in range(nbits):
        before.append(flip(total, bit, count))
        if bit == 1:
            q, qf = run_query(total)
            done = (q,)
            from_last = lax.ppermute(near, AXES, [(i, i + 1) for i in range(count - 1)])
        elif bit >= 2 and len(kepts) < groups:
            done = run_mixer(total)
        if bit < nbits - 1:
            total = joined(total, before[-1], done)
    while len(kepts) < groups:
        run_mixer(total)
    before.append(from_last)

    ftile_ff = block((CHUNK, ff), at)
    otile = block((CHUNK, gh * LANES), at)
    (result, mixed, first, act, d_outer, d_inner, d_branch, d_r1, dn, back, near, vgrad, state_in) = call(
        functools.partial(token_kernel, split=12, scans=nbits + 1),
        nchunk,
        [
            otile, otile, otile, ftile, col, tile, tile,
            square, whole((width, ff)), whole((ff, width)), vspec, fspec,
        ] + [pspec] * (nbits + 1),
        [
            ((rows, width), bf16), ((rows, width), bf16), ((rows, width), bf16), ((rows, ff), bf16),
            ((rows, width), bf16), ((rows, ff), bf16), ((rows, width), bf16), ((rows, width), f32),
            ((rows, feat), bf16), (packed, bf16), (packed, bf16), ((VEC_ROWS, width), f32), (packed, bf16),
        ],
        [
            tile, tile, tile, ftile_ff, tile, ftile_ff, tile, tile, ftile,
            fixed(packed), fixed(packed), fixed((VEC_ROWS, width)), fixed(packed),
        ],
        [
            pltpu.VMEM((heads, LANES, LANES), bf16),
            pltpu.VMEM((CHUNK, width), f32),
            pltpu.VMEM((CHUNK, width), f32),
            pltpu.VMEM((CHUNK, ff), f32),
            pltpu.VMEM(packed, f32),
            pltpu.VMEM((CHUNK, width), f32),
            pltpu.VMEM((CHUNK, width), f32),
            pltpu.VMEM((CHUNK, LANES), f32),
            pltpu.VMEM((8 * (V_B1 + parts), width), f32),
        ],
        spot,
        (*locals_, qf, st, tokens, out_grad, w_output, w_inner, w_outer, vecs, flags, *before),
        50,
    )

    piece_o = ff // count
    piece = width // count
    per_step = width // piece_o
    sums = {}

    def run_outer(after):
        cut = piece_o // 2
        spec = block((per_step // 2, cut, width), lambda i: (i, 0, 0))
        out = call(
            functools.partial(outer_grad_kernel, piece=piece_o),
            parts,
            [block((rows, width), lambda i: (0, i)), whole((rows, width))],
            [((half, cut, width), bf16)] * 4,
            [spec] * 4,
            [],
            spot,
            (act, d_outer),
            9,
            hbm=(0,),
            after=after,
            vmem=FILL,
        )
        sums["outer0"] = Halving("outer0", out[0], out[1], count)
        sums["outer1"] = Halving("outer1", out[2], out[3], count)
        return (out[1],)

    def run_inner(after, lead):
        n = parts // 2
        full = fixed((half, n * piece, width))
        send, keep = call(
            functools.partial(inner_grad_kernel, piece=piece, parts=n),
            n,
            [whole((rows, width)), block((rows, width), lambda i: (0, lead * n + i))],
            [((half, n * piece, width), bf16)] * 2,
            [full, full],
            [],
            spot,
            (first, d_inner),
            5,
            hbm=(1,),
            after=after,
            vmem=FILL,
        )
        sums[f"inner{lead}"] = Halving(f"inner{lead}", send, keep, count)
        return (keep,)

    halves = 2
    hp = npair // halves
    hw = hp * LANES
    dqs = []

    def run_query_back(n, after):
        last = n == halves - 1
        at_ = (lambda i: jnp.minimum(i, nchunk - 1)) if last else (lambda i: i)
        fcol = block((CHUNK, 2 * hw), lambda i: (at_(i), n))
        vcol = block((CHUNK, hw), lambda i: (at_(i), n))
        lcol = block((CHUNK, LANES), lambda i: (at_(i), 0))
        out = block((CHUNK, hw), lambda i: (at_(i), 0))
        kept = block((1, gh, LANES, LANES), lambda i: (at_(i), 0, 0, 0))
        depth = piece + 8
        full = fixed((half, depth, width))
        wide = whole((rows, width))
        got = call(
            functools.partial(
                query_back_kernel, pair0=n * hp, npair=npair, nchunk=nchunk, piece=piece, last=last
            ),
            nchunk + last,
            [fcol, fcol, vcol, fcol, vcol, kept, kept, kept, pspec, lcol, lcol]
            + [wide, whole((rows, hw)), wide, wide, whole((VEC_ROWS, width))] * last,
            [((rows, hw), bf16)] + [((half, depth, width), bf16)] * (4 * last),
            [out] + [full] * (4 * last),
            [pltpu.VMEM((rows, hw), bf16)] * last,
            spot,
            (qf, kf, v, dn, q, *kepts, state_in, st, cs)
            + ((tokens, dqs[0], mixed, d_branch, vgrad) if last else ()),
            9 if last else 7,
            after=after,
            vmem=FILL,
        )
        dqs.append(got[0])
        if last:
            sums["query"] = Halving("query", got[1], got[2], count)
            sums["output"] = Halving("output", got[3], got[4], count)
        return (got[0],)

    theirs = []
    b1, b2 = 1, 2

    def round_of(bit):
        theirs.append(flip(back, bit, count))

    def recvs(*names):
        return tuple(sums[n].recv for n in names)

    round_of(0)
    back = joined(back, theirs[0])
    round_of(1)
    done = run_outer((back,))
    back = joined(back, theirs[1], done)

    round_of(2)
    sums["outer0"].launch(back)
    sums["outer1"].launch(back)
    done = run_inner((back,), 0)
    done = run_inner(done, 1)
    back = joined(back, theirs[2], done + recvs("outer0", "outer1"))

    round_of(3)
    _, done = add_step(spot, [([sums["outer0"]], b1), ([sums["outer1"]], b2)], (back,))
    sums["inner0"].launch(*done)
    sums["inner1"].launch(*done)
    done = run_query_back(0, done)
    back = joined(back, theirs[3], done + recvs("outer0", "outer1", "inner0", "inner1"))

    round_of(4)
    near, *_ = lax.optimization_barrier((near, back))
    from_next = lax.ppermute(near, AXES, [(i + 1, i) for i in range(count - 1)])
    _, done = add_step(spot, [([sums["inner0"]], b1), ([sums["inner1"]], b2)], (back,))
    done = run_query_back(1, done)
    for bit in range(5, nbits):
        back = joined(back, theirs[-1], done)
        round_of(bit)
    done += recvs("inner0", "inner1")
    (back_in,) = call(
        functools.partial(taken_kernel, lane=F_AFTER),
        1,
        [pspec] * (nbits + 1) + [fspec],
        [(packed, bf16)],
        [fixed(packed)],
        [],
        spot,
        (*theirs, from_next, flags),
        1,
        after=done,
        vmem=4,
    )

    dks, dvs = [], []

    def run_value_back(n, after):
        index = lambda i: nchunk - 1 - jnp.minimum(i, nchunk - 1)
        fcol = block((CHUNK, 2 * hw), lambda i: (index(i), n))
        vcol = block((CHUNK, hw), lambda i: (index(i), n))
        bcol = block((CHUNK, LANES), lambda i: (index(i), 0))
        grad = block((CHUNK, hw), lambda i: (index(i), 0))
        full = fixed((half, piece + 8, 2 * hw))
        dk, dv, send, keep = call(
            functools.partial(
                value_back_kernel, pair0=n * hp, npair=npair, nchunk=nchunk, piece=piece, rows=rows
            ),
            nchunk + 1,
            [fcol, fcol, vcol, fcol, vcol, pspec, bcol, bcol, bcol, whole((rows, width))],
            [((rows, hw), bf16)] * 2 + [((half, piece + 8, 2 * hw), bf16)] * 2,
            [grad, grad, full, full],
            [
                pltpu.VMEM((2 * hp, LANES, LANES), f32),
                pltpu.VMEM((rows, 2 * hw), bf16),
                pltpu.VMEM((8, 2 * hw), f32),
            ],
            spot,
            (qf, kf, v, dn, k, back_in, st, en, cs, tokens),
            10,
            after=after,
            vmem=FILL,
        )
        dks.append(dk)
        dvs.append(dv)
        sums[f"value{n}"] = Halving(f"value{n}", send, keep, count)

    g0, g1 = [sums["outer0"], sums["inner0"]], [sums["outer1"], sums["inner1"]]
    (f0, f1), done = add_step(spot, [(g0, b2), (g1, b1)], (back_in,))
    sums["query"].launch(*done)
    sums["output"].launch(*done)
    run_value_back(0, done)

    rest = list(range(3, nbits))
    q, o, kv0 = sums["query"], sums["output"], sums["value0"]
    done = (dks[0], f0.recv, f1.recv, q.recv, o.recv)
    (ffn, q, o), done = add_step(spot, [([f0, f1], rest[0]), ([q], b1), ([o], b2)], done)
    kv0.launch(*done)
    run_value_back(1, done)

    kv1 = sums["value1"]
    kv1.launch(dks[1], ffn.recv, q.recv, o.recv)
    groups = [([kv1], b1), ([kv0], b2), ([q], b2), ([o], b1), ([ffn], rest[1])]
    (kv1, kv0, q, o, ffn), done = add_step(spot, groups, (dks[1], ffn.recv, q.recv, o.recv))

    (grad_tokens,) = call(
        tokens_grad_kernel,
        nchunk,
        [tile] + [block((CHUNK, hw), at)] * 6 + [square] * 3,
        [((rows, width), bf16)],
        [tile],
        [],
        spot,
        (d_r1, *dqs, *dks, *dvs, w_query, w_key, w_value),
        8,
        hbm=(0, 1, 2, 3, 4, 5, 6, 7, 8, 9),
        after=done,
        vmem=FILL,
    )
    done = (grad_tokens, ffn.recv, q.recv, o.recv, kv0.recv, kv1.recv)
    groups = [([kv1], b2), ([kv0], b1), ([q, o], rest[0])]
    more = [([ffn], rest[2])] if len(rest) > 2 else []
    (kv1, kv0, qo, *_), done = add_step(spot, groups + more, done)
    done = (kv0.recv, kv1.recv, qo.recv)
    (kv, qo), done = add_step(spot, [([kv0, kv1], rest[0]), ([qo], rest[1])], done)
    while kv.left:
        open_ = [one for one in (kv, qo, ffn) if one.left]
        add_step(spot, [([one], one.left[-1]) for one in open_])

    found = {}
    for one in (ffn, qo, kv):
        found.update(one.result())
    g_outer = jnp.concatenate([found["outer0"], found["outer1"]])
    cuts = []
    for lead in range(2):
        block_sum = found[f"inner{lead}"]
        cuts += [block_sum[i * piece : (i + 1) * piece] for i in range(parts // 2)]
    g_inner = jnp.concatenate(cuts, axis=1)
    g_query, g_output = found["query"][:piece], found["output"][:piece]
    vec = jnp.concatenate([found["query"][piece:], found["output"][piece:]])
    kv = [found[f"value{n}"] for n in range(halves)]
    g_kv = [jnp.concatenate([s[:piece, m * hw : (m + 1) * hw] for s in kv], axis=1) for m in range(2)]
    b_kv = [jnp.concatenate([s[piece, m * hw : (m + 1) * hw] for s in kv]) for m in range(2)]

    def share(line):
        size = line.shape[0] // count
        return lax.dynamic_slice(line, (place * size,), (size,))

    return (
        result,
        grad_tokens,
        g_query,
        share(vec[VEC_ROWS - 1]),
        g_kv[0],
        share(b_kv[0]),
        g_kv[1],
        share(b_kv[1]),
        g_output,
        share(vec[V_BO]),
        g_inner,
        share(vec[V_B1 : V_B1 + parts].reshape(-1)),
        g_outer,
        share(vec[V_B2]),
        share(vec[V_G1]),
        share(vec[V_E1]),
        share(vec[V_G2]),
        share(vec[V_E2]),
    )


def solution(mesh):
    split = P(AXES, None)
    line = P(AXES)
    return jax.shard_map(
        per_device,
        mesh=mesh,
        in_specs=(split, split) + (P(),) * 17,
        out_specs=(split, split) + (split, line) * 6 + (line,) * 4,
        check_vma=False,
    )
```

```python
import functools
import math

import jax
import jax.numpy as jnp
from jax import lax
from jax.experimental import pallas as pl
from jax.experimental.pallas import tpu as pltpu
from jax.sharding import PartitionSpec as P

DH = 64
LANES = 128
CHUNK = 256
SLICE = 16
EPS = 1e-05
HALF_PI = math.pi / 2.0
MIB = 1 << 20
VMEM = 60
COST = 0.01
FILL = 30
AXES = ("wide", "narrow")

f32 = jnp.float32
bf16 = jnp.bfloat16

R_BQ, R_BK, R_BV, R_BO, R_G1, R_E1, R_B2, R_G2, R_E2, R_B1 = range(10)
V_B2, V_G2, V_E2, V_G1, V_E1, V_BO, V_B1 = range(7)
VEC_ROWS = 16


def nn(a, b):
    return jnp.dot(a, b, preferred_element_type=f32)


def nt(a, b):
    return lax.dot_general(a, b, (((1,), (1,)), ((), ())), preferred_element_type=f32)


def tn(a, b):
    return lax.dot_general(a, b, (((0,), (0,)), ((), ())), preferred_element_type=f32)


def lane_iota(rows, lanes=LANES):
    return lax.broadcasted_iota(jnp.int32, (rows, lanes), 1)


def row_iota(rows, lanes=LANES):
    return lax.broadcasted_iota(jnp.int32, (rows, lanes), 0)


def swap_halves(x):
    return pltpu.roll(x, DH, 1)


def softplus(x):
    return jnp.maximum(x, 0.0) + jnp.log1p(jnp.exp(-jnp.abs(x)))


def sigmoid(x):
    return 1.0 / (1.0 + jnp.exp(-x))


def sine(b):
    s = b * b
    p = 1.0 / 6227020800.0
    for c in (-1.0 / 39916800.0, 1.0 / 362880.0, -1.0 / 5040.0, 1.0 / 120.0, -1.0 / 6.0):
        p = p * s + c
    return b + b * s * p


def features(pair, cs, lo):
    soft = softplus(pair)
    other = swap_halves(soft)
    return (
        (jnp.where(lo, soft, other) * cs).astype(bf16),
        (jnp.where(lo, other, soft) * cs).astype(bf16),
    )


def extended(v, lo):
    one = jnp.ones_like(v)
    return jnp.where(lo, v, one), jnp.where(lo, one, v)


def pairs_of(width):
    return width // LANES


def lookup(len_ref, pos):
    start = jnp.zeros(pos.shape, jnp.int32)
    end = jnp.zeros(pos.shape, jnp.int32)
    edge = jnp.int32(0)
    for doc in range(len_ref.shape[0]):
        here = pos >= edge
        after = edge + len_ref[doc]
        start = jnp.where(here, edge, start)
        end = jnp.where(here, after, end)
        edge = after
    return start, end


F_BEFORE, F_NEXT_B, F_AFTER, F_NEXT_A, F_CLOSING, F_OPENING = range(6)


def flag_table(len_ref, place, rows):
    bit, lane = row_iota(8), lane_iota(8)
    upper = jnp.bitwise_and(jnp.right_shift(jnp.full_like(bit, place), bit), 1) == 1
    base, close = place * rows, (place + 1) * rows
    is_before = (lane == F_BEFORE) | (lane == F_NEXT_B)
    is_after = (lane == F_AFTER) | (lane == F_NEXT_A)
    pos = jnp.where(
        is_before,
        base - 1,
        jnp.where(is_after, close, jnp.where(lane == F_CLOSING, close - 1, base)),
    )
    start, end = lookup(len_ref, pos)
    one, zero = jnp.ones(bit.shape, f32), jnp.zeros(bit.shape, f32)
    is_long = jnp.where((end - start) > rows, one, zero)
    near = jnp.where((pos >= 0) & (pos < end), 1.0 - is_long, zero)
    out = is_long
    out = jnp.where(lane == F_BEFORE, jnp.where(upper, is_long, zero), out)
    out = jnp.where(lane == F_AFTER, jnp.where(upper, zero, is_long), out)
    return jnp.where((lane == F_NEXT_B) | (lane == F_NEXT_A), near, out)


def key_kernel(
    spot_ref, len_ref, x_ref, wk_ref, wv_ref,
    bq, bk, bv, bo, g1, e1, b2, g2, e2, b1,
    k_ref, v_ref, kf_ref, cs_ref, st_ref, en_ref, state_ref, next_ref, flag_ref, vec_ref,
    total,
    *, rows,
):
    step = pl.program_id(0)
    base = spot_ref[0]
    width = x_ref.shape[1]
    first = base + step * CHUNK
    pos = first + row_iota(CHUNK)
    lane = lane_iota(CHUNK)
    lo = lane < DH

    @pl.when(step == 0)
    def _():
        total[...] = jnp.zeros_like(total)
        flag_ref[...] = flag_table(len_ref, spot_ref[1], rows)
        for r, ref in enumerate((bq, bk, bv, bo, g1, e1, b2, g2, e2)):
            vec_ref[r : r + 1, :] = ref[...].astype(f32).reshape(1, width)
        for r in range(b1.shape[0] // width):
            vec_ref[R_B1 + r : R_B1 + r + 1, :] = (
                b1[r * width : (r + 1) * width].astype(f32).reshape(1, width)
            )

    start, end = lookup(len_ref, pos)
    part = jnp.where(lo, end - pos, pos - start).astype(f32)
    cs = sine(HALF_PI * part / (end - start).astype(f32))
    cs_ref[...] = cs
    st_ref[...] = start
    en_ref[...] = end

    x = x_ref[...]
    k = (nn(x, wk_ref[...]) + vec_ref[R_BK : R_BK + 1, :]).astype(bf16)
    v = (nn(x, wv_ref[...]) + vec_ref[R_BV : R_BV + 1, :]).astype(bf16)
    k_ref[...] = k
    v_ref[...] = v
    closing = end >= base + rows
    slots = lane_iota(LANES)
    lo_state = slots < DH

    npair = pairs_of(width)
    zcol = jnp.zeros((LANES, LANES), f32)
    for g in range(npair):
        cols = slice(g * LANES, (g + 1) * LANES)
        fa, fb = features(k[:, cols].astype(f32), cs, lo)
        kf_ref[:, 2 * g * LANES : (2 * g + 1) * LANES] = fa
        kf_ref[:, (2 * g + 1) * LANES : (2 * g + 2) * LANES] = fb
        va, vb = extended(v[:, cols], lo)
        zero = jnp.zeros_like(fa)
        sa = tn(jnp.where(closing, fa, zero), va)
        sb = tn(jnp.where(closing, fb, zero), vb)
        total[g] += jnp.where(lo_state, sa, sb)
        zcol = jnp.where(slots == DH + g, sa, jnp.where(slots == g, sb, zcol))
    total[npair] += zcol

    @pl.when(step == pl.num_programs(0) - 1)
    def _():
        split_long(total[...], flag_ref[0:1, F_CLOSING : F_CLOSING + 1], state_ref, next_ref)


def split_long(total, flag, long_ref, next_ref):
    long_ref[...] = (total * flag).astype(bf16)
    next_ref[...] = (total * (1.0 - flag)).astype(bf16)


def taken_sum(refs, flags, lane):
    *scans, near = refs
    total = near[...].astype(f32) * flags[0:1, lane + 1 : lane + 2]
    for bit, ref in enumerate(scans):
        total = total + ref[...].astype(f32) * flags[bit : bit + 1, lane : lane + 1]
    return total.astype(bf16)


def unpack_state(state_ref, g, npair, lo, slots):
    pair = state_ref[g].astype(f32)
    z = state_ref[npair].astype(f32)
    za = z[:, DH + g : DH + g + 1]
    zb = z[:, g : g + 1]
    return jnp.where(lo, pair, za), jnp.where(lo, zb, pair)


def unpack_grad_state(state_ref, g, npair, lo, slots):
    pair = state_ref[g].astype(f32)
    z = state_ref[npair].astype(f32)
    za = jnp.where(slots == DH, z[:, DH + g : DH + g + 1], 0.0)
    zb = jnp.where(slots == 0, z[:, g : g + 1], 0.0)
    return jnp.where(lo, pair, za), jnp.where(lo, zb, pair)


def query_kernel(spot_ref, x_ref, wq_ref, vec_ref, cs_ref, q_ref, qf_ref):
    q = (nn(x_ref[...], wq_ref[...]) + vec_ref[R_BQ : R_BQ + 1, :]).astype(bf16)
    q_ref[...] = q
    lo = lane_iota(CHUNK) < DH
    cs = cs_ref[...]
    for g in range(pairs_of(q.shape[1])):
        fa, fb = features(q[:, g * LANES : (g + 1) * LANES].astype(f32), cs, lo)
        qf_ref[:, 2 * g * LANES : (2 * g + 1) * LANES] = fa
        qf_ref[:, (2 * g + 1) * LANES : (2 * g + 2) * LANES] = fb


def mixer_kernel(spot_ref, qf_ref, kf_ref, v_ref, st_ref, en_ref, o_ref, kept_ref, local):
    step = pl.program_id(0)
    first = spot_ref[0] + step * CHUNK
    start, end = st_ref[...], en_ref[...]
    start2 = jnp.concatenate([start, start], axis=1)
    ipos = first + row_iota(CHUNK, CHUNK)
    jpos = first + lane_iota(CHUNK, CHUNK)
    mask = (jpos <= ipos) & (jpos >= start2)
    carried = start < first
    closing = end >= first + CHUNK
    keep = start[CHUNK - 1 : CHUNK, :] < first
    lo = lane_iota(CHUNK) < DH

    @pl.when(step == 0)
    def _():
        local[...] = jnp.zeros_like(local)

    for g in range(pairs_of(v_ref.shape[1])):
        vs = extended(v_ref[:, g * LANES : (g + 1) * LANES], lo)
        for s in range(2):
            h = 2 * g + s
            cols = slice(h * LANES, (h + 1) * LANES)
            qf, kf, v = qf_ref[:, cols], kf_ref[:, cols], vs[s]
            probs = jnp.where(mask, nt(qf, kf), 0.0).astype(bf16)
            held = local[h].astype(bf16)
            kept_ref[0, h] = held
            o_ref[:, cols] = nn(probs, v) + jnp.where(carried, nn(qf, held), 0.0)
            local[h] = jnp.where(keep, local[h], 0.0) + tn(
                jnp.where(closing, kf, jnp.zeros_like(kf)), v
            )


def gelu_and_slope(u):
    z = jnp.abs(u) * (1.0 / math.sqrt(2.0))
    t = 1.0 / (1.0 + 0.3275911 * z)
    p = 0.5 * 1.061405429
    for c in (-1.453152027, 1.421413741, -0.284496736, 0.254829592):
        p = p * t + 0.5 * c
    e = jnp.exp(-0.5 * u * u)
    tail = p * t * e
    gauss = jnp.where(u >= 0.0, 1.0 - tail, tail)
    return u * gauss, gauss + u * e * (1.0 / math.sqrt(2.0 * math.pi))


def token_kernel(
    spot_ref, o0_ref, o1_ref, o2_ref, qf_ref, st_ref, x_ref, go_ref,
    wo_ref, w1_ref, w2_ref, vec_ref, flag_ref, *refs, split, scans,
):
    theirs = refs[:scans]
    (
        out_ref, mixed_ref, first_ref, act_ref, douter_ref, dinner_ref, dbranch_ref, dr1_ref,
        dn_ref, back_ref, near_ref, vgrad_ref, state_ref,
        states, ratio, rden_s, slope, back_s, flow, norm_s, rstd_s, sums,
    ) = refs[scans:]
    step = pl.program_id(0)
    base = spot_ref[0]
    chunk, width = x_ref.shape
    ff = w1_ref.shape[1]
    npair = pairs_of(width)
    lane = lane_iota(chunk)
    lo = lane < DH
    slots = lane_iota(LANES)
    lo_state = slots < DH
    start = st_ref[...]

    @pl.when(step == 0)
    def _():
        state_ref[...] = taken_sum(theirs, flag_ref[...], F_BEFORE)
        for g in range(npair):
            a, b = unpack_state(state_ref, g, npair, lo_state, slots)
            states[2 * g] = a.astype(bf16)
            states[2 * g + 1] = b.astype(bf16)
        back_s[...] = jnp.zeros_like(back_s)
        sums[...] = jnp.zeros_like(sums)

    carried = start < base
    o_refs = (o0_ref, o1_ref, o2_ref)
    for g in range(npair):
        both = []
        for s in range(2):
            h = 2 * g + s
            o_of = o_refs[h // 4]
            local = o_of[:, (h % 4) * LANES : (h % 4 + 1) * LANES]
            far = nn(qf_ref[:, h * LANES : (h + 1) * LANES], states[h])
            both.append(local + jnp.where(carried, far, 0.0))
        numer = jnp.where(lo, both[0], both[1])
        rden = 1.0 / swap_halves(jnp.where(lo, both[1], both[0]))
        cols = slice(g * LANES, (g + 1) * LANES)
        rden_s[:, cols] = rden
        mix = numer * rden
        ratio[:, cols] = mix
        mixed_ref[:, cols] = mix.astype(bf16)

    def row(r):
        return vec_ref[r : r + 1, :]

    def mean(v):
        return jnp.sum(v, axis=-1, keepdims=True) * (1.0 / width)

    def norm(resid):
        cent = resid - mean(resid)
        rstd = lax.rsqrt(mean(cent * cent) + EPS)
        return cent * rstd, rstd

    def norm_back(grad, normed, rstd, gain):
        d_n = grad * gain
        return rstd * (d_n - mean(d_n) - normed * mean(d_n * normed))

    def add_sum(r, v, cols=slice(None)):
        sums[8 * r : 8 * r + 8, cols] += v

    flow[...] = nn(mixed_ref[...], wo_ref[...])
    for at in range(0, chunk, SLICE):
        sl = slice(at, at + SLICE)
        n1, rstd1 = norm(x_ref[sl, :].astype(f32) + flow[sl, :] + row(R_BO))
        norm_s[sl, :] = n1
        rstd_s[sl, :] = jnp.broadcast_to(rstd1, (SLICE, LANES))
        first_ref[sl, :] = (n1 * row(R_G1) + row(R_E1)).astype(bf16)

    part = ff // split

    def inner_of(i):
        flat, off = i * part // width, i * part % width
        bias = vec_ref[R_B1 + flat : R_B1 + flat + 1, off : off + part]
        return nn(first_ref[...], w1_ref[:, i * part : (i + 1) * part]) + bias

    ahead = inner_of(0)
    outer = jnp.zeros((chunk, width), f32)
    last = None
    for i in range(split):
        cols = slice(i * part, (i + 1) * part)
        now = ahead
        if i + 1 < split:
            ahead = inner_of(i + 1)
        if last is not None:
            outer = outer + nn(last, w2_ref[(i - 1) * part : i * part, :])
        act, sl = gelu_and_slope(now)
        last = act.astype(bf16)
        act_ref[:, cols] = last
        slope[:, cols] = sl
    flow[...] = outer + nn(last, w2_ref[(split - 1) * part :, :])

    g2_sum = e2_sum = b2_sum = jnp.zeros((8, width), f32)
    for at in range(0, chunk, SLICE):
        sl = slice(at, at + SLICE)
        n2, rstd2 = norm(first_ref[sl, :].astype(f32) + flow[sl, :] + row(R_B2))
        out_ref[sl, :] = (n2 * row(R_G2) + row(R_E2)).astype(bf16)
        grad = go_ref[sl, :].astype(f32)
        g2_sum = g2_sum + fold_rows(grad * n2)
        e2_sum = e2_sum + fold_rows(grad)
        d_r2 = norm_back(grad, n2, rstd2, row(R_G2))
        b2_sum = b2_sum + fold_rows(d_r2)
        douter_ref[sl, :] = d_r2.astype(bf16)
        dr1_ref[sl, :] = d_r2
    add_sum(V_G2, g2_sum)
    add_sum(V_E2, e2_sum)
    add_sum(V_B2, b2_sum)

    for i in range(split):
        cols = slice(i * part, (i + 1) * part)
        flat = i * part // width
        off = i * part % width
        d_inner = nt(douter_ref[...], w2_ref[cols, :]) * slope[:, cols]
        dinner_ref[:, cols] = d_inner.astype(bf16)
        add_sum(V_B1 + flat, fold_rows(d_inner), slice(off, off + part))
    flow[...] = nt(dinner_ref[...], w1_ref[...])

    g1_sum = e1_sum = bo_sum = jnp.zeros((8, width), f32)
    for at in range(0, chunk, SLICE):
        sl = slice(at, at + SLICE)
        d_first = dr1_ref[sl, :] + flow[sl, :]
        n1 = norm_s[sl, :]
        g1_sum = g1_sum + fold_rows(d_first * n1)
        e1_sum = e1_sum + fold_rows(d_first)
        d_r1 = norm_back(d_first, n1, rstd_s[sl, 0:1], row(R_G1))
        bo_sum = bo_sum + fold_rows(d_r1)
        dr1_ref[sl, :] = d_r1
        dbranch_ref[sl, :] = d_r1.astype(bf16)
    add_sum(V_G1, g1_sum)
    add_sum(V_E1, e1_sum)
    add_sum(V_BO, bo_sum)

    flow[...] = nt(dbranch_ref[...], wo_ref[...])
    opening = start <= base
    zcol = jnp.zeros((LANES, LANES), f32)
    for g in range(npair):
        cols = slice(g * LANES, (g + 1) * LANES)
        dn = flow[:, cols] * rden_s[:, cols]
        prod = dn * ratio[:, cols]
        dda = -jnp.sum(jnp.where(lo, prod, 0.0), axis=1, keepdims=True)
        ddb = -jnp.sum(jnp.where(lo, 0.0, prod), axis=1, keepdims=True)
        hia, hib = dda.astype(bf16).astype(f32), ddb.astype(bf16).astype(f32)
        exa = jnp.where(lane == DH, hia, jnp.where(lane == DH + 1, dda - hia, 0.0))
        exb = jnp.where(lane == 0, hib, jnp.where(lane == 1, ddb - hib, 0.0))
        dna = jnp.where(lo, dn, exa).astype(bf16)
        dnb = jnp.where(lo, exb, dn).astype(bf16)
        ca = slice(2 * g * LANES, (2 * g + 1) * LANES)
        cb = slice((2 * g + 1) * LANES, (2 * g + 2) * LANES)
        dn_ref[:, ca] = dna
        dn_ref[:, cb] = dnb
        zero = jnp.zeros((chunk, LANES), bf16)
        ga = tn(jnp.where(opening, qf_ref[:, ca], zero), dna)
        gb = tn(jnp.where(opening, qf_ref[:, cb], zero), dnb)
        back_s[g] += jnp.where(lo_state, ga, gb)
        za = ga[:, DH : DH + 1] + ga[:, DH + 1 : DH + 2]
        zb = gb[:, 0:1] + gb[:, 1:2]
        zcol = jnp.where(slots == DH + g, za, jnp.where(slots == g, zb, zcol))
    back_s[npair] += zcol

    @pl.when(step == pl.num_programs(0) - 1)
    def _():
        split_long(back_s[...], flag_ref[0:1, F_OPENING : F_OPENING + 1], back_ref, near_ref)
        vgrad_ref[...] = jnp.zeros_like(vgrad_ref)
        for r in range(sums.shape[0] // 8):
            vgrad_ref[r : r + 1, :] = jnp.sum(sums[8 * r : 8 * r + 8, :], axis=0, keepdims=True)


def fold_rows(v):
    return jnp.sum(v.reshape(v.shape[0] // 8, 8, v.shape[1]), axis=0)


def store_pieces(own, value, rows, send_ref, keep_ref, at):
    count = value.shape[0] // rows
    value = value.astype(bf16)
    for bit in range(2):

        @pl.when(own == bit)
        def _():
            for d in range(count):
                ref = keep_ref if d % 2 == bit else send_ref
                ref[d // 2, at : at + rows, :] = value[d * rows : (d + 1) * rows, :]


def store_lines(line, send_ref, keep_ref, at):
    line = line.astype(bf16)
    for m in range(send_ref.shape[0]):
        send_ref[m, at : at + line.shape[0], :] = line
        keep_ref[m, at : at + line.shape[0], :] = line


def query_back_kernel(
    spot_ref, qf_ref, kf_ref, v_ref, dn_ref, q_ref, kept0, kept1, kept2, state_ref, st_ref, cs_ref, *refs,
    pair0, npair, nchunk, piece, last,
):
    if last:
        x_ref, other_ref, mixed_ref, dbranch_ref, vec_ref, dq_ref, send0, keep0, send1, keep1, grads = refs
    else:
        (dq_ref,) = refs
    step = pl.program_id(0)
    base = spot_ref[0]
    keepers = (kept0, kept1, kept2)
    two = range(2)

    def chunk_step():
        lo = lane_iota(CHUNK) < DH
        slots = lane_iota(LANES)
        lo_state = slots < DH
        first = base + step * CHUNK
        start, cs = st_ref[...], cs_ref[...]
        start2 = jnp.concatenate([start, start], axis=1)
        ipos = first + row_iota(CHUNK, CHUNK)
        jpos = first + lane_iota(CHUNK, CHUNK)
        mask = (jpos <= ipos) & (jpos >= start2)
        carried = start < first
        from_far = start[0:1, :] < base
        at = pl.ds(pl.multiple_of(step * CHUNK, CHUNK), CHUNK)
        for g in range(pairs_of(v_ref.shape[1])):
            pair = slice(g * LANES, (g + 1) * LANES)
            cols = [slice((2 * g + s) * LANES, (2 * g + s + 1) * LANES) for s in two]
            heads = [2 * (pair0 + g) + s for s in two]
            vs = extended(v_ref[:, pair], lo)
            far = unpack_state(state_ref, pair0 + g, npair, lo_state, slots)
            dns = [dn_ref[:, c] for c in cols]
            d_probs = [nt(dns[s], vs[s]) for s in two]
            d_probs = [jnp.where(mask, d, 0.0).astype(bf16) for d in d_probs]
            held = [
                (keepers[heads[s] // 4][0, heads[s] % 4].astype(f32) + jnp.where(from_far, far[s], 0.0)).astype(bf16)
                for s in two
            ]
            d_qf = [
                nn(d_probs[s], kf_ref[:, cols[s]]) + jnp.where(carried, nt(dns[s], held[s]), 0.0) for s in two
            ]
            turned = [d * cs for d in d_qf]
            turned = [t + swap_halves(t) for t in turned]
            value = jnp.where(lo, turned[0], turned[1]) * sigmoid(q_ref[:, pair].astype(f32))
            value = value.astype(bf16)
            dq_ref[:, pair] = value
            if last:
                grads[at, pair] = value

    if not last:
        chunk_step()
        return

    pl.when(step < nchunk)(chunk_step)

    @pl.when(step == nchunk)
    def _():
        own = spot_ref[2]
        whole_q = jnp.concatenate([other_ref[...], grads[...]], axis=1)
        store_pieces(own, tn(x_ref[...], whole_q), piece, send0, keep0, 0)
        store_pieces(own, tn(mixed_ref[...], dbranch_ref[...]), piece, send1, keep1, 0)
        total = jnp.sum(fold_rows(whole_q.astype(f32)), axis=0, keepdims=True)
        vec = jnp.where(row_iota(VEC_ROWS, total.shape[1]) == VEC_ROWS - 1, total, vec_ref[...])
        store_lines(vec[:8], send0, keep0, piece)
        store_lines(vec[8:], send1, keep1, piece)


def value_back_kernel(
    spot_ref, qf_ref, kf_ref, v_ref, dn_ref, k_ref, back_ref, st_ref, en_ref, cs_ref, x_ref,
    dk_ref, dv_ref, send_ref, keep_ref,
    onward_state, grads, lines,
    *, pair0, npair, nchunk, piece, rows,
):
    base = spot_ref[0]
    wide = v_ref.shape[1]

    @pl.when(pl.program_id(0) == 0)
    def _():
        onward_state[...] = jnp.zeros_like(onward_state)
        lines[...] = jnp.zeros_like(lines)

    @pl.when(pl.program_id(0) < nchunk)
    def _():
        lo = lane_iota(CHUNK) < DH
        slots = lane_iota(LANES)
        lo_state = slots < DH
        step = nchunk - 1 - pl.program_id(0)
        first = base + step * CHUNK
        start, end, cs = st_ref[...], en_ref[...], cs_ref[...]
        end2 = jnp.concatenate([end, end], axis=1)
        jpos = first + row_iota(CHUNK, CHUNK)
        ipos = first + lane_iota(CHUNK, CHUNK)
        mask = (jpos <= ipos) & (ipos < end2)
        onward = end > first + CHUNK
        opening = start <= first
        to_far = end[CHUNK - 1 : CHUNK, :] > base + rows
        keep = end[0:1, :] > first + CHUNK
        at = pl.ds(pl.multiple_of(step * CHUNK, CHUNK), CHUNK)
        zero = jnp.zeros((CHUNK, LANES), bf16)
        two = range(2)
        for g in range(pairs_of(wide)):
            pair = slice(g * LANES, (g + 1) * LANES)
            cols = [slice((2 * g + s) * LANES, (2 * g + s + 1) * LANES) for s in two]
            vs = extended(v_ref[:, pair], lo)
            far = unpack_grad_state(back_ref, pair0 + g, npair, lo_state, slots)
            qf, kf = [qf_ref[:, c] for c in cols], [kf_ref[:, c] for c in cols]
            dn = [dn_ref[:, c] for c in cols]
            probs = [nt(kf[s], qf[s]) for s in two]
            d_probs = [nt(vs[s], dn[s]) for s in two]
            probs = [jnp.where(mask, p, 0.0).astype(bf16) for p in probs]
            d_probs = [jnp.where(mask, p, 0.0).astype(bf16) for p in d_probs]
            ahead = [onward_state[2 * g + s] for s in two]
            ahead16 = [(ahead[s] + jnp.where(to_far, far[s], 0.0)).astype(bf16) for s in two]
            more = [tn(jnp.where(opening, qf[s], zero), dn[s]) for s in two]
            d_kf = [nn(d_probs[s], qf[s]) + jnp.where(onward, nt(vs[s], ahead16[s]), 0.0) for s in two]
            d_v = [nn(probs[s], dn[s]) + jnp.where(onward, nn(kf[s], ahead16[s]), 0.0) for s in two]
            for s in two:
                onward_state[2 * g + s] = jnp.where(keep, ahead[s], 0.0) + more[s]
            turned = [d * cs for d in d_kf]
            turned = [t + swap_halves(t) for t in turned]
            both = (
                (jnp.where(lo, turned[0], turned[1]) * sigmoid(k_ref[:, pair].astype(f32)), dk_ref),
                (jnp.where(lo, d_v[0], d_v[1]), dv_ref),
            )
            for n, (value, ref) in enumerate(both):
                spread = slice(n * wide + g * LANES, n * wide + (g + 1) * LANES)
                lines[0:8, spread] += fold_rows(value)
                value = value.astype(bf16)
                ref[:, pair] = value
                grads[at, spread] = value

    @pl.when(pl.program_id(0) == nchunk)
    def _():
        store_pieces(spot_ref[2], tn(x_ref[...], grads[...]), piece, send_ref, keep_ref, 0)
        total = jnp.sum(lines[...], axis=0, keepdims=True)
        store_lines(jnp.broadcast_to(total, lines.shape), send_ref, keep_ref, piece)


def outer_grad_kernel(spot_ref, act_ref, d_ref, send0, keep0, send1, keep1, *, piece):
    value = tn(act_ref[...], d_ref[...]).astype(bf16)
    cut = piece // 2
    for bit in range(2):

        @pl.when(spot_ref[2] == bit)
        def _():
            for d in range(value.shape[0] // piece):
                first, second = (keep0, keep1) if d % 2 == bit else (send0, send1)
                first[d // 2] = value[d * piece : d * piece + cut, :]
                second[d // 2] = value[d * piece + cut : (d + 1) * piece, :]


def inner_grad_kernel(spot_ref, first_ref, dinner_ref, send_ref, keep_ref, *, piece, parts):
    for i in range(parts):

        @pl.when(pl.program_id(0) == i)
        def _():
            value = tn(first_ref[...], dinner_ref[...])
            store_pieces(spot_ref[2], value, piece, send_ref, keep_ref, i * piece)


def tokens_grad_kernel(spot_ref, dr1_ref, q0, q1, k0, k1, v0, v1, wq_ref, wk_ref, wv_ref, out_ref):
    total = dr1_ref[...]
    for refs, w in (((q0, q1), wq_ref), ((k0, k1), wk_ref), ((v0, v1), wv_ref)):
        total = total + nt(jnp.concatenate([r[...] for r in refs], axis=1), w[...])
    out_ref[...] = total.astype(bf16)


def taken_kernel(spot_ref, *refs, lane):
    *theirs, flag_ref, out_ref = refs
    out_ref[...] = taken_sum(theirs, flag_ref[...], lane)


def exchange(x, mask, count):
    return lax.ppermute(x, AXES, [(i, i ^ mask) for i in range(count)])


def flip(x, bit, count):
    return exchange(x, 1 << bit, count)


class Halving:

    def __init__(self, name, send, keep, count):
        self.count = count
        self.left = list(range(count.bit_length() - 2, 0, -1))
        self.tail = send.shape[1:]
        self.parts = [(name, self.tail[0])]
        self.keep = keep
        self.send = send
        self.bit = 0

    def launch(self, *after):
        send, *_ = lax.optimization_barrier((self.send, *after))
        self.recv = exchange(send, 1 << self.bit, self.count)

    def view(self, bit):
        axis = self.left.index(bit)
        a, b = 1 << axis, 1 << (len(self.left) - 1 - axis)
        shape = (a, 2, b, *self.tail)
        return self.keep.reshape(shape), self.recv.reshape(shape)

    def result(self):
        total = self.keep.reshape(self.tail).astype(f32) + self.recv.reshape(self.tail).astype(f32)
        out, at = {}, 0
        for name, n in self.parts:
            out[name] = total[at : at + n]
            at += n
        return out


def add_step(spot, groups, after=()):
    args, shapes, spans = [], [], []
    for sums, bit in groups:
        views = [one.view(bit) for one in sums]
        args += [x for v in views for x in v]
        a, _, b = views[0][0].shape[:3]
        rows = sum(one.tail[0] for one in sums)
        shapes += [jax.ShapeDtypeStruct((a, b, rows, sums[0].tail[1]), bf16)] * 2
    nargs = len(args)

    def body(spot_ref, *refs):
        ins, outs = iter(refs[:nargs]), iter(refs[nargs + len(after) :])
        for sums, bit in groups:
            send, left = next(outs), next(outs)
            own = spot_ref[2 + bit]
            at = 0
            for one in sums:
                keep, recv = next(ins), next(ins)
                n = one.tail[0]
                for half, ref in ((1 - own, send), (own, left)):
                    ref[:, :, at : at + n, :] = (keep[:, half].astype(f32) + recv[:, half].astype(f32)).astype(bf16)
                at += n

    vmem = pl.BlockSpec(memory_space=pltpu.VMEM)
    out = pl.pallas_call(
        body,
        in_specs=[pl.BlockSpec(memory_space=pltpu.SMEM)]
        + [vmem] * nargs
        + [pl.BlockSpec(memory_space=pl.ANY)] * len(after),
        out_specs=[vmem] * len(shapes),
        out_shape=shapes,
        compiler_params=pltpu.CompilerParams(vmem_limit_bytes=16 * MIB),
        cost_estimate=pl.CostEstimate(flops=int(1e5), bytes_accessed=int(1e5), transcendentals=0),
    )(spot, *args, *after)
    got = []
    for n, (sums, bit) in enumerate(groups):
        one = sums[0]
        one.parts = [p for s in sums for p in s.parts]
        one.left = [x for x in one.left if x != bit]
        one.tail = out[2 * n].shape[2:]
        one.send, one.keep, one.bit = out[2 * n], out[2 * n + 1], bit
        one.launch()
        got.append(one)
    return got, (out[-1],)


def block(shape, index):
    return pl.BlockSpec(shape, lambda i, spot: index(i))


def whole(shape):
    return pl.BlockSpec(shape, lambda i, spot: (0,) * len(shape), pipeline_mode=pl.Buffered(1))


SMEM = pl.BlockSpec(memory_space=pltpu.SMEM)


def call(kernel, grid, in_specs, outs, out_specs, scratch, spot, args, micros, after=(), vmem=VMEM, hbm=()):
    nin, nafter = len(in_specs), len(after)
    args = [
        pltpu.with_memory_space_constraint(x, pltpu.HBM) if n in hbm else x for n, x in enumerate(args)
    ]

    def body(spot_ref, *refs):
        kernel(spot_ref, *refs[:nin], *refs[nin + nafter :])

    return pl.pallas_call(
        body,
        grid_spec=pltpu.PrefetchScalarGridSpec(
            num_scalar_prefetch=1,
            grid=(grid,),
            in_specs=[*in_specs, *[pl.BlockSpec(memory_space=pl.ANY)] * nafter],
            out_specs=list(out_specs),
            scratch_shapes=scratch,
        ),
        out_shape=[jax.ShapeDtypeStruct(s, d) for s, d in outs],
        compiler_params=pltpu.CompilerParams(
            dimension_semantics=("arbitrary",), vmem_limit_bytes=vmem * MIB
        ),
        cost_estimate=pl.CostEstimate(flops=int(COST * 1e9 * micros), bytes_accessed=int(1e4), transcendentals=0),
    )(spot, *args, *after)


def per_device(
    tokens, out_grad, doc_lengths, w_query, b_query, w_key, b_key, w_value, b_value, w_output, b_output,
    w_inner, b_inner, w_outer, b_outer, gain_first, shift_first, gain_second, shift_second,
):
    rows, width = tokens.shape
    ff = w_inner.shape[1]
    count = lax.axis_size("wide") * lax.axis_size("narrow")
    place = lax.axis_index("wide") * lax.axis_size("narrow") + lax.axis_index("narrow")
    place = place.astype(jnp.int32)
    nchunk = rows // CHUNK
    npair = width // LANES
    heads = 2 * npair
    feat = heads * LANES
    nbits = count.bit_length() - 1
    half = count // 2
    parts = ff // width
    spot = jnp.stack([place * rows, place] + [(place >> b) & 1 for b in range(nbits)])
    at = lambda i: (i, 0)
    tile = block((CHUNK, width), at)
    ftile = block((CHUNK, feat), at)
    col = block((CHUNK, LANES), at)
    square = whole((width, width))
    nvec = R_B1 + parts
    vspec = whole((nvec, width))
    packed = (npair + 1, LANES, LANES)
    pspec = whole(packed)
    fspec = whole((8, LANES))
    fixed = lambda shape: pl.BlockSpec(shape, lambda i, spot: (0,) * len(shape))

    lines = (b_query, b_key, b_value, b_output, gain_first, shift_first, b_outer, gain_second, shift_second)
    k, v, kf, cs, st, en, total, near, flags, vecs = call(
        functools.partial(key_kernel, rows=rows),
        nchunk,
        [SMEM, tile, square, square] + [whole((width,))] * 9 + [whole((ff,))],
        [
            ((rows, width), bf16), ((rows, width), bf16), ((rows, feat), bf16),
            ((rows, LANES), f32), ((rows, LANES), jnp.int32), ((rows, LANES), jnp.int32), (packed, bf16), (packed, bf16),
            ((8, LANES), f32), ((nvec, width), f32),
        ],
        [tile, tile, ftile, col, col, col, fixed(packed), fixed(packed), fixed((8, LANES)), fixed((nvec, width))],
        [pltpu.VMEM(packed, f32)],
        spot,
        (doc_lengths, tokens, w_key, w_value, *lines, b_inner),
        12,
    )

    def run_query(sent):
        return call(
            query_kernel,
            nchunk,
            [tile, square, vspec, col],
            [((rows, width), bf16), ((rows, feat), bf16)],
            [tile, ftile],
            [],
            spot,
            (tokens, w_query, vecs, cs),
            4,
            after=(sent,),
            vmem=FILL,
        )

    groups = 3
    gh = heads // groups
    locals_, kepts = [], []

    def run_mixer(sent):
        n = len(kepts)
        fcol = block((CHUNK, gh * LANES), lambda i: (i, n))
        vcol = block((CHUNK, gh * DH), lambda i: (i, n))
        o, kept = call(
            mixer_kernel,
            nchunk,
            [fcol, fcol, vcol, col, col],
            [((rows, gh * LANES), f32), ((nchunk, gh, LANES, LANES), bf16)],
            [block((CHUNK, gh * LANES), at), block((1, gh, LANES, LANES), lambda i: (i, 0, 0, 0))],
            [pltpu.VMEM((gh, LANES, LANES), f32)],
            spot,
            (qf, kf, v, st, en),
            4,
            after=(sent,),
            vmem=FILL,
        )
        locals_.append(o)
        kepts.append(kept)
        return (o,)

    def joined(a, b, after=()):
        a, b, *after = lax.optimization_barrier((a, b, *after))
        return (a.astype(f32) + b.astype(f32)).astype(bf16)

    before = []
    done = ()
    for bit in range(nbits):
        before.append(flip(total, bit, count))
        if bit == 1:
            q, qf = run_query(total)
            done = (q,)
            from_last = lax.ppermute(near, AXES, [(i, i + 1) for i in range(count - 1)])
        elif bit >= 2 and len(kepts) < groups:
            done = run_mixer(total)
        if bit < nbits - 1:
            total = joined(total, before[-1], done)
    while len(kepts) < groups:
        run_mixer(total)
    before.append(from_last)

    ftile_ff = block((CHUNK, ff), at)
    otile = block((CHUNK, gh * LANES), at)
    (result, mixed, first, act, d_outer, d_inner, d_branch, d_r1, dn, back, near, vgrad, state_in) = call(
        functools.partial(token_kernel, split=12, scans=nbits + 1),
        nchunk,
        [
            otile, otile, otile, ftile, col, tile, tile,
            square, whole((width, ff)), whole((ff, width)), vspec, fspec,
        ] + [pspec] * (nbits + 1),
        [
            ((rows, width), bf16), ((rows, width), bf16), ((rows, width), bf16), ((rows, ff), bf16),
            ((rows, width), bf16), ((rows, ff), bf16), ((rows, width), bf16), ((rows, width), f32),
            ((rows, feat), bf16), (packed, bf16), (packed, bf16), ((VEC_ROWS, width), f32), (packed, bf16),
        ],
        [
            tile, tile, tile, ftile_ff, tile, ftile_ff, tile, tile, ftile,
            fixed(packed), fixed(packed), fixed((VEC_ROWS, width)), fixed(packed),
        ],
        [
            pltpu.VMEM((heads, LANES, LANES), bf16),
            pltpu.VMEM((CHUNK, width), f32),
            pltpu.VMEM((CHUNK, width), f32),
            pltpu.VMEM((CHUNK, ff), f32),
            pltpu.VMEM(packed, f32),
            pltpu.VMEM((CHUNK, width), f32),
            pltpu.VMEM((CHUNK, width), f32),
            pltpu.VMEM((CHUNK, LANES), f32),
            pltpu.VMEM((8 * (V_B1 + parts), width), f32),
        ],
        spot,
        (*locals_, qf, st, tokens, out_grad, w_output, w_inner, w_outer, vecs, flags, *before),
        50,
    )

    piece_o = ff // count
    piece = width // count
    per_step = width // piece_o
    sums = {}

    def run_outer(after):
        cut = piece_o // 2
        spec = block((per_step // 2, cut, width), lambda i: (i, 0, 0))
        out = call(
            functools.partial(outer_grad_kernel, piece=piece_o),
            parts,
            [block((rows, width), lambda i: (0, i)), whole((rows, width))],
            [((half, cut, width), bf16)] * 4,
            [spec] * 4,
            [],
            spot,
            (act, d_outer),
            9,
            hbm=(0,),
            after=after,
            vmem=FILL,
        )
        sums["outer0"] = Halving("outer0", out[0], out[1], count)
        sums["outer1"] = Halving("outer1", out[2], out[3], count)
        return (out[1],)

    def run_inner(after, lead):
        n = parts // 2
        full = fixed((half, n * piece, width))
        send, keep = call(
            functools.partial(inner_grad_kernel, piece=piece, parts=n),
            n,
            [whole((rows, width)), block((rows, width), lambda i: (0, lead * n + i))],
            [((half, n * piece, width), bf16)] * 2,
            [full, full],
            [],
            spot,
            (first, d_inner),
            5,
            hbm=(1,),
            after=after,
            vmem=FILL,
        )
        sums[f"inner{lead}"] = Halving(f"inner{lead}", send, keep, count)
        return (keep,)

    halves = 2
    hp = npair // halves
    hw = hp * LANES
    dqs = []

    def run_query_back(n, after):
        last = n == halves - 1
        at_ = (lambda i: jnp.minimum(i, nchunk - 1)) if last else (lambda i: i)
        fcol = block((CHUNK, 2 * hw), lambda i: (at_(i), n))
        vcol = block((CHUNK, hw), lambda i: (at_(i), n))
        lcol = block((CHUNK, LANES), lambda i: (at_(i), 0))
        out = block((CHUNK, hw), lambda i: (at_(i), 0))
        kept = block((1, gh, LANES, LANES), lambda i: (at_(i), 0, 0, 0))
        depth = piece + 8
        full = fixed((half, depth, width))
        wide = whole((rows, width))
        got = call(
            functools.partial(
                query_back_kernel, pair0=n * hp, npair=npair, nchunk=nchunk, piece=piece, last=last
            ),
            nchunk + last,
            [fcol, fcol, vcol, fcol, vcol, kept, kept, kept, pspec, lcol, lcol]
            + [wide, whole((rows, hw)), wide, wide, whole((VEC_ROWS, width))] * last,
            [((rows, hw), bf16)] + [((half, depth, width), bf16)] * (4 * last),
            [out] + [full] * (4 * last),
            [pltpu.VMEM((rows, hw), bf16)] * last,
            spot,
            (qf, kf, v, dn, q, *kepts, state_in, st, cs)
            + ((tokens, dqs[0], mixed, d_branch, vgrad) if last else ()),
            9 if last else 7,
            after=after,
            vmem=FILL,
        )
        dqs.append(got[0])
        if last:
            sums["query"] = Halving("query", got[1], got[2], count)
            sums["output"] = Halving("output", got[3], got[4], count)
        return (got[0],)

    theirs = []
    b1, b2 = 1, 2

    def round_of(bit):
        theirs.append(flip(back, bit, count))

    def recvs(*names):
        return tuple(sums[n].recv for n in names)

    round_of(0)
    back = joined(back, theirs[0])
    round_of(1)
    done = run_outer((back,))
    back = joined(back, theirs[1], done)

    round_of(2)
    near, *_ = lax.optimization_barrier((near, back))
    from_next = lax.ppermute(near, AXES, [(i + 1, i) for i in range(count - 1)])
    sums["outer0"].launch(back)
    sums["outer1"].launch(back)
    done = run_inner((back,), 0)
    done = run_inner(done, 1)
    back = joined(back, theirs[2], (from_next,) + done + recvs("outer0", "outer1"))

    round_of(3)
    _, done = add_step(spot, [([sums["outer0"]], b1), ([sums["outer1"]], b2)], (back,))
    sums["inner0"].launch(*done)
    sums["inner1"].launch(*done)
    done = run_query_back(0, done)
    back = joined(back, theirs[3], done + recvs("outer0", "outer1", "inner0", "inner1"))

    round_of(4)
    _, done = add_step(spot, [([sums["inner0"]], b1), ([sums["inner1"]], b2)], (back,))
    done = run_query_back(1, done)
    for bit in range(5, nbits):
        back = joined(back, theirs[-1], done)
        round_of(bit)
    done += recvs("inner0", "inner1")
    (back_in,) = call(
        functools.partial(taken_kernel, lane=F_AFTER),
        1,
        [pspec] * (nbits + 1) + [fspec],
        [(packed, bf16)],
        [fixed(packed)],
        [],
        spot,
        (*theirs, from_next, flags),
        1,
        after=done,
        vmem=4,
    )

    dks, dvs = [], []

    def run_value_back(n, after):
        index = lambda i: nchunk - 1 - jnp.minimum(i, nchunk - 1)
        fcol = block((CHUNK, 2 * hw), lambda i: (index(i), n))
        vcol = block((CHUNK, hw), lambda i: (index(i), n))
        bcol = block((CHUNK, LANES), lambda i: (index(i), 0))
        grad = block((CHUNK, hw), lambda i: (index(i), 0))
        full = fixed((half, piece + 8, 2 * hw))
        dk, dv, send, keep = call(
            functools.partial(
                value_back_kernel, pair0=n * hp, npair=npair, nchunk=nchunk, piece=piece, rows=rows
            ),
            nchunk + 1,
            [fcol, fcol, vcol, fcol, vcol, pspec, bcol, bcol, bcol, whole((rows, width))],
            [((rows, hw), bf16)] * 2 + [((half, piece + 8, 2 * hw), bf16)] * 2,
            [grad, grad, full, full],
            [
                pltpu.VMEM((2 * hp, LANES, LANES), f32),
                pltpu.VMEM((rows, 2 * hw), bf16),
                pltpu.VMEM((8, 2 * hw), f32),
            ],
            spot,
            (qf, kf, v, dn, k, back_in, st, en, cs, tokens),
            10,
            after=after,
            vmem=FILL,
        )
        dks.append(dk)
        dvs.append(dv)
        sums[f"value{n}"] = Halving(f"value{n}", send, keep, count)

    g0, g1 = [sums["outer0"], sums["inner0"]], [sums["outer1"], sums["inner1"]]
    (f0, f1), done = add_step(spot, [(g0, b2), (g1, b1)], (back_in,))
    sums["query"].launch(*done)
    sums["output"].launch(*done)
    run_value_back(0, done)

    rest = list(range(3, nbits))
    q, o, kv0 = sums["query"], sums["output"], sums["value0"]
    done = (dks[0], f0.recv, f1.recv, q.recv, o.recv)
    (ffn, q, o), done = add_step(spot, [([f0, f1], rest[0]), ([q], b1), ([o], b2)], done)
    kv0.launch(*done)
    run_value_back(1, done)

    kv1 = sums["value1"]
    kv1.launch(dks[1], ffn.recv, q.recv, o.recv)
    groups = [([kv1], b1), ([kv0], b2), ([q], b2), ([o], b1), ([ffn], rest[1])]
    (kv1, kv0, q, o, ffn), done = add_step(spot, groups, (dks[1], ffn.recv, q.recv, o.recv))

    (grad_tokens,) = call(
        tokens_grad_kernel,
        nchunk,
        [tile] + [block((CHUNK, hw), at)] * 6 + [square] * 3,
        [((rows, width), bf16)],
        [tile],
        [],
        spot,
        (d_r1, *dqs, *dks, *dvs, w_query, w_key, w_value),
        8,
        hbm=(0, 1, 2, 3, 4, 5, 6, 7, 8, 9),
        after=done,
        vmem=18,
    )
    done = (grad_tokens, ffn.recv, q.recv, o.recv, kv0.recv, kv1.recv)
    groups = [([kv1], b2), ([kv0], b1), ([q, o], rest[0])]
    more = [([ffn], rest[2])] if len(rest) > 2 else []
    (kv1, kv0, qo, *_), done = add_step(spot, groups + more, done)
    done = (kv0.recv, kv1.recv, qo.recv)
    (kv, qo), done = add_step(spot, [([kv0, kv1], rest[0]), ([qo], rest[1])], done)
    while kv.left:
        open_ = [one for one in (kv, qo, ffn) if one.left]
        add_step(spot, [([one], one.left[-1]) for one in open_])

    found = {}
    for one in (ffn, qo, kv):
        found.update(one.result())
    g_outer = jnp.concatenate([found["outer0"], found["outer1"]])
    cuts = []
    for lead in range(2):
        block_sum = found[f"inner{lead}"]
        cuts += [block_sum[i * piece : (i + 1) * piece] for i in range(parts // 2)]
    g_inner = jnp.concatenate(cuts, axis=1)
    g_query, g_output = found["query"][:piece], found["output"][:piece]
    vec = jnp.concatenate([found["query"][piece:], found["output"][piece:]])
    kv = [found[f"value{n}"] for n in range(halves)]
    g_kv = [jnp.concatenate([s[:piece, m * hw : (m + 1) * hw] for s in kv], axis=1) for m in range(2)]
    b_kv = [jnp.concatenate([s[piece, m * hw : (m + 1) * hw] for s in kv]) for m in range(2)]

    def share(line):
        size = line.shape[0] // count
        return lax.dynamic_slice(line, (place * size,), (size,))

    return (
        result,
        grad_tokens,
        g_query,
        share(vec[VEC_ROWS - 1]),
        g_kv[0],
        share(b_kv[0]),
        g_kv[1],
        share(b_kv[1]),
        g_output,
        share(vec[V_BO]),
        g_inner,
        share(vec[V_B1 : V_B1 + parts].reshape(-1)),
        g_outer,
        share(vec[V_B2]),
        share(vec[V_G1]),
        share(vec[V_E1]),
        share(vec[V_G2]),
        share(vec[V_E2]),
    )


def solution(mesh):
    split = P(AXES, None)
    line = P(AXES)
    return jax.shard_map(
        per_device,
        mesh=mesh,
        in_specs=(split, split) + (P(),) * 17,
        out_specs=(split, split) + (split, line) * 6 + (line,) * 4,
        check_vma=False,
    )
```

```python
import functools
import math

import jax
import jax.numpy as jnp
from jax import lax
from jax.experimental import pallas as pl
from jax.experimental.pallas import tpu as pltpu
from jax.sharding import PartitionSpec as P

DH = 64
LANES = 128
CHUNK = 256
SLICE = 16
EPS = 1e-05
HALF_PI = math.pi / 2.0
MIB = 1 << 20
VMEM = 60
COST = 0.01
FILL = 30
AXES = ("wide", "narrow")

f32 = jnp.float32
bf16 = jnp.bfloat16

R_BQ, R_BK, R_BV, R_BO, R_G1, R_E1, R_B2, R_G2, R_E2, R_B1 = range(10)
V_B2, V_G2, V_E2, V_G1, V_E1, V_BO, V_B1 = range(7)
VEC_ROWS = 16


def nn(a, b):
    return jnp.dot(a, b, preferred_element_type=f32)


def nt(a, b):
    return lax.dot_general(a, b, (((1,), (1,)), ((), ())), preferred_element_type=f32)


def tn(a, b):
    return lax.dot_general(a, b, (((0,), (0,)), ((), ())), preferred_element_type=f32)


def lane_iota(rows, lanes=LANES):
    return lax.broadcasted_iota(jnp.int32, (rows, lanes), 1)


def row_iota(rows, lanes=LANES):
    return lax.broadcasted_iota(jnp.int32, (rows, lanes), 0)


def swap_halves(x):
    return pltpu.roll(x, DH, 1)


def softplus(x):
    return jnp.maximum(x, 0.0) + jnp.log1p(jnp.exp(-jnp.abs(x)))


def sigmoid(x):
    return 1.0 / (1.0 + jnp.exp(-x))


def sine(b):
    s = b * b
    p = 1.0 / 6227020800.0
    for c in (-1.0 / 39916800.0, 1.0 / 362880.0, -1.0 / 5040.0, 1.0 / 120.0, -1.0 / 6.0):
        p = p * s + c
    return b + b * s * p


def features(pair, cs, lo):
    soft = softplus(pair)
    other = swap_halves(soft)
    return (
        (jnp.where(lo, soft, other) * cs).astype(bf16),
        (jnp.where(lo, other, soft) * cs).astype(bf16),
    )


def extended(v, lo):
    one = jnp.ones_like(v)
    return jnp.where(lo, v, one), jnp.where(lo, one, v)


def pairs_of(width):
    return width // LANES


def lookup(len_ref, pos):
    start = jnp.zeros(pos.shape, jnp.int32)
    end = jnp.zeros(pos.shape, jnp.int32)
    edge = jnp.int32(0)
    for doc in range(len_ref.shape[0]):
        here = pos >= edge
        after = edge + len_ref[doc]
        start = jnp.where(here, edge, start)
        end = jnp.where(here, after, end)
        edge = after
    return start, end


F_BEFORE, F_NEXT_B, F_AFTER, F_NEXT_A, F_CLOSING, F_OPENING = range(6)


def flag_table(len_ref, place, rows):
    bit, lane = row_iota(8), lane_iota(8)
    upper = jnp.bitwise_and(jnp.right_shift(jnp.full_like(bit, place), bit), 1) == 1
    base, close = place * rows, (place + 1) * rows
    is_before = (lane == F_BEFORE) | (lane == F_NEXT_B)
    is_after = (lane == F_AFTER) | (lane == F_NEXT_A)
    pos = jnp.where(
        is_before,
        base - 1,
        jnp.where(is_after, close, jnp.where(lane == F_CLOSING, close - 1, base)),
    )
    start, end = lookup(len_ref, pos)
    one, zero = jnp.ones(bit.shape, f32), jnp.zeros(bit.shape, f32)
    is_long = jnp.where((end - start) > rows, one, zero)
    near = jnp.where((pos >= 0) & (pos < end), 1.0 - is_long, zero)
    out = is_long
    out = jnp.where(lane == F_BEFORE, jnp.where(upper, is_long, zero), out)
    out = jnp.where(lane == F_AFTER, jnp.where(upper, zero, is_long), out)
    return jnp.where((lane == F_NEXT_B) | (lane == F_NEXT_A), near, out)


def key_kernel(
    spot_ref, len_ref, x_ref, wk_ref, wv_ref,
    bq, bk, bv, bo, g1, e1, b2, g2, e2, b1,
    k_ref, v_ref, kf_ref, cs_ref, st_ref, en_ref, state_ref, next_ref, flag_ref, vec_ref,
    total,
    *, rows,
):
    step = pl.program_id(0)
    base = spot_ref[0]
    width = x_ref.shape[1]
    first = base + step * CHUNK
    pos = first + row_iota(CHUNK)
    lane = lane_iota(CHUNK)
    lo = lane < DH

    @pl.when(step == 0)
    def _():
        total[...] = jnp.zeros_like(total)
        flag_ref[...] = flag_table(len_ref, spot_ref[1], rows)
        for r, ref in enumerate((bq, bk, bv, bo, g1, e1, b2, g2, e2)):
            vec_ref[r : r + 1, :] = ref[...].astype(f32).reshape(1, width)
        for r in range(b1.shape[0] // width):
            vec_ref[R_B1 + r : R_B1 + r + 1, :] = (
                b1[r * width : (r + 1) * width].astype(f32).reshape(1, width)
            )

    start, end = lookup(len_ref, pos)
    part = jnp.where(lo, end - pos, pos - start).astype(f32)
    cs = sine(HALF_PI * part / (end - start).astype(f32))
    cs_ref[...] = cs
    st_ref[...] = start
    en_ref[...] = end

    x = x_ref[...]
    k = (nn(x, wk_ref[...]) + vec_ref[R_BK : R_BK + 1, :]).astype(bf16)
    v = (nn(x, wv_ref[...]) + vec_ref[R_BV : R_BV + 1, :]).astype(bf16)
    k_ref[...] = k
    v_ref[...] = v
    closing = end >= base + rows
    slots = lane_iota(LANES)
    lo_state = slots < DH

    npair = pairs_of(width)
    zcol = jnp.zeros((LANES, LANES), f32)
    for g in range(npair):
        cols = slice(g * LANES, (g + 1) * LANES)
        fa, fb = features(k[:, cols].astype(f32), cs, lo)
        kf_ref[:, 2 * g * LANES : (2 * g + 1) * LANES] = fa
        kf_ref[:, (2 * g + 1) * LANES : (2 * g + 2) * LANES] = fb
        va, vb = extended(v[:, cols], lo)
        zero = jnp.zeros_like(fa)
        sa = tn(jnp.where(closing, fa, zero), va)
        sb = tn(jnp.where(closing, fb, zero), vb)
        total[g] += jnp.where(lo_state, sa, sb)
        zcol = jnp.where(slots == DH + g, sa, jnp.where(slots == g, sb, zcol))
    total[npair] += zcol

    @pl.when(step == pl.num_programs(0) - 1)
    def _():
        split_long(total[...], flag_ref[0:1, F_CLOSING : F_CLOSING + 1], state_ref, next_ref)


def split_long(total, flag, long_ref, next_ref):
    long_ref[...] = (total * flag).astype(bf16)
    next_ref[...] = (total * (1.0 - flag)).astype(bf16)


def taken_sum(refs, flags, lane):
    *scans, near = refs
    total = near[...].astype(f32) * flags[0:1, lane + 1 : lane + 2]
    for bit, ref in enumerate(scans):
        total = total + ref[...].astype(f32) * flags[bit : bit + 1, lane : lane + 1]
    return total.astype(bf16)


def unpack_state(state_ref, g, npair, lo, slots):
    pair = state_ref[g].astype(f32)
    z = state_ref[npair].astype(f32)
    za = z[:, DH + g : DH + g + 1]
    zb = z[:, g : g + 1]
    return jnp.where(lo, pair, za), jnp.where(lo, zb, pair)


def unpack_grad_state(state_ref, g, npair, lo, slots):
    pair = state_ref[g].astype(f32)
    z = state_ref[npair].astype(f32)
    za = jnp.where(slots == DH, z[:, DH + g : DH + g + 1], 0.0)
    zb = jnp.where(slots == 0, z[:, g : g + 1], 0.0)
    return jnp.where(lo, pair, za), jnp.where(lo, zb, pair)


def query_kernel(spot_ref, x_ref, wq_ref, vec_ref, cs_ref, q_ref, qf_ref):
    q = (nn(x_ref[...], wq_ref[...]) + vec_ref[R_BQ : R_BQ + 1, :]).astype(bf16)
    q_ref[...] = q
    lo = lane_iota(CHUNK) < DH
    cs = cs_ref[...]
    for g in range(pairs_of(q.shape[1])):
        fa, fb = features(q[:, g * LANES : (g + 1) * LANES].astype(f32), cs, lo)
        qf_ref[:, 2 * g * LANES : (2 * g + 1) * LANES] = fa
        qf_ref[:, (2 * g + 1) * LANES : (2 * g + 2) * LANES] = fb


def mixer_kernel(spot_ref, qf_ref, kf_ref, v_ref, st_ref, en_ref, o_ref, kept_ref, local):
    step = pl.program_id(0)
    first = spot_ref[0] + step * CHUNK
    start, end = st_ref[...], en_ref[...]
    start2 = jnp.concatenate([start, start], axis=1)
    ipos = first + row_iota(CHUNK, CHUNK)
    jpos = first + lane_iota(CHUNK, CHUNK)
    mask = (jpos <= ipos) & (jpos >= start2)
    carried = start < first
    closing = end >= first + CHUNK
    keep = start[CHUNK - 1 : CHUNK, :] < first
    lo = lane_iota(CHUNK) < DH

    @pl.when(step == 0)
    def _():
        local[...] = jnp.zeros_like(local)

    for g in range(pairs_of(v_ref.shape[1])):
        vs = extended(v_ref[:, g * LANES : (g + 1) * LANES], lo)
        two = range(2)
        cols = [slice((2 * g + s) * LANES, (2 * g + s + 1) * LANES) for s in two]
        qf, kf = [qf_ref[:, c] for c in cols], [kf_ref[:, c] for c in cols]
        probs = [nt(qf[s], kf[s]) for s in two]
        probs = [jnp.where(mask, p, 0.0).astype(bf16) for p in probs]
        before = [local[2 * g + s] for s in two]
        held = [b.astype(bf16) for b in before]
        more = [tn(jnp.where(closing, kf[s], jnp.zeros_like(kf[s])), vs[s]) for s in two]
        out = [nn(probs[s], vs[s]) + jnp.where(carried, nn(qf[s], held[s]), 0.0) for s in two]
        for s in two:
            kept_ref[0, 2 * g + s] = held[s]
            o_ref[:, cols[s]] = out[s]
            local[2 * g + s] = jnp.where(keep, before[s], 0.0) + more[s]


def gelu_and_slope(u):
    z = jnp.abs(u) * (1.0 / math.sqrt(2.0))
    t = 1.0 / (1.0 + 0.3275911 * z)
    p = 0.5 * 1.061405429
    for c in (-1.453152027, 1.421413741, -0.284496736, 0.254829592):
        p = p * t + 0.5 * c
    e = jnp.exp(-0.5 * u * u)
    tail = p * t * e
    gauss = jnp.where(u >= 0.0, 1.0 - tail, tail)
    return u * gauss, gauss + u * e * (1.0 / math.sqrt(2.0 * math.pi))


def token_kernel(
    spot_ref, o0_ref, o1_ref, o2_ref, qf_ref, st_ref, x_ref, go_ref,
    wo_ref, w1_ref, w2_ref, vec_ref, flag_ref, *refs, split, scans,
):
    theirs = refs[:scans]
    (
        out_ref, mixed_ref, first_ref, act_ref, douter_ref, dinner_ref, dbranch_ref, dr1_ref,
        dn_ref, back_ref, near_ref, vgrad_ref, state_ref,
        states, ratio, rden_s, slope, back_s, flow, norm_s, rstd_s, sums,
    ) = refs[scans:]
    step = pl.program_id(0)
    base = spot_ref[0]
    chunk, width = x_ref.shape
    ff = w1_ref.shape[1]
    npair = pairs_of(width)
    lane = lane_iota(chunk)
    lo = lane < DH
    slots = lane_iota(LANES)
    lo_state = slots < DH
    start = st_ref[...]

    @pl.when(step == 0)
    def _():
        state_ref[...] = taken_sum(theirs, flag_ref[...], F_BEFORE)
        for g in range(npair):
            a, b = unpack_state(state_ref, g, npair, lo_state, slots)
            states[2 * g] = a.astype(bf16)
            states[2 * g + 1] = b.astype(bf16)
        back_s[...] = jnp.zeros_like(back_s)
        sums[...] = jnp.zeros_like(sums)

    carried = start < base
    o_refs = (o0_ref, o1_ref, o2_ref)
    for g in range(npair):
        both = []
        for s in range(2):
            h = 2 * g + s
            o_of = o_refs[h // 4]
            local = o_of[:, (h % 4) * LANES : (h % 4 + 1) * LANES]
            far = nn(qf_ref[:, h * LANES : (h + 1) * LANES], states[h])
            both.append(local + jnp.where(carried, far, 0.0))
        numer = jnp.where(lo, both[0], both[1])
        rden = 1.0 / swap_halves(jnp.where(lo, both[1], both[0]))
        cols = slice(g * LANES, (g + 1) * LANES)
        rden_s[:, cols] = rden
        mix = numer * rden
        ratio[:, cols] = mix
        mixed_ref[:, cols] = mix.astype(bf16)

    def row(r):
        return vec_ref[r : r + 1, :]

    def mean(v):
        return jnp.sum(v, axis=-1, keepdims=True) * (1.0 / width)

    def norm(resid):
        cent = resid - mean(resid)
        rstd = lax.rsqrt(mean(cent * cent) + EPS)
        return cent * rstd, rstd

    def norm_back(grad, normed, rstd, gain):
        d_n = grad * gain
        return rstd * (d_n - mean(d_n) - normed * mean(d_n * normed))

    def add_sum(r, v, cols=slice(None)):
        sums[8 * r : 8 * r + 8, cols] += v

    flow[...] = nn(mixed_ref[...], wo_ref[...])
    for at in range(0, chunk, SLICE):
        sl = slice(at, at + SLICE)
        n1, rstd1 = norm(x_ref[sl, :].astype(f32) + flow[sl, :] + row(R_BO))
        norm_s[sl, :] = n1
        rstd_s[sl, :] = jnp.broadcast_to(rstd1, (SLICE, LANES))
        first_ref[sl, :] = (n1 * row(R_G1) + row(R_E1)).astype(bf16)

    part = ff // split

    def inner_of(i):
        flat, off = i * part // width, i * part % width
        bias = vec_ref[R_B1 + flat : R_B1 + flat + 1, off : off + part]
        return nn(first_ref[...], w1_ref[:, i * part : (i + 1) * part]) + bias

    ahead = inner_of(0)
    outer = jnp.zeros((chunk, width), f32)
    last = None
    for i in range(split):
        cols = slice(i * part, (i + 1) * part)
        now = ahead
        if i + 1 < split:
            ahead = inner_of(i + 1)
        if last is not None:
            outer = outer + nn(last, w2_ref[(i - 1) * part : i * part, :])
        act, sl = gelu_and_slope(now)
        last = act.astype(bf16)
        act_ref[:, cols] = last
        slope[:, cols] = sl
    flow[...] = outer + nn(last, w2_ref[(split - 1) * part :, :])

    g2_sum = e2_sum = b2_sum = jnp.zeros((8, width), f32)
    for at in range(0, chunk, SLICE):
        sl = slice(at, at + SLICE)
        n2, rstd2 = norm(first_ref[sl, :].astype(f32) + flow[sl, :] + row(R_B2))
        out_ref[sl, :] = (n2 * row(R_G2) + row(R_E2)).astype(bf16)
        grad = go_ref[sl, :].astype(f32)
        g2_sum = g2_sum + fold_rows(grad * n2)
        e2_sum = e2_sum + fold_rows(grad)
        d_r2 = norm_back(grad, n2, rstd2, row(R_G2))
        b2_sum = b2_sum + fold_rows(d_r2)
        douter_ref[sl, :] = d_r2.astype(bf16)
        dr1_ref[sl, :] = d_r2
    add_sum(V_G2, g2_sum)
    add_sum(V_E2, e2_sum)
    add_sum(V_B2, b2_sum)

    for i in range(split):
        cols = slice(i * part, (i + 1) * part)
        flat = i * part // width
        off = i * part % width
        d_inner = nt(douter_ref[...], w2_ref[cols, :]) * slope[:, cols]
        dinner_ref[:, cols] = d_inner.astype(bf16)
        add_sum(V_B1 + flat, fold_rows(d_inner), slice(off, off + part))
    flow[...] = nt(dinner_ref[...], w1_ref[...])

    g1_sum = e1_sum = bo_sum = jnp.zeros((8, width), f32)
    for at in range(0, chunk, SLICE):
        sl = slice(at, at + SLICE)
        d_first = dr1_ref[sl, :] + flow[sl, :]
        n1 = norm_s[sl, :]
        g1_sum = g1_sum + fold_rows(d_first * n1)
        e1_sum = e1_sum + fold_rows(d_first)
        d_r1 = norm_back(d_first, n1, rstd_s[sl, 0:1], row(R_G1))
        bo_sum = bo_sum + fold_rows(d_r1)
        dr1_ref[sl, :] = d_r1
        dbranch_ref[sl, :] = d_r1.astype(bf16)
    add_sum(V_G1, g1_sum)
    add_sum(V_E1, e1_sum)
    add_sum(V_BO, bo_sum)

    flow[...] = nt(dbranch_ref[...], wo_ref[...])
    opening = start <= base
    zcol = jnp.zeros((LANES, LANES), f32)
    for g in range(npair):
        cols = slice(g * LANES, (g + 1) * LANES)
        dn = flow[:, cols] * rden_s[:, cols]
        prod = dn * ratio[:, cols]
        dda = -jnp.sum(jnp.where(lo, prod, 0.0), axis=1, keepdims=True)
        ddb = -jnp.sum(jnp.where(lo, 0.0, prod), axis=1, keepdims=True)
        hia, hib = dda.astype(bf16).astype(f32), ddb.astype(bf16).astype(f32)
        exa = jnp.where(lane == DH, hia, jnp.where(lane == DH + 1, dda - hia, 0.0))
        exb = jnp.where(lane == 0, hib, jnp.where(lane == 1, ddb - hib, 0.0))
        dna = jnp.where(lo, dn, exa).astype(bf16)
        dnb = jnp.where(lo, exb, dn).astype(bf16)
        ca = slice(2 * g * LANES, (2 * g + 1) * LANES)
        cb = slice((2 * g + 1) * LANES, (2 * g + 2) * LANES)
        dn_ref[:, ca] = dna
        dn_ref[:, cb] = dnb
        zero = jnp.zeros((chunk, LANES), bf16)
        ga = tn(jnp.where(opening, qf_ref[:, ca], zero), dna)
        gb = tn(jnp.where(opening, qf_ref[:, cb], zero), dnb)
        back_s[g] += jnp.where(lo_state, ga, gb)
        za = ga[:, DH : DH + 1] + ga[:, DH + 1 : DH + 2]
        zb = gb[:, 0:1] + gb[:, 1:2]
        zcol = jnp.where(slots == DH + g, za, jnp.where(slots == g, zb, zcol))
    back_s[npair] += zcol

    @pl.when(step == pl.num_programs(0) - 1)
    def _():
        split_long(back_s[...], flag_ref[0:1, F_OPENING : F_OPENING + 1], back_ref, near_ref)
        vgrad_ref[...] = jnp.zeros_like(vgrad_ref)
        for r in range(sums.shape[0] // 8):
            vgrad_ref[r : r + 1, :] = jnp.sum(sums[8 * r : 8 * r + 8, :], axis=0, keepdims=True)


def fold_rows(v):
    return jnp.sum(v.reshape(v.shape[0] // 8, 8, v.shape[1]), axis=0)


def store_pieces(own, value, rows, send_ref, keep_ref, at):
    count = value.shape[0] // rows
    value = value.astype(bf16)
    for bit in range(2):

        @pl.when(own == bit)
        def _():
            for d in range(count):
                ref = keep_ref if d % 2 == bit else send_ref
                ref[d // 2, at : at + rows, :] = value[d * rows : (d + 1) * rows, :]


def store_lines(line, send_ref, keep_ref, at):
    line = line.astype(bf16)
    for m in range(send_ref.shape[0]):
        send_ref[m, at : at + line.shape[0], :] = line
        keep_ref[m, at : at + line.shape[0], :] = line


def query_back_kernel(
    spot_ref, qf_ref, kf_ref, v_ref, dn_ref, q_ref, kept0, kept1, kept2, state_ref, st_ref, cs_ref, *refs,
    pair0, npair, nchunk, piece, last,
):
    if last:
        x_ref, other_ref, mixed_ref, dbranch_ref, vec_ref, dq_ref, send0, keep0, send1, keep1, grads = refs
    else:
        (dq_ref,) = refs
    step = pl.program_id(0)
    base = spot_ref[0]
    keepers = (kept0, kept1, kept2)
    two = range(2)

    def chunk_step():
        lo = lane_iota(CHUNK) < DH
        slots = lane_iota(LANES)
        lo_state = slots < DH
        first = base + step * CHUNK
        start, cs = st_ref[...], cs_ref[...]
        start2 = jnp.concatenate([start, start], axis=1)
        ipos = first + row_iota(CHUNK, CHUNK)
        jpos = first + lane_iota(CHUNK, CHUNK)
        mask = (jpos <= ipos) & (jpos >= start2)
        carried = start < first
        from_far = start[0:1, :] < base
        at = pl.ds(pl.multiple_of(step * CHUNK, CHUNK), CHUNK)
        for g in range(pairs_of(v_ref.shape[1])):
            pair = slice(g * LANES, (g + 1) * LANES)
            cols = [slice((2 * g + s) * LANES, (2 * g + s + 1) * LANES) for s in two]
            heads = [2 * (pair0 + g) + s for s in two]
            vs = extended(v_ref[:, pair], lo)
            far = unpack_state(state_ref, pair0 + g, npair, lo_state, slots)
            dns = [dn_ref[:, c] for c in cols]
            d_probs = [nt(dns[s], vs[s]) for s in two]
            d_probs = [jnp.where(mask, d, 0.0).astype(bf16) for d in d_probs]
            held = [
                (keepers[heads[s] // 4][0, heads[s] % 4].astype(f32) + jnp.where(from_far, far[s], 0.0)).astype(bf16)
                for s in two
            ]
            d_qf = [
                nn(d_probs[s], kf_ref[:, cols[s]]) + jnp.where(carried, nt(dns[s], held[s]), 0.0) for s in two
            ]
            turned = [d * cs for d in d_qf]
            turned = [t + swap_halves(t) for t in turned]
            value = jnp.where(lo, turned[0], turned[1]) * sigmoid(q_ref[:, pair].astype(f32))
            value = value.astype(bf16)
            dq_ref[:, pair] = value
            if last:
                grads[at, pair] = value

    if not last:
        chunk_step()
        return

    pl.when(step < nchunk)(chunk_step)

    @pl.when(step == nchunk)
    def _():
        own = spot_ref[2]
        whole_q = jnp.concatenate([other_ref[...], grads[...]], axis=1)
        store_pieces(own, tn(x_ref[...], whole_q), piece, send0, keep0, 0)
        store_pieces(own, tn(mixed_ref[...], dbranch_ref[...]), piece, send1, keep1, 0)
        total = jnp.sum(fold_rows(whole_q.astype(f32)), axis=0, keepdims=True)
        vec = jnp.where(row_iota(VEC_ROWS, total.shape[1]) == VEC_ROWS - 1, total, vec_ref[...])
        store_lines(vec[:8], send0, keep0, piece)
        store_lines(vec[8:], send1, keep1, piece)


def value_back_kernel(
    spot_ref, qf_ref, kf_ref, v_ref, dn_ref, k_ref, back_ref, st_ref, en_ref, cs_ref, x_ref,
    dk_ref, dv_ref, send_ref, keep_ref,
    onward_state, grads, lines,
    *, pair0, npair, nchunk, piece, rows,
):
    base = spot_ref[0]
    wide = v_ref.shape[1]

    @pl.when(pl.program_id(0) == 0)
    def _():
        onward_state[...] = jnp.zeros_like(onward_state)
        lines[...] = jnp.zeros_like(lines)

    @pl.when(pl.program_id(0) < nchunk)
    def _():
        lo = lane_iota(CHUNK) < DH
        slots = lane_iota(LANES)
        lo_state = slots < DH
        step = nchunk - 1 - pl.program_id(0)
        first = base + step * CHUNK
        start, end, cs = st_ref[...], en_ref[...], cs_ref[...]
        end2 = jnp.concatenate([end, end], axis=1)
        jpos = first + row_iota(CHUNK, CHUNK)
        ipos = first + lane_iota(CHUNK, CHUNK)
        mask = (jpos <= ipos) & (ipos < end2)
        onward = end > first + CHUNK
        opening = start <= first
        to_far = end[CHUNK - 1 : CHUNK, :] > base + rows
        keep = end[0:1, :] > first + CHUNK
        at = pl.ds(pl.multiple_of(step * CHUNK, CHUNK), CHUNK)
        zero = jnp.zeros((CHUNK, LANES), bf16)
        two = range(2)
        for g in range(pairs_of(wide)):
            pair = slice(g * LANES, (g + 1) * LANES)
            cols = [slice((2 * g + s) * LANES, (2 * g + s + 1) * LANES) for s in two]
            vs = extended(v_ref[:, pair], lo)
            far = unpack_grad_state(back_ref, pair0 + g, npair, lo_state, slots)
            qf, kf = [qf_ref[:, c] for c in cols], [kf_ref[:, c] for c in cols]
            dn = [dn_ref[:, c] for c in cols]
            probs = [nt(kf[s], qf[s]) for s in two]
            d_probs = [nt(vs[s], dn[s]) for s in two]
            probs = [jnp.where(mask, p, 0.0).astype(bf16) for p in probs]
            d_probs = [jnp.where(mask, p, 0.0).astype(bf16) for p in d_probs]
            ahead = [onward_state[2 * g + s] for s in two]
            ahead16 = [(ahead[s] + jnp.where(to_far, far[s], 0.0)).astype(bf16) for s in two]
            more = [tn(jnp.where(opening, qf[s], zero), dn[s]) for s in two]
            d_kf = [nn(d_probs[s], qf[s]) + jnp.where(onward, nt(vs[s], ahead16[s]), 0.0) for s in two]
            d_v = [nn(probs[s], dn[s]) + jnp.where(onward, nn(kf[s], ahead16[s]), 0.0) for s in two]
            for s in two:
                onward_state[2 * g + s] = jnp.where(keep, ahead[s], 0.0) + more[s]
            turned = [d * cs for d in d_kf]
            turned = [t + swap_halves(t) for t in turned]
            both = (
                (jnp.where(lo, turned[0], turned[1]) * sigmoid(k_ref[:, pair].astype(f32)), dk_ref),
                (jnp.where(lo, d_v[0], d_v[1]), dv_ref),
            )
            for n, (value, ref) in enumerate(both):
                spread = slice(n * wide + g * LANES, n * wide + (g + 1) * LANES)
                lines[0:8, spread] += fold_rows(value)
                value = value.astype(bf16)
                ref[:, pair] = value
                grads[at, spread] = value

    @pl.when(pl.program_id(0) == nchunk)
    def _():
        store_pieces(spot_ref[2], tn(x_ref[...], grads[...]), piece, send_ref, keep_ref, 0)
        total = jnp.sum(lines[...], axis=0, keepdims=True)
        store_lines(jnp.broadcast_to(total, lines.shape), send_ref, keep_ref, piece)


def outer_grad_kernel(spot_ref, act_ref, d_ref, send0, keep0, send1, keep1, *, piece):
    value = tn(act_ref[...], d_ref[...]).astype(bf16)
    cut = piece // 2
    for bit in range(2):

        @pl.when(spot_ref[2] == bit)
        def _():
            for d in range(value.shape[0] // piece):
                first, second = (keep0, keep1) if d % 2 == bit else (send0, send1)
                first[d // 2] = value[d * piece : d * piece + cut, :]
                second[d // 2] = value[d * piece + cut : (d + 1) * piece, :]


def inner_grad_kernel(spot_ref, first_ref, dinner_ref, send_ref, keep_ref, *, piece, parts):
    for i in range(parts):

        @pl.when(pl.program_id(0) == i)
        def _():
            value = tn(first_ref[...], dinner_ref[...])
            store_pieces(spot_ref[2], value, piece, send_ref, keep_ref, i * piece)


def tokens_grad_kernel(spot_ref, dr1_ref, q0, q1, k0, k1, v0, v1, wq_ref, wk_ref, wv_ref, out_ref):
    total = dr1_ref[...]
    for refs, w in (((q0, q1), wq_ref), ((k0, k1), wk_ref), ((v0, v1), wv_ref)):
        total = total + nt(jnp.concatenate([r[...] for r in refs], axis=1), w[...])
    out_ref[...] = total.astype(bf16)


def taken_kernel(spot_ref, *refs, lane):
    *theirs, flag_ref, out_ref = refs
    out_ref[...] = taken_sum(theirs, flag_ref[...], lane)


def exchange(x, mask, count):
    return lax.ppermute(x, AXES, [(i, i ^ mask) for i in range(count)])


def flip(x, bit, count):
    return exchange(x, 1 << bit, count)


class Halving:

    def __init__(self, name, send, keep, count):
        self.count = count
        self.left = list(range(count.bit_length() - 2, 0, -1))
        self.tail = send.shape[1:]
        self.parts = [(name, self.tail[0])]
        self.keep = keep
        self.send = send
        self.bit = 0

    def launch(self, *after):
        send, *_ = lax.optimization_barrier((self.send, *after))
        self.recv = exchange(send, 1 << self.bit, self.count)

    def view(self, bit):
        axis = self.left.index(bit)
        a, b = 1 << axis, 1 << (len(self.left) - 1 - axis)
        shape = (a, 2, b, *self.tail)
        return self.keep.reshape(shape), self.recv.reshape(shape)

    def result(self):
        total = self.keep.reshape(self.tail).astype(f32) + self.recv.reshape(self.tail).astype(f32)
        out, at = {}, 0
        for name, n in self.parts:
            out[name] = total[at : at + n]
            at += n
        return out


def add_step(spot, groups, after=()):
    args, shapes, spans = [], [], []
    for sums, bit in groups:
        views = [one.view(bit) for one in sums]
        args += [x for v in views for x in v]
        a, _, b = views[0][0].shape[:3]
        rows = sum(one.tail[0] for one in sums)
        shapes += [jax.ShapeDtypeStruct((a, b, rows, sums[0].tail[1]), bf16)] * 2
    nargs = len(args)

    def body(spot_ref, *refs):
        ins, outs = iter(refs[:nargs]), iter(refs[nargs + len(after) :])
        for sums, bit in groups:
            send, left = next(outs), next(outs)
            own = spot_ref[2 + bit]
            at = 0
            for one in sums:
                keep, recv = next(ins), next(ins)
                n = one.tail[0]
                for half, ref in ((1 - own, send), (own, left)):
                    ref[:, :, at : at + n, :] = (keep[:, half].astype(f32) + recv[:, half].astype(f32)).astype(bf16)
                at += n

    vmem = pl.BlockSpec(memory_space=pltpu.VMEM)
    out = pl.pallas_call(
        body,
        in_specs=[pl.BlockSpec(memory_space=pltpu.SMEM)]
        + [vmem] * nargs
        + [pl.BlockSpec(memory_space=pl.ANY)] * len(after),
        out_specs=[vmem] * len(shapes),
        out_shape=shapes,
        compiler_params=pltpu.CompilerParams(vmem_limit_bytes=16 * MIB),
        cost_estimate=pl.CostEstimate(flops=int(1e5), bytes_accessed=int(1e5), transcendentals=0),
    )(spot, *args, *after)
    got = []
    for n, (sums, bit) in enumerate(groups):
        one = sums[0]
        one.parts = [p for s in sums for p in s.parts]
        one.left = [x for x in one.left if x != bit]
        one.tail = out[2 * n].shape[2:]
        one.send, one.keep, one.bit = out[2 * n], out[2 * n + 1], bit
        one.launch()
        got.append(one)
    return got, (out[-1],)


def block(shape, index):
    return pl.BlockSpec(shape, lambda i, spot: index(i))


def whole(shape):
    return pl.BlockSpec(shape, lambda i, spot: (0,) * len(shape), pipeline_mode=pl.Buffered(1))


SMEM = pl.BlockSpec(memory_space=pltpu.SMEM)


def call(kernel, grid, in_specs, outs, out_specs, scratch, spot, args, micros, after=(), vmem=VMEM, hbm=()):
    nin, nafter = len(in_specs), len(after)
    args = [
        pltpu.with_memory_space_constraint(x, pltpu.HBM) if n in hbm else x for n, x in enumerate(args)
    ]

    def body(spot_ref, *refs):
        kernel(spot_ref, *refs[:nin], *refs[nin + nafter :])

    return pl.pallas_call(
        body,
        grid_spec=pltpu.PrefetchScalarGridSpec(
            num_scalar_prefetch=1,
            grid=(grid,),
            in_specs=[*in_specs, *[pl.BlockSpec(memory_space=pl.ANY)] * nafter],
            out_specs=list(out_specs),
            scratch_shapes=scratch,
        ),
        out_shape=[jax.ShapeDtypeStruct(s, d) for s, d in outs],
        compiler_params=pltpu.CompilerParams(
            dimension_semantics=("arbitrary",), vmem_limit_bytes=vmem * MIB
        ),
        cost_estimate=pl.CostEstimate(flops=int(COST * 1e9 * micros), bytes_accessed=int(1e4), transcendentals=0),
    )(spot, *args, *after)


def per_device(
    tokens, out_grad, doc_lengths, w_query, b_query, w_key, b_key, w_value, b_value, w_output, b_output,
    w_inner, b_inner, w_outer, b_outer, gain_first, shift_first, gain_second, shift_second,
):
    rows, width = tokens.shape
    ff = w_inner.shape[1]
    count = lax.axis_size("wide") * lax.axis_size("narrow")
    place = lax.axis_index("wide") * lax.axis_size("narrow") + lax.axis_index("narrow")
    place = place.astype(jnp.int32)
    nchunk = rows // CHUNK
    npair = width // LANES
    heads = 2 * npair
    feat = heads * LANES
    nbits = count.bit_length() - 1
    half = count // 2
    parts = ff // width
    spot = jnp.stack([place * rows, place] + [(place >> b) & 1 for b in range(nbits)])
    at = lambda i: (i, 0)
    tile = block((CHUNK, width), at)
    ftile = block((CHUNK, feat), at)
    col = block((CHUNK, LANES), at)
    square = whole((width, width))
    nvec = R_B1 + parts
    vspec = whole((nvec, width))
    packed = (npair + 1, LANES, LANES)
    pspec = whole(packed)
    fspec = whole((8, LANES))
    fixed = lambda shape: pl.BlockSpec(shape, lambda i, spot: (0,) * len(shape))

    lines = (b_query, b_key, b_value, b_output, gain_first, shift_first, b_outer, gain_second, shift_second)
    k, v, kf, cs, st, en, total, near, flags, vecs = call(
        functools.partial(key_kernel, rows=rows),
        nchunk,
        [SMEM, tile, square, square] + [whole((width,))] * 9 + [whole((ff,))],
        [
            ((rows, width), bf16), ((rows, width), bf16), ((rows, feat), bf16),
            ((rows, LANES), f32), ((rows, LANES), jnp.int32), ((rows, LANES), jnp.int32), (packed, bf16), (packed, bf16),
            ((8, LANES), f32), ((nvec, width), f32),
        ],
        [tile, tile, ftile, col, col, col, fixed(packed), fixed(packed), fixed((8, LANES)), fixed((nvec, width))],
        [pltpu.VMEM(packed, f32)],
        spot,
        (doc_lengths, tokens, w_key, w_value, *lines, b_inner),
        12,
    )

    def run_query(sent):
        return call(
            query_kernel,
            nchunk,
            [tile, square, vspec, col],
            [((rows, width), bf16), ((rows, feat), bf16)],
            [tile, ftile],
            [],
            spot,
            (tokens, w_query, vecs, cs),
            4,
            after=(sent,),
            vmem=FILL,
        )

    groups = 3
    gh = heads // groups
    locals_, kepts = [], []

    def run_mixer(sent):
        n = len(kepts)
        fcol = block((CHUNK, gh * LANES), lambda i: (i, n))
        vcol = block((CHUNK, gh * DH), lambda i: (i, n))
        o, kept = call(
            mixer_kernel,
            nchunk,
            [fcol, fcol, vcol, col, col],
            [((rows, gh * LANES), f32), ((nchunk, gh, LANES, LANES), bf16)],
            [block((CHUNK, gh * LANES), at), block((1, gh, LANES, LANES), lambda i: (i, 0, 0, 0))],
            [pltpu.VMEM((gh, LANES, LANES), f32)],
            spot,
            (qf, kf, v, st, en),
            4,
            after=(sent,),
            vmem=FILL,
        )
        locals_.append(o)
        kepts.append(kept)
        return (o,)

    def joined(a, b, after=()):
        a, b, *after = lax.optimization_barrier((a, b, *after))
        return (a.astype(f32) + b.astype(f32)).astype(bf16)

    before = []
    done = ()
    for bit in range(nbits):
        before.append(flip(total, bit, count))
        if bit == 1:
            q, qf = run_query(total)
            done = (q,)
            from_last = lax.ppermute(near, AXES, [(i, i + 1) for i in range(count - 1)])
        elif bit >= 2 and len(kepts) < groups:
            done = run_mixer(total)
        if bit < nbits - 1:
            total = joined(total, before[-1], done)
    while len(kepts) < groups:
        run_mixer(total)
    before.append(from_last)

    ftile_ff = block((CHUNK, ff), at)
    otile = block((CHUNK, gh * LANES), at)
    (result, mixed, first, act, d_outer, d_inner, d_branch, d_r1, dn, back, near, vgrad, state_in) = call(
        functools.partial(token_kernel, split=12, scans=nbits + 1),
        nchunk,
        [
            otile, otile, otile, ftile, col, tile, tile,
            square, whole((width, ff)), whole((ff, width)), vspec, fspec,
        ] + [pspec] * (nbits + 1),
        [
            ((rows, width), bf16), ((rows, width), bf16), ((rows, width), bf16), ((rows, ff), bf16),
            ((rows, width), bf16), ((rows, ff), bf16), ((rows, width), bf16), ((rows, width), f32),
            ((rows, feat), bf16), (packed, bf16), (packed, bf16), ((VEC_ROWS, width), f32), (packed, bf16),
        ],
        [
            tile, tile, tile, ftile_ff, tile, ftile_ff, tile, tile, ftile,
            fixed(packed), fixed(packed), fixed((VEC_ROWS, width)), fixed(packed),
        ],
        [
            pltpu.VMEM((heads, LANES, LANES), bf16),
            pltpu.VMEM((CHUNK, width), f32),
            pltpu.VMEM((CHUNK, width), f32),
            pltpu.VMEM((CHUNK, ff), f32),
            pltpu.VMEM(packed, f32),
            pltpu.VMEM((CHUNK, width), f32),
            pltpu.VMEM((CHUNK, width), f32),
            pltpu.VMEM((CHUNK, LANES), f32),
            pltpu.VMEM((8 * (V_B1 + parts), width), f32),
        ],
        spot,
        (*locals_, qf, st, tokens, out_grad, w_output, w_inner, w_outer, vecs, flags, *before),
        50,
    )

    piece_o = ff // count
    piece = width // count
    per_step = width // piece_o
    sums = {}

    def run_outer(after):
        cut = piece_o // 2
        spec = block((per_step // 2, cut, width), lambda i: (i, 0, 0))
        out = call(
            functools.partial(outer_grad_kernel, piece=piece_o),
            parts,
            [block((rows, width), lambda i: (0, i)), whole((rows, width))],
            [((half, cut, width), bf16)] * 4,
            [spec] * 4,
            [],
            spot,
            (act, d_outer),
            9,
            hbm=(0,),
            after=after,
            vmem=FILL,
        )
        sums["outer0"] = Halving("outer0", out[0], out[1], count)
        sums["outer1"] = Halving("outer1", out[2], out[3], count)
        return (out[1],)

    def run_inner(after, lead):
        n = parts // 2
        full = fixed((half, n * piece, width))
        send, keep = call(
            functools.partial(inner_grad_kernel, piece=piece, parts=n),
            n,
            [whole((rows, width)), block((rows, width), lambda i: (0, lead * n + i))],
            [((half, n * piece, width), bf16)] * 2,
            [full, full],
            [],
            spot,
            (first, d_inner),
            5,
            hbm=(1,),
            after=after,
            vmem=FILL,
        )
        sums[f"inner{lead}"] = Halving(f"inner{lead}", send, keep, count)
        return (keep,)

    halves = 2
    hp = npair // halves
    hw = hp * LANES
    dqs = []

    def run_query_back(n, after):
        last = n == halves - 1
        at_ = (lambda i: jnp.minimum(i, nchunk - 1)) if last else (lambda i: i)
        fcol = block((CHUNK, 2 * hw), lambda i: (at_(i), n))
        vcol = block((CHUNK, hw), lambda i: (at_(i), n))
        lcol = block((CHUNK, LANES), lambda i: (at_(i), 0))
        out = block((CHUNK, hw), lambda i: (at_(i), 0))
        kept = block((1, gh, LANES, LANES), lambda i: (at_(i), 0, 0, 0))
        depth = piece + 8
        full = fixed((half, depth, width))
        wide = whole((rows, width))
        got = call(
            functools.partial(
                query_back_kernel, pair0=n * hp, npair=npair, nchunk=nchunk, piece=piece, last=last
            ),
            nchunk + last,
            [fcol, fcol, vcol, fcol, vcol, kept, kept, kept, pspec, lcol, lcol]
            + [wide, whole((rows, hw)), wide, wide, whole((VEC_ROWS, width))] * last,
            [((rows, hw), bf16)] + [((half, depth, width), bf16)] * (4 * last),
            [out] + [full] * (4 * last),
            [pltpu.VMEM((rows, hw), bf16)] * last,
            spot,
            (qf, kf, v, dn, q, *kepts, state_in, st, cs)
            + ((tokens, dqs[0], mixed, d_branch, vgrad) if last else ()),
            9 if last else 7,
            after=after,
            vmem=FILL,
        )
        dqs.append(got[0])
        if last:
            sums["query"] = Halving("query", got[1], got[2], count)
            sums["output"] = Halving("output", got[3], got[4], count)
        return (got[0],)

    theirs = []
    b1, b2 = 1, 2

    def round_of(bit):
        theirs.append(flip(back, bit, count))

    def recvs(*names):
        return tuple(sums[n].recv for n in names)

    round_of(0)
    back = joined(back, theirs[0])
    round_of(1)
    done = run_outer((back,))
    back = joined(back, theirs[1], done)

    round_of(2)
    near, *_ = lax.optimization_barrier((near, back))
    from_next = lax.ppermute(near, AXES, [(i + 1, i) for i in range(count - 1)])
    sums["outer0"].launch(back)
    sums["outer1"].launch(back)
    done = run_inner((back,), 0)
    done = run_inner(done, 1)
    back = joined(back, theirs[2], (from_next,) + done + recvs("outer0", "outer1"))

    round_of(3)
    _, done = add_step(spot, [([sums["outer0"]], b1), ([sums["outer1"]], b2)], (back,))
    sums["inner0"].launch(*done)
    sums["inner1"].launch(*done)
    done = run_query_back(0, done)
    back = joined(back, theirs[3], done + recvs("outer0", "outer1", "inner0", "inner1"))

    round_of(4)
    _, done = add_step(spot, [([sums["inner0"]], b1), ([sums["inner1"]], b2)], (back,))
    done = run_query_back(1, done)
    for bit in range(5, nbits):
        back = joined(back, theirs[-1], done)
        round_of(bit)
    done += recvs("inner0", "inner1")
    (back_in,) = call(
        functools.partial(taken_kernel, lane=F_AFTER),
        1,
        [pspec] * (nbits + 1) + [fspec],
        [(packed, bf16)],
        [fixed(packed)],
        [],
        spot,
        (*theirs, from_next, flags),
        1,
        after=done,
        vmem=4,
    )

    dks, dvs = [], []

    def run_value_back(n, after):
        index = lambda i: nchunk - 1 - jnp.minimum(i, nchunk - 1)
        fcol = block((CHUNK, 2 * hw), lambda i: (index(i), n))
        vcol = block((CHUNK, hw), lambda i: (index(i), n))
        bcol = block((CHUNK, LANES), lambda i: (index(i), 0))
        grad = block((CHUNK, hw), lambda i: (index(i), 0))
        full = fixed((half, piece + 8, 2 * hw))
        dk, dv, send, keep = call(
            functools.partial(
                value_back_kernel, pair0=n * hp, npair=npair, nchunk=nchunk, piece=piece, rows=rows
            ),
            nchunk + 1,
            [fcol, fcol, vcol, fcol, vcol, pspec, bcol, bcol, bcol, whole((rows, width))],
            [((rows, hw), bf16)] * 2 + [((half, piece + 8, 2 * hw), bf16)] * 2,
            [grad, grad, full, full],
            [
                pltpu.VMEM((2 * hp, LANES, LANES), f32),
                pltpu.VMEM((rows, 2 * hw), bf16),
                pltpu.VMEM((8, 2 * hw), f32),
            ],
            spot,
            (qf, kf, v, dn, k, back_in, st, en, cs, tokens),
            10,
            after=after,
            vmem=FILL,
        )
        dks.append(dk)
        dvs.append(dv)
        sums[f"value{n}"] = Halving(f"value{n}", send, keep, count)

    g0, g1 = [sums["outer0"], sums["inner0"]], [sums["outer1"], sums["inner1"]]
    (f0, f1), done = add_step(spot, [(g0, b2), (g1, b1)], (back_in,))
    sums["query"].launch(*done)
    sums["output"].launch(*done)
    run_value_back(0, done)

    rest = list(range(3, nbits))
    q, o, kv0 = sums["query"], sums["output"], sums["value0"]
    done = (dks[0], f0.recv, f1.recv, q.recv, o.recv)
    (ffn, q, o), done = add_step(spot, [([f0, f1], rest[0]), ([q], b1), ([o], b2)], done)
    kv0.launch(*done)
    run_value_back(1, done)

    kv1 = sums["value1"]
    kv1.launch(dks[1], ffn.recv, q.recv, o.recv)
    groups = [([kv1], b1), ([kv0], b2), ([q], b2), ([o], b1), ([ffn], rest[1])]
    (kv1, kv0, q, o, ffn), done = add_step(spot, groups, (dks[1], ffn.recv, q.recv, o.recv))

    (grad_tokens,) = call(
        tokens_grad_kernel,
        nchunk,
        [tile] + [block((CHUNK, hw), at)] * 6 + [square] * 3,
        [((rows, width), bf16)],
        [tile],
        [],
        spot,
        (d_r1, *dqs, *dks, *dvs, w_query, w_key, w_value),
        8,
        hbm=(0, 1, 2, 3, 4, 5, 6, 7, 8, 9),
        after=done,
        vmem=18,
    )
    done = (grad_tokens, ffn.recv, q.recv, o.recv, kv0.recv, kv1.recv)
    groups = [([kv1], b2), ([kv0], b1), ([q, o], rest[0])]
    more = [([ffn], rest[2])] if len(rest) > 2 else []
    (kv1, kv0, qo, *_), done = add_step(spot, groups + more, done)
    done = (kv0.recv, kv1.recv, qo.recv)
    (kv, qo), done = add_step(spot, [([kv0, kv1], rest[0]), ([qo], rest[1])], done)
    while kv.left:
        open_ = [one for one in (kv, qo, ffn) if one.left]
        add_step(spot, [([one], one.left[-1]) for one in open_])

    found = {}
    for one in (ffn, qo, kv):
        found.update(one.result())
    g_outer = jnp.concatenate([found["outer0"], found["outer1"]])
    cuts = []
    for lead in range(2):
        block_sum = found[f"inner{lead}"]
        cuts += [block_sum[i * piece : (i + 1) * piece] for i in range(parts // 2)]
    g_inner = jnp.concatenate(cuts, axis=1)
    g_query, g_output = found["query"][:piece], found["output"][:piece]
    vec = jnp.concatenate([found["query"][piece:], found["output"][piece:]])
    kv = [found[f"value{n}"] for n in range(halves)]
    g_kv = [jnp.concatenate([s[:piece, m * hw : (m + 1) * hw] for s in kv], axis=1) for m in range(2)]
    b_kv = [jnp.concatenate([s[piece, m * hw : (m + 1) * hw] for s in kv]) for m in range(2)]

    def share(line):
        size = line.shape[0] // count
        return lax.dynamic_slice(line, (place * size,), (size,))

    return (
        result,
        grad_tokens,
        g_query,
        share(vec[VEC_ROWS - 1]),
        g_kv[0],
        share(b_kv[0]),
        g_kv[1],
        share(b_kv[1]),
        g_output,
        share(vec[V_BO]),
        g_inner,
        share(vec[V_B1 : V_B1 + parts].reshape(-1)),
        g_outer,
        share(vec[V_B2]),
        share(vec[V_G1]),
        share(vec[V_E1]),
        share(vec[V_G2]),
        share(vec[V_E2]),
    )


def solution(mesh):
    split = P(AXES, None)
    line = P(AXES)
    return jax.shard_map(
        per_device,
        mesh=mesh,
        in_specs=(split, split) + (P(),) * 17,
        out_specs=(split, split) + (split, line) * 6 + (line,) * 4,
        check_vma=False,
    )
```
